512 devices in a mesh: row: 16 (over z), col: 32 (over x, y, core).
Axes of the slice: x: 4, y: 4, z: 16, core: 2. Of those that a mesh axis runs over, the one named last changes fastest.
Arguments:
- heights: int32 [1024, 2048], P('row', 'col'), may hold values from 0 to 199
- blocked: int32 [1024, 2048], P('row', 'col'), may hold values 0 or 1
- estimate: bfloat16 [1024, 65536], P('row', 'col'), may hold values from 0 to 48
- portal_index: int32 [16, 32, 32], P('row', 'col'), may hold values from 0 to 4095, as said below
Outputs:
- relaxed: bfloat16 [1024, 65536], P('row', 'col')
- merged: float32 [16, 32, 32, 32], P('row', 'col')
The draws below stay inside these ranges and needn't reach their ends.
Inputs may be any that keep to these rules, and one draw needn't show every extreme that they name: `portal_index`: the 32 portal cells of a tile are all different.
All inputs are finite; a program needn't handle non-finite values. No bound on the sum of `blocked` on one device may be relied on, other than what follows from the above.
Results may differ from the reference program's by a relative error of at most 0.001.
Values sent between devices are 32-bit elements; how exact they have to be, the bound alone decides.
A program may use at most 128 MiB of HBM per device.

```python
import jax
import jax.numpy as jnp
from jax import lax

TILE = 64
P_SIZE = 32
SWEEPS = 8
LEVELS = 2
GR = 16
GC = 32
NR = 1024
NC = 2048


def draw_portal_index(key, part):
    key = jax.random.fold_in(key, 7)
    tile_keys = jax.random.split(key, GR * GC)
    chosen = jax.vmap(lambda one_key: jax.random.permutation(one_key, TILE * TILE)[:P_SIZE])(tile_keys)
    return chosen.astype(jnp.int32).reshape(GR, GC, P_SIZE)


def set_ends(array, rng, smallest, largest):
    index_at = [jax.random.randint(jax.random.fold_in(rng, axis), (), 0, length) for axis, length in enumerate(array.shape)]
    main_axis = array.shape.index(max(array.shape))
    next_to = index_at[:main_axis] + [(index_at[main_axis] + 1) % array.shape[main_axis]] + index_at[main_axis + 1:]
    return array.at[tuple(index_at)].set(smallest).at[tuple(next_to)].set(largest)


def shard_levels(own_key, dims, pieces, low, top_value):
    factor_of, own = 1.0, jax.random.fold_in(own_key, 6)
    for axis_at, blocks in pieces:
        steps = jnp.exp(jax.random.uniform(jax.random.fold_in(own, axis_at), (blocks,), jnp.float32, low / len(pieces), top_value / len(pieces)))
        factor_of = factor_of * jnp.repeat(steps, dims[axis_at] // blocks).reshape([-1 if axis == axis_at else 1 for axis in range(len(dims))])
    return factor_of


def setup_inputs(seed: int = 0) -> dict:
    arg_keys = jax.random.split(jax.random.key(seed), 5)
    return {
        "heights": set_ends(jax.random.randint(arg_keys[0], (NR, NC), 0, 200), jax.random.fold_in(arg_keys[0], 1), 0, 199).astype(jnp.int32),
        "blocked": set_ends((jax.random.randint(arg_keys[1], (NR, NC), 0, 8) < 1).astype(jnp.int32), jax.random.fold_in(arg_keys[1], 1), 0, 1),
        "estimate": jnp.clip(48.0 * jax.random.uniform(arg_keys[2], (NR, NC * P_SIZE), jnp.float32) ** shard_levels(arg_keys[2], (NR, NC * P_SIZE), ((0, 16), (1, 32)), -0.2, 0.2), 0.0, 48.0).astype(jnp.bfloat16),
        "portal_index": draw_portal_index(jax.random.fold_in(arg_keys[4], 71), 0),
    }


far_value = 1000000.0

def slope_cost(padded_heights, blocked):
    grad_x = (padded_heights[1:-1, 2:] - padded_heights[1:-1, :-2]).astype(jnp.float32) * 0.01
    grad_y = (padded_heights[2:, 1:-1] - padded_heights[:-2, 1:-1]).astype(jnp.float32) * 0.01
    grad_sq = grad_x * grad_x + grad_y * grad_y
    return 1.0 + 2.0 * grad_sq + 0.5 * grad_y / jnp.sqrt(1.0 + grad_sq) + 30.0 * blocked.astype(jnp.float32)

def relax_once(extended, cost_ext):
    centre_cost = cost_ext[1:-1, 1:-1, None]
    centre_cells = extended[1:-1, 1:-1]
    north = extended[:-2, 1:-1] + 0.5 * (centre_cost + cost_ext[:-2, 1:-1, None])
    south = extended[2:, 1:-1] + 0.5 * (centre_cost + cost_ext[2:, 1:-1, None])
    west = extended[1:-1, :-2] + 0.5 * (centre_cost + cost_ext[1:-1, :-2, None])
    east = extended[1:-1, 2:] + 0.5 * (centre_cost + cost_ext[1:-1, 2:, None])
    nearest = jnp.minimum(jnp.minimum(north, south), jnp.minimum(west, east))
    return jnp.minimum(centre_cells, nearest)

def minplus(left, right):
    return lax.optimization_barrier(jnp.min(left[..., :, :, None] + right[..., None, :, :], axis=-2))

def merge_pair(table_now, partner):
    return jnp.minimum(table_now, minplus(minplus(table_now, partner), table_now))

def reference(heights, blocked, estimate, portal_index):
    step_cost = slope_cost(jnp.pad(heights, 1, mode='edge'), blocked)
    cost_ext = jnp.pad(step_cost, 1)
    dist_field = estimate.astype(jnp.float32).reshape(NR, NC, P_SIZE)
    cell_rows = jnp.arange(GR, dtype=jnp.int32)[:, None, None] * TILE + portal_index // TILE
    cell_cols = jnp.arange(GC, dtype=jnp.int32)[None, :, None] * TILE + portal_index % TILE
    classes = jnp.broadcast_to(jnp.arange(P_SIZE, dtype=jnp.int32)[None, None, :], portal_index.shape)
    dist_field = dist_field.at[cell_rows, cell_cols, classes].set(0.0)
    for sweep_step in range(SWEEPS):
        extended = jnp.pad(dist_field, ((1, 1), (1, 1), (0, 0)), constant_values=far_value)
        dist_field = relax_once(extended, cost_ext)
    table_now = dist_field[cell_rows, cell_cols]
    for level in range(LEVELS):
        row_partner = jnp.arange(GR) ^ 1 << level
        table_now = merge_pair(table_now, table_now[row_partner])
        col_partner = jnp.arange(GC) ^ 1 << level
        table_now = merge_pair(table_now, table_now[:, col_partner])
    return (dist_field.reshape(NR, NC * P_SIZE).astype(jnp.bfloat16), table_now * 0.0625)
```

```python
import functools

import jax
import jax.numpy as jnp
from jax import lax
from jax.experimental import pallas as pl
from jax.experimental.pallas import tpu as pltpu
from jax.sharding import PartitionSpec as P

TILE = 64
PORTALS = 32
SWEEPS = 8
HALO = 8
EXT = TILE + 2 * HALO
LANES = 128
CELLS = LANES // PORTALS
GROUPS = EXT // CELLS
SIDE = HALO // CELLS
STEP = EXT // 8
STRIP = 16
FAR = 1000000.0

AROUND = ((-1, 0), (1, 0), (0, -1), (0, 1), (-1, -1), (-1, 1), (1, -1), (1, 1))


def lane_take(values, index):
    return jnp.take_along_axis(values, index, axis=1, mode="promise_in_bounds")


def kernel(
    portal_smem, heights_hbm, blocked_hbm, estimate_hbm, portal_hbm,
    relaxed_hbm, merged_hbm,
    heights, blocked, estimate, portal, relaxed, merged,
    ground, strips, ground_in, high, cost_rows,
    field, cost, dist, rows, shifts, table, table_in, right_rows,
    load_sem, store_sem, ground_send, ground_recv, field_send, field_recv,
    table_send, table_recv,
):
    row_index, col_index = lax.axis_index("row"), lax.axis_index("col")
    row_count, col_count = lax.axis_size("row"), lax.axis_size("col")
    around = [
        (lax.rem(row_index + dr + row_count, row_count), lax.rem(col_index + dc + col_count, col_count))
        for dr, dc in AROUND
    ]

    def other(index, bit):
        return index + bit - 2 * bit * lax.rem(index // bit, 2)

    partners = []
    for level in range(2):
        bit = 1 << level
        partners.append(
            [
                (other(row_index, bit), col_index),
                (row_index, other(col_index, bit)),
                (other(row_index, bit), other(col_index, bit)),
            ]
        )

    loads = [
        pltpu.make_async_copy(source, target, load_sem.at[at])
        for at, (source, target) in enumerate(
            (
                (heights_hbm, heights),
                (blocked_hbm, blocked),
                (portal_hbm, portal),
                (estimate_hbm, estimate),
            )
        )
    ]
    for load in loads:
        load.start()

    barrier = pltpu.get_barrier_semaphore()
    met = around + partners[1]
    for device in met:
        pl.semaphore_signal(barrier, inc=1, device_id=device, device_id_type=pl.DeviceIdType.MESH)

    def send(source, target, send_sem, recv_sem, device):
        copy = pltpu.make_async_remote_copy(
            src_ref=source, dst_ref=target, send_sem=send_sem, recv_sem=recv_sem,
            device_id=device, device_id_type=pl.DeviceIdType.MESH,
        )
        copy.start()
        return copy

    lane = lax.broadcasted_iota(jnp.int32, (8, LANES), 1)
    sublane = lax.broadcasted_iota(jnp.int32, (8, LANES), 0)
    lane_block = lane // PORTALS
    lane_class = lane % PORTALS

    loads[0].wait()
    loads[1].wait()
    ground[:, 0:TILE] = heights[...]
    ground[:, TILE : 2 * TILE] = blocked[...]
    wide = lax.broadcasted_iota(jnp.int32, (STRIP, LANES), 1)
    west = jnp.zeros((STRIP, LANES), jnp.int32)
    east = jnp.zeros((STRIP, LANES), jnp.int32)
    for part in range(4):
        here = ground[part * STRIP : (part + 1) * STRIP]
        base = part * 32
        in_height = (wide >= base) & (wide < base + 16)
        in_block = (wide >= base + 16) & (wide < base + 32)
        west = jnp.where(in_height, pltpu.roll(here, base % LANES, 1), west)
        west = jnp.where(in_block, pltpu.roll(here, (base + 16 - 64) % LANES, 1), west)
        east = jnp.where(in_height, pltpu.roll(here, (base - 48) % LANES, 1), east)
        east = jnp.where(in_block, pltpu.roll(here, (base + 16 - 112) % LANES, 1), east)
    strips[0] = west
    strips[1] = east

    pl.semaphore_wait(barrier, len(met))

    top, bottom = ground.at[0:STRIP], ground.at[TILE - STRIP : TILE]
    ground_source = {-1: top, 1: bottom}
    ground_copies = []
    for at, (dr, dc) in enumerate(AROUND):
        if dr:
            source = ground_source[dr]
        else:
            source = strips.at[0 if dc < 0 else 1]
        slot = AROUND.index((-dr, -dc))
        ground_copies.append(
            send(source, ground_in.at[slot], ground_send.at[at], ground_recv.at[slot], around[at])
        )

    loads[2].wait()
    own = jnp.broadcast_to(portal[0, 0:1, :], (8, PORTALS))
    portal_cells = jnp.concatenate([own] * CELLS, axis=1)
    loads[3].wait()

    def prepare(part, group):
        values = estimate[part * 16 : (part + 1) * 16, group * LANES : (group + 1) * LANES]
        values = values.astype(jnp.float32)
        for half in range(2):
            row = part * 16 + half * 8
            cell = (row + sublane) * TILE + lane_block + group * CELLS
            here = jnp.where(portal_cells == cell, 0.0, values[half * 8 : (half + 1) * 8])
            field[SIDE + group, HALO + row : HALO + row + 8, :] = here

    inner = TILE // CELLS
    for part in (0, 3):
        for group in range(inner):
            prepare(part, group)
    for part in (1, 2):
        for group in (0, 1, inner - 2, inner - 1):
            prepare(part, group)

    def span(step, own_start, length, halo):
        if step < 0:
            return (own_start, halo), (own_start + length, halo)
        if step > 0:
            return (own_start + length - halo, halo), (own_start - halo, halo)
        return (own_start, length), (own_start, length)

    field_copies = []
    for at, (dr, dc) in enumerate(AROUND):
        (row_from, row_len), (row_to, _) = span(dr, HALO, TILE, HALO)
        (grp_from, grp_len), (grp_to, _) = span(dc, SIDE, inner, SIDE)
        slot = AROUND.index((-dr, -dc))
        field_copies.append(
            send(
                field.at[pl.ds(grp_from, grp_len), pl.ds(row_from, row_len), :],
                field.at[pl.ds(grp_to, grp_len), pl.ds(row_to, row_len), :],
                field_send.at[at], field_recv.at[slot], around[at],
            )
        )

    for part in (1, 2):
        for group in range(2, inner - 2):
            prepare(part, group)

    for copy in ground_copies:
        copy.wait_recv()
    slots = {step: at for at, step in enumerate(AROUND)}

    def lay(row, west_height, middle, east_height, west_block, east_block):
        height = jnp.where(wide < 16, west_height, jnp.where(wide < 80, pltpu.roll(middle, 16, 1), east_height))
        block = jnp.where(wide < 16, west_block, jnp.where(wide < 80, pltpu.roll(middle, 80, 1), east_block))
        high[0, row : row + STRIP, :] = height.astype(jnp.float32)
        high[1, row : row + STRIP, :] = block.astype(jnp.float32)

    for dr, row in ((-1, 0), (1, STRIP + TILE)):
        west_in, middle, east_in = (ground_in[slots[(dr, dc)]] for dc in (-1, 0, 1))
        lay(
            row, pltpu.roll(west_in, 80, 1), middle, pltpu.roll(east_in, 80, 1),
            pltpu.roll(west_in, 16, 1), pltpu.roll(east_in, 16, 1),
        )
    west_in, east_in = ground_in[slots[(0, -1)]], ground_in[slots[(0, 1)]]
    for part in range(4):
        base = part * 32
        lay(
            STRIP + part * STRIP,
            pltpu.roll(west_in, (-base) % LANES, 1),
            ground[part * STRIP : (part + 1) * STRIP],
            pltpu.roll(east_in, (80 - base) % LANES, 1),
            pltpu.roll(west_in, (-base - 16) % LANES, 1),
            pltpu.roll(east_in, (64 - base) % LANES, 1),
        )

    @pl.when(row_index == 0)
    def _():
        high[0, STRIP - 1 : STRIP, :] = high[0, STRIP : STRIP + 1, :]

    @pl.when(row_index == row_count - 1)
    def _():
        high[0, STRIP + TILE : STRIP + TILE + 1, :] = high[0, STRIP + TILE - 1 : STRIP + TILE, :]

    shift = STRIP - HALO
    near = high[0, shift : shift + EXT, :]
    up = high[0, shift - 1 : shift - 1 + EXT, :]
    down = high[0, shift + 1 : shift + 1 + EXT, :]
    col = lax.broadcasted_iota(jnp.int32, (EXT, LANES), 1) - STRIP
    row = lax.broadcasted_iota(jnp.int32, (EXT, LANES), 0) - HALO
    grid_col = col_index * TILE + col
    grid_row = row_index * TILE + row
    before = jnp.where(grid_col == 0, near, pltpu.roll(near, 1, 1))
    after = jnp.where(grid_col == col_count * TILE - 1, near, pltpu.roll(near, LANES - 1, 1))
    grad_x = (after - before) * 0.01
    grad_y = (down - up) * 0.01
    grad_sq = grad_x * grad_x + grad_y * grad_y
    step_cost = (
        1.0 + 2.0 * grad_sq + 0.5 * grad_y / jnp.sqrt(1.0 + grad_sq)
        + 30.0 * high[1, shift : shift + EXT, :]
    )
    inside = (
        (grid_row >= 0) & (grid_row < row_count * TILE)
        & (grid_col >= 0) & (grid_col < col_count * TILE)
    )
    cost_rows[...] = jnp.where(inside, step_cost, FAR)
    for at in range(STEP):
        values = cost_rows[pl.ds(at, 8, stride=STEP), :]
        for group in range(GROUPS):
            cost[group, at] = lane_take(values, lane_block + (group * CELLS + shift))

    for copy in field_copies:
        copy.wait_recv()
    for group in range(GROUPS):
        for at in range(STEP):
            here = cost[group, at]
            start = field[group, pl.ds(at, 8, stride=STEP), :] + 0.5 * here
            dist[group, at] = jnp.where(here >= FAR, FAR, start)

    first_block, last_block = lane < PORTALS, lane >= LANES - PORTALS

    def sweep(_, carry):
        now = [dist[0, at] for at in range(STEP)]
        pair_west = now
        for group in range(GROUPS):
            later = [dist[group + 1, at] for at in range(STEP)] if group < GROUPS - 1 else now
            east_of = [
                pltpu.roll(jnp.where(first_block, later[at], now[at]), LANES - PORTALS, 1)
                for at in range(STEP)
            ]
            below = east_of[1:] + [pltpu.roll(east_of[0], 7, 0)]
            pairs = [jnp.minimum(now[at], below[at]) for at in range(STEP)]
            north = [pltpu.roll(pairs[STEP - 1], 1, 0)] + pairs[:-1]
            for at in range(STEP):
                west_of = pltpu.roll(jnp.where(last_block, pair_west[at], pairs[at]), PORTALS, 1)
                nearest = cost[group, at] + jnp.minimum(north[at], west_of)
                dist[group, at] = jnp.minimum(now[at], nearest)
            pair_west, now = pairs, later
        return carry

    lax.fori_loop(0, SWEEPS, sweep, 0)

    for copy in field_copies:
        copy.wait_send()
    for group in range(SIDE, GROUPS - SIDE):
        for at in range(STEP):
            field[group, pl.ds(at, 8, stride=STEP), :] = dist[group, at] - 0.5 * cost[group, at]

    for at in range(PORTALS):
        cell = portal_smem[0, 0, at]
        rows[at : at + 1, :] = field[SIDE + (cell % TILE) // CELLS, pl.ds(HALO + cell // TILE, 1), :]
        shifts[at : at + 1, :] = jnp.full((1, LANES), (cell % CELLS) * PORTALS, jnp.int32)
    first = jnp.zeros((8, LANES), jnp.float32)
    for part in range(4):
        index = shifts[part * 8 : part * 8 + 8, :] + lane_class
        first = jnp.where(lane_block == part, lane_take(rows[part * 8 : part * 8 + 8, :], index), first)
    table[0] = first

    table_copies = []

    def exchange(level):
        copies = [
            send(
                table.at[level], table_in.at[3 * level + at],
                table_send.at[3 * level + at], table_recv.at[3 * level + at], device,
            )
            for at, device in enumerate(partners[level])
        ]
        table_copies.extend(copies)
        return copies

    def left_of(values):
        return [lane_take(values, lane_block * PORTALS + at) for at in range(PORTALS)]

    def right_of(values, slot):
        for part in range(4):
            right_rows[slot, part * 8 : part * 8 + 8, :] = lane_take(values, lane_class + part * PORTALS)
        return [
            jnp.broadcast_to(right_rows[slot, at : at + 1, :], (8, LANES)) for at in range(PORTALS)
        ]

    def minplus(left, right):
        sums = [a + b for a, b in zip(left, right)]
        while len(sums) > 1:
            sums = [jnp.minimum(a, b) for a, b in zip(sums[::2], sums[1::2])]
        return sums[0]

    def pair(near_table, far_table, slot):
        through = minplus(left_of(near_table), right_of(far_table, slot))
        return jnp.minimum(near_table, minplus(left_of(through), right_of(near_table, slot + 1)))

    copies = exchange(0)

    for group in range(inner):
        for part in range(4):
            values = field[SIDE + group, HALO + part * 16 : HALO + part * 16 + 16, :]
            relaxed[part * 16 : part * 16 + 16, group * LANES : (group + 1) * LANES] = values.astype(jnp.bfloat16)
    store = pltpu.make_async_copy(relaxed, relaxed_hbm, store_sem.at[0])
    store.start()

    now = first
    for level in range(2):
        for copy in copies:
            copy.wait_recv()
        by_row, by_col, by_both = (table_in[3 * level + at] for at in range(3))
        here = pair(now, by_row, 6 * level)
        there = pair(by_col, by_both, 6 * level + 2)
        now = pair(here, there, 6 * level + 4)
        if level == 0:
            table[1] = now
            copies = exchange(1)
    now = now * 0.0625
    for part in range(4):
        merged[0, 0, part * 8 : part * 8 + 8, :] = now[:, part * PORTALS : (part + 1) * PORTALS]
    last = pltpu.make_async_copy(merged, merged_hbm, store_sem.at[1])
    last.start()

    for copy in ground_copies + table_copies:
        copy.wait_send()
    store.wait()
    last.wait()


def body(heights, blocked, estimate, portal_index):
    anywhere = pl.BlockSpec(memory_space=pl.ANY)
    return pl.pallas_call(
        kernel,
        out_shape=(
            jax.ShapeDtypeStruct(estimate.shape, jnp.bfloat16),
            jax.ShapeDtypeStruct((1, 1, PORTALS, PORTALS), jnp.float32),
        ),
        in_specs=[pl.BlockSpec(memory_space=pltpu.SMEM)] + [anywhere] * 4,
        out_specs=(anywhere, anywhere),
        scratch_shapes=[
            pltpu.VMEM((TILE, TILE), jnp.int32),
            pltpu.VMEM((TILE, TILE), jnp.int32),
            pltpu.VMEM((TILE, TILE * PORTALS), jnp.bfloat16),
            pltpu.VMEM((1, 1, PORTALS), jnp.int32),
            pltpu.VMEM((TILE, TILE * PORTALS), jnp.bfloat16),
            pltpu.VMEM((1, 1, PORTALS, PORTALS), jnp.float32),
            pltpu.VMEM((TILE, LANES), jnp.int32),
            pltpu.VMEM((2, STRIP, LANES), jnp.int32),
            pltpu.VMEM((8, STRIP, LANES), jnp.int32),
            pltpu.VMEM((2, TILE + 2 * STRIP, LANES), jnp.float32),
            pltpu.VMEM((EXT, LANES), jnp.float32),
            pltpu.VMEM((GROUPS, EXT, LANES), jnp.float32),
            pltpu.VMEM((GROUPS, STEP, 8, LANES), jnp.float32),
            pltpu.VMEM((GROUPS, STEP, 8, LANES), jnp.float32),
            pltpu.VMEM((PORTALS, LANES), jnp.float32),
            pltpu.VMEM((PORTALS, LANES), jnp.int32),
            pltpu.VMEM((2, 8, LANES), jnp.float32),
            pltpu.VMEM((6, 8, LANES), jnp.float32),
            pltpu.VMEM((12, PORTALS, LANES), jnp.float32),
            pltpu.SemaphoreType.DMA((4,)),
            pltpu.SemaphoreType.DMA((2,)),
            pltpu.SemaphoreType.DMA((8,)),
            pltpu.SemaphoreType.DMA((8,)),
            pltpu.SemaphoreType.DMA((8,)),
            pltpu.SemaphoreType.DMA((8,)),
            pltpu.SemaphoreType.DMA((6,)),
            pltpu.SemaphoreType.DMA((6,)),
        ],
        compiler_params=pltpu.CompilerParams(
            collective_id=0, has_side_effects=True, vmem_limit_bytes=16 * 2**20
        ),
    )(portal_index, heights, blocked, estimate, portal_index)


def solution(mesh):
    placed = (P("row", "col"), P("row", "col"), P("row", "col"), P("row", "col", None))
    return jax.shard_map(
        body,
        mesh=mesh,
        in_specs=placed,
        out_specs=(P("row", "col"), P("row", "col", None, None)),
        check_vma=False,
    )
```

```python
import functools

import jax
import jax.numpy as jnp
from jax import lax
from jax.experimental import pallas as pl
from jax.experimental.pallas import tpu as pltpu
from jax.sharding import PartitionSpec as P

TILE = 64
PORTALS = 32
SWEEPS = 8
HALO = 8
EXT = TILE + 2 * HALO
LANES = 128
BLOCKS = LANES // PORTALS
OWN = TILE // BLOCKS
GROUPS = EXT // BLOCKS
STEP = EXT // 8
STRIP = 16
FAR = 1000000.0


AROUND = ((-1, 0), (1, 0), (0, -1), (0, 1), (-1, -1), (-1, 1), (1, -1), (1, 1))


def lane_take(values, index):
    return jnp.take_along_axis(values, index, axis=1, mode="promise_in_bounds")


def kernel(
    heights_hbm, blocked_hbm, estimate_hbm, portal_hbm,
    relaxed, merged,
    heights, blocked, estimate, portal, portal_smem,
    ground, strips, ground_in, high, cost_rows,
    field, side_out, side_in, cost, dist, rows, shifts, table, table_in, right_rows,
    load_sem, ground_send, ground_recv, field_send, field_recv, table_send, table_recv,
):
    row_index, col_index = lax.axis_index("row"), lax.axis_index("col")
    row_count, col_count = lax.axis_size("row"), lax.axis_size("col")
    around = [
        (lax.rem(row_index + dr + row_count, row_count), lax.rem(col_index + dc + col_count, col_count))
        for dr, dc in AROUND
    ]

    def other(index, bit):
        return index + bit - 2 * bit * lax.rem(index // bit, 2)

    partners = []
    for level in range(2):
        bit = 1 << level
        partners.append(
            [
                (other(row_index, bit), col_index),
                (row_index, other(col_index, bit)),
                (other(row_index, bit), other(col_index, bit)),
            ]
        )

    loads = [
        pltpu.make_async_copy(source, target, load_sem.at[at])
        for at, (source, target) in enumerate(
            (
                (heights_hbm, heights),
                (blocked_hbm, blocked),
                (portal_hbm, portal),
                (estimate_hbm.at[0:16], estimate.at[0:16]),
                (estimate_hbm.at[48:64], estimate.at[48:64]),
                (estimate_hbm.at[16:48], estimate.at[16:48]),
                (portal_hbm, portal_smem),
            )
        )
    ]
    for load in loads:
        load.start()

    barrier = pltpu.get_barrier_semaphore()
    met = around + partners[1]
    for device in met:
        pl.semaphore_signal(barrier, inc=1, device_id=device, device_id_type=pl.DeviceIdType.MESH)

    def send(source, target, send_sem, recv_sem, device):
        copy = pltpu.make_async_remote_copy(
            src_ref=source, dst_ref=target, send_sem=send_sem, recv_sem=recv_sem,
            device_id=device, device_id_type=pl.DeviceIdType.MESH,
        )
        copy.start()
        return copy

    lane = lax.broadcasted_iota(jnp.int32, (8, LANES), 1)
    sublane = lax.broadcasted_iota(jnp.int32, (8, LANES), 0)
    lane_block = lane // PORTALS
    lane_class = lane % PORTALS

    loads[0].wait()
    loads[1].wait()
    ground[:, 0:TILE] = heights[...]
    ground[:, TILE : 2 * TILE] = blocked[...]
    wide = lax.broadcasted_iota(jnp.int32, (STRIP, LANES), 1)
    west = jnp.zeros((STRIP, LANES), jnp.int32)
    east = jnp.zeros((STRIP, LANES), jnp.int32)
    for part in range(4):
        here = ground[part * STRIP : (part + 1) * STRIP]
        base = part * 32
        in_height = (wide >= base) & (wide < base + 16)
        in_block = (wide >= base + 16) & (wide < base + 32)
        west = jnp.where(in_height, pltpu.roll(here, base % LANES, 1), west)
        west = jnp.where(in_block, pltpu.roll(here, (base + 16 - 64) % LANES, 1), west)
        east = jnp.where(in_height, pltpu.roll(here, (base - 48) % LANES, 1), east)
        east = jnp.where(in_block, pltpu.roll(here, (base + 16 - 112) % LANES, 1), east)
    strips[0] = west
    strips[1] = east

    pl.semaphore_wait(barrier, len(met))

    top, bottom = ground.at[0:STRIP], ground.at[TILE - STRIP : TILE]
    ground_source = {-1: top, 1: bottom}
    ground_copies = []
    for at, (dr, dc) in enumerate(AROUND):
        if dr:
            source = ground_source[dr]
        else:
            source = strips.at[0 if dc < 0 else 1]
        slot = AROUND.index((-dr, -dc))
        ground_copies.append(
            send(source, ground_in.at[slot], ground_send.at[at], ground_recv.at[slot], around[at])
        )

    loads[2].wait()
    own = jnp.broadcast_to(portal[0, 0:1, :], (8, PORTALS))
    portal_cells = jnp.concatenate([own] * BLOCKS, axis=1)
    loads[3].wait()
    loads[4].wait()
    loads[5].wait()
    low = lane < 2 * PORTALS
    even = lane_block % 2 == 0
    swapped_blocks = lane_class + (lane_block + 1 - 2 * (lane_block % 2)) * PORTALS

    def transposed(a):
        t = [None] * 4
        for at in range(2):
            turned = pltpu.roll(jnp.where(low, a[at + 2], a[at]), 2 * PORTALS, 1)
            t[at], t[at + 2] = jnp.where(low, a[at], turned), jnp.where(low, turned, a[at + 2])
        out = [None] * 4
        for at in (0, 2):
            turned = lane_take(jnp.where(even, t[at + 1], t[at]), swapped_blocks)
            out[at], out[at + 1] = jnp.where(even, t[at], turned), jnp.where(even, turned, t[at + 1])
        return out

    def estimates(part, group):
        values = estimate[part * 16 : (part + 1) * 16, group * LANES : (group + 1) * LANES]
        values = values.astype(jnp.float32)
        return values[0:8], values[8:16]

    def prepare(part):
        for first in range(4):
            halves = [estimates(part, first + 4 * at) for at in range(4)]
            for half in range(2):
                row = part * 16 + half * 8
                cell = (row + sublane) * TILE + lane_block * OWN
                for at, values in enumerate(transposed([pieces[half] for pieces in halves])):
                    group = 4 * first + at
                    field[group, HALO + row : HALO + row + 8, :] = jnp.where(
                        portal_cells == cell + group, 0.0, values
                    )

    def edges(part):
        columns = (0, 1, OWN - 2, OWN - 1)
        pieces = [estimates(part, group) for group in columns]
        for half in range(2):
            row = part * 16 + half * 8
            cell = (row + sublane) * TILE + lane_block
            w0, w1, e0, e1 = (
                jnp.where(portal_cells == cell + group * BLOCKS, 0.0, piece[half])
                for group, piece in zip(columns, pieces)
            )
            side_out[0, 0, row : row + 8, :] = jnp.where(even, w0, pltpu.roll(w1, 32, 1))
            side_out[0, 1, row : row + 8, :] = jnp.where(even, pltpu.roll(w0, 96, 1), w1)
            side_out[1, 0, row : row + 8, :] = jnp.where(even, pltpu.roll(e0, 64, 1), pltpu.roll(e1, 96, 1))
            side_out[1, 1, row : row + 8, :] = jnp.where(even, pltpu.roll(e0, 32, 1), pltpu.roll(e1, 64, 1))

    prepare(0)
    prepare(3)
    for part in range(4):
        edges(part)

    field_copies = []
    for at, (dr, dc) in enumerate(AROUND):
        row_from, row_to, row_len = {
            -1: (0, HALO + TILE, HALO), 0: (0, HALO, TILE), 1: (TILE - HALO, 0, HALO)
        }[dr]
        if dc:
            side = 0 if dc < 0 else 1
            source = side_out.at[side, :, pl.ds(row_from, row_len), :]
            target = side_in.at[side, :, pl.ds(row_to, row_len), :]
        else:
            source = field.at[:, pl.ds(HALO + row_from, row_len), :]
            target = field.at[:, pl.ds(row_to, row_len), :]
        slot = AROUND.index((-dr, -dc))
        field_copies.append(send(source, target, field_send.at[at], field_recv.at[slot], around[at]))

    prepare(1)
    prepare(2)

    for copy in ground_copies:
        copy.wait_recv()
    slots = {step: at for at, step in enumerate(AROUND)}

    def lay(row, west_height, middle, east_height, west_block, east_block):
        height = jnp.where(wide < 16, west_height, jnp.where(wide < 80, pltpu.roll(middle, 16, 1), east_height))
        block = jnp.where(wide < 16, west_block, jnp.where(wide < 80, pltpu.roll(middle, 80, 1), east_block))
        high[0, row : row + STRIP, :] = height.astype(jnp.float32)
        high[1, row : row + STRIP, :] = block.astype(jnp.float32)

    for dr, row in ((-1, 0), (1, STRIP + TILE)):
        west_in, middle, east_in = (ground_in[slots[(dr, dc)]] for dc in (-1, 0, 1))
        lay(
            row, pltpu.roll(west_in, 80, 1), middle, pltpu.roll(east_in, 80, 1),
            pltpu.roll(west_in, 16, 1), pltpu.roll(east_in, 16, 1),
        )
    west_in, east_in = ground_in[slots[(0, -1)]], ground_in[slots[(0, 1)]]
    for part in range(4):
        base = part * 32
        lay(
            STRIP + part * STRIP,
            pltpu.roll(west_in, (-base) % LANES, 1),
            ground[part * STRIP : (part + 1) * STRIP],
            pltpu.roll(east_in, (80 - base) % LANES, 1),
            pltpu.roll(west_in, (-base - 16) % LANES, 1),
            pltpu.roll(east_in, (64 - base) % LANES, 1),
        )

    @pl.when(row_index == 0)
    def _():
        high[0, STRIP - 1 : STRIP, :] = high[0, STRIP : STRIP + 1, :]

    @pl.when(row_index == row_count - 1)
    def _():
        high[0, STRIP + TILE : STRIP + TILE + 1, :] = high[0, STRIP + TILE - 1 : STRIP + TILE, :]

    shift = STRIP - HALO
    near = high[0, shift : shift + EXT, :]
    up = high[0, shift - 1 : shift - 1 + EXT, :]
    down = high[0, shift + 1 : shift + 1 + EXT, :]
    col = lax.broadcasted_iota(jnp.int32, (EXT, LANES), 1) - STRIP
    row = lax.broadcasted_iota(jnp.int32, (EXT, LANES), 0) - HALO
    grid_col = col_index * TILE + col
    grid_row = row_index * TILE + row
    before = jnp.where(grid_col == 0, near, pltpu.roll(near, 1, 1))
    after = jnp.where(grid_col == col_count * TILE - 1, near, pltpu.roll(near, LANES - 1, 1))
    grad_x = (after - before) * 0.01
    grad_y = (down - up) * 0.01
    grad_sq = grad_x * grad_x + grad_y * grad_y
    step_cost = (
        1.0 + 2.0 * grad_sq + 0.5 * grad_y / jnp.sqrt(1.0 + grad_sq)
        + 30.0 * high[1, shift : shift + EXT, :]
    )
    inside = (
        (grid_row >= 0) & (grid_row < row_count * TILE)
        & (grid_col >= 0) & (grid_col < col_count * TILE)
    )
    cost_rows[...] = jnp.where(inside, step_cost, FAR)
    first_column = STRIP + lane_block * OWN
    halo_shift = jnp.where(low, TILE + 4 * lane_block, 4 * lane_block - 16) - lane_block * OWN
    for at in range(STEP):
        values = cost_rows[pl.ds(at, 8, stride=STEP), :]
        for group in range(GROUPS):
            cost[group, at] = lane_take(values, first_column + (group if group < OWN else group - OWN + halo_shift))

    for copy in field_copies:
        copy.wait_recv()

    def start(group, at, distance):
        here = cost[group, at]
        dist[group, at] = jnp.where(here >= FAR, FAR, distance + 0.5 * here)

    for at in range(STEP):
        for group in range(OWN):
            start(group, at, field[group, pl.ds(at, 8, stride=STEP), :])
        for piece in range(2):
            from_east = side_in[0, piece, pl.ds(at, 8, stride=STEP), :]
            from_west = side_in[1, piece, pl.ds(at, 8, stride=STEP), :]
            start(OWN + piece, at, jnp.where(low, from_east, from_west))
            start(OWN + piece + 2, at, pltpu.roll(jnp.where(low, from_west, from_east), 64, 1))

    first_block, last_block = lane_block == 0, lane_block == BLOCKS - 1

    def sweep(_, carry):
        def pairs_of(here, east_of):
            below = east_of[1:] + [pltpu.roll(east_of[0], 7, 0)]
            return [jnp.minimum(a, b) for a, b in zip(here, below)]

        def column(group):
            return [dist[group, at] for at in range(STEP)]

        own_first, halo_first = column(0), column(OWN)
        own_pairs = pairs_of(
            column(OWN - 1),
            [pltpu.roll(jnp.where(first_block, a, b), LANES - PORTALS, 1) for a, b in zip(halo_first, own_first)],
        )
        halo_pairs = pairs_of(
            column(GROUPS - 1),
            [pltpu.roll(jnp.where(first_block, a, b), LANES - PORTALS, 1) for a, b in zip(own_first, halo_first)],
        )
        own_west = [pltpu.roll(jnp.where(last_block, a, b), PORTALS, 1) for a, b in zip(halo_pairs, own_pairs)]
        halo_west = [pltpu.roll(jnp.where(last_block, a, b), PORTALS, 1) for a, b in zip(own_pairs, halo_pairs)]
        for begin, end, west_of, end_pairs in ((0, OWN, own_west, own_pairs), (OWN, GROUPS, halo_west, halo_pairs)):
            now = own_first if begin == 0 else column(begin)
            for group in range(begin, end):
                if group < end - 1:
                    later = column(group + 1)
                    pairs = pairs_of(now, later)
                else:
                    pairs = end_pairs
                north = [pltpu.roll(pairs[STEP - 1], 1, 0)] + pairs[:-1]
                for at in range(STEP):
                    nearest = cost[group, at] + jnp.minimum(north[at], west_of[at])
                    dist[group, at] = jnp.minimum(now[at], nearest)
                west_of, now = pairs, later
        return carry

    lax.fori_loop(0, SWEEPS, sweep, 0)

    for copy in field_copies:
        copy.wait_send()
    for group in range(OWN):
        for at in range(STEP):
            field[group, pl.ds(at, 8, stride=STEP), :] = dist[group, at] - 0.5 * cost[group, at]

    loads[6].wait()
    for at in range(PORTALS):
        cell = portal_smem[0, 0, at]
        column_at = cell % TILE
        rows[at : at + 1, :] = field[column_at % OWN, pl.ds(HALO + cell // TILE, 1), :]
        shifts[at : at + 1, :] = jnp.full((1, LANES), column_at // OWN * PORTALS, jnp.int32)
    first = jnp.zeros((8, LANES), jnp.float32)
    for part in range(4):
        index = shifts[part * 8 : part * 8 + 8, :] + lane_class
        first = jnp.where(lane_block == part, lane_take(rows[part * 8 : part * 8 + 8, :], index), first)
    table[0] = first

    table_copies = []

    def exchange(level):
        copies = [
            send(
                table.at[level], table_in.at[3 * level + at],
                table_send.at[3 * level + at], table_recv.at[3 * level + at], device,
            )
            for at, device in enumerate(partners[level])
        ]
        table_copies.extend(copies)
        return copies

    def left_of(values):
        return [lane_take(values, lane_block * PORTALS + at) for at in range(PORTALS)]

    def right_of(values, slot):
        for part in range(4):
            right_rows[slot, part * 8 : part * 8 + 8, :] = lane_take(values, lane_class + part * PORTALS)
        return [
            jnp.broadcast_to(right_rows[slot, at : at + 1, :], (8, LANES)) for at in range(PORTALS)
        ]

    def minplus(left, right):
        sums = [a + b for a, b in zip(left, right)]
        while len(sums) > 1:
            sums = [jnp.minimum(a, b) for a, b in zip(sums[::2], sums[1::2])]
        return sums[0]

    def pair(near_table, near_left, near_right, far_right):
        through = minplus(near_left, far_right)
        return jnp.minimum(near_table, minplus(left_of(through), near_right))

    def relax_out(part):
        for first_at in range(4):
            for_rows = [
                transposed(
                    [
                        field[4 * first_at + at, HALO + part * 16 + half * 8 : HALO + part * 16 + half * 8 + 8, :]
                        for at in range(4)
                    ]
                )
                for half in range(2)
            ]
            for at in range(4):
                group = first_at + 4 * at
                values = jnp.concatenate([for_rows[0][at], for_rows[1][at]], axis=0)
                relaxed[part * 16 : part * 16 + 16, group * LANES : (group + 1) * LANES] = values.astype(jnp.bfloat16)

    now = first
    for level in range(2):
        copies = exchange(level)
        now_left, now_right = left_of(now), right_of(now, 6 * level)
        relax_out(2 * level)
        relax_out(2 * level + 1)
        for copy in copies:
            copy.wait_recv()
        by_row, by_col, by_both = (table_in[3 * level + at] for at in range(3))
        here = pair(now, now_left, now_right, right_of(by_row, 6 * level + 1))
        there = pair(by_col, left_of(by_col), right_of(by_col, 6 * level + 2), right_of(by_both, 6 * level + 3))
        now = pair(here, left_of(here), right_of(here, 6 * level + 4), right_of(there, 6 * level + 5))
        if level == 0:
            table[1] = now
    now = now * 0.0625
    for part in range(4):
        merged[0, 0, part * 8 : part * 8 + 8, :] = now[:, part * PORTALS : (part + 1) * PORTALS]

    for copy in ground_copies + table_copies:
        copy.wait_send()


def body(heights, blocked, estimate, portal_index):
    in_hbm = pl.BlockSpec(memory_space=pltpu.HBM)
    in_vmem = pl.BlockSpec(memory_space=pltpu.VMEM)
    return pl.pallas_call(
        kernel,
        out_shape=(
            jax.ShapeDtypeStruct(estimate.shape, jnp.bfloat16),
            jax.ShapeDtypeStruct((1, 1, PORTALS, PORTALS), jnp.float32),
        ),
        in_specs=[in_hbm] * 4,
        out_specs=(in_vmem, in_vmem),
        scratch_shapes=[
            pltpu.VMEM((TILE, TILE), jnp.int32),
            pltpu.VMEM((TILE, TILE), jnp.int32),
            pltpu.VMEM((TILE, TILE * PORTALS), jnp.bfloat16),
            pltpu.VMEM((1, 1, PORTALS), jnp.int32),
            pltpu.SMEM((1, 1, PORTALS), jnp.int32),
            pltpu.VMEM((TILE, LANES), jnp.int32),
            pltpu.VMEM((2, STRIP, LANES), jnp.int32),
            pltpu.VMEM((8, STRIP, LANES), jnp.int32),
            pltpu.VMEM((2, TILE + 2 * STRIP, LANES), jnp.float32),
            pltpu.VMEM((EXT, LANES), jnp.float32),
            pltpu.VMEM((OWN, EXT, LANES), jnp.float32),
            pltpu.VMEM((2, 2, TILE, LANES), jnp.float32),
            pltpu.VMEM((2, 2, EXT, LANES), jnp.float32),
            pltpu.VMEM((GROUPS, STEP, 8, LANES), jnp.float32),
            pltpu.VMEM((GROUPS, STEP, 8, LANES), jnp.float32),
            pltpu.VMEM((PORTALS, LANES), jnp.float32),
            pltpu.VMEM((PORTALS, LANES), jnp.int32),
            pltpu.VMEM((2, 8, LANES), jnp.float32),
            pltpu.VMEM((6, 8, LANES), jnp.float32),
            pltpu.VMEM((12, PORTALS, LANES), jnp.float32),
            pltpu.SemaphoreType.DMA((7,)),
            pltpu.SemaphoreType.DMA((8,)),
            pltpu.SemaphoreType.DMA((8,)),
            pltpu.SemaphoreType.DMA((8,)),
            pltpu.SemaphoreType.DMA((8,)),
            pltpu.SemaphoreType.DMA((6,)),
            pltpu.SemaphoreType.DMA((6,)),
        ],
        compiler_params=pltpu.CompilerParams(
            collective_id=0, has_side_effects=True, vmem_limit_bytes=16 * 2**20
        ),
    )(heights, blocked, estimate, portal_index)


def solution(mesh):
    placed = (P("row", "col"), P("row", "col"), P("row", "col"), P("row", "col", None))
    return jax.shard_map(
        body,
        mesh=mesh,
        in_specs=placed,
        out_specs=(P("row", "col"), P("row", "col", None, None)),
        check_vma=False,
    )
```

```python
import functools

import jax
import jax.numpy as jnp
from jax import lax
from jax.experimental import pallas as pl
from jax.experimental.pallas import tpu as pltpu
from jax.sharding import PartitionSpec as P

TILE = 64
PORTALS = 32
SWEEPS = 8
HALO = 8
EXT = TILE + 2 * HALO
LANES = 128
BLOCKS = LANES // PORTALS
OWN = TILE // BLOCKS
GROUPS = EXT // BLOCKS
STEP = EXT // 8
STRIP = 16
FAR = 1000000.0


AROUND = ((-1, -1), (-1, 1), (1, -1), (1, 1), (-1, 0), (1, 0), (0, -1), (0, 1))


def lane_take(values, index):
    return jnp.take_along_axis(values, index, axis=1, mode="promise_in_bounds")


def kernel(
    heights_hbm, blocked_hbm, estimate_hbm, portal_hbm,
    relaxed, merged,
    heights, blocked, estimate, portal, portal_smem,
    ground, strips, ground_in, high, cost_rows,
    field, side_out, side_in, cost, dist, rows, shifts, table, table_in, right_rows,
    load_sem, ground_send, ground_recv, field_send, field_recv, table_send, table_recv,
):
    row_index, col_index = lax.axis_index("row"), lax.axis_index("col")
    row_count, col_count = lax.axis_size("row"), lax.axis_size("col")
    around = [
        (lax.rem(row_index + dr + row_count, row_count), lax.rem(col_index + dc + col_count, col_count))
        for dr, dc in AROUND
    ]

    def other(index, bit):
        return index + bit - 2 * bit * lax.rem(index // bit, 2)

    partners = []
    for level in range(2):
        bit = 1 << level
        partners.append(
            [
                (other(row_index, bit), col_index),
                (row_index, other(col_index, bit)),
                (other(row_index, bit), other(col_index, bit)),
            ]
        )

    loads = [
        pltpu.make_async_copy(source, target, load_sem.at[at])
        for at, (source, target) in enumerate(
            (
                (heights_hbm, heights),
                (blocked_hbm, blocked),
                (portal_hbm, portal),
                (estimate_hbm.at[0:16], estimate.at[0:16]),
                (estimate_hbm.at[48:64], estimate.at[48:64]),
                (estimate_hbm.at[16:48], estimate.at[16:48]),
                (portal_hbm, portal_smem),
            )
        )
    ]
    for load in loads:
        load.start()

    barrier = pltpu.get_barrier_semaphore()
    met = around + partners[1]
    for device in met:
        pl.semaphore_signal(barrier, inc=1, device_id=device, device_id_type=pl.DeviceIdType.MESH)

    def send(source, target, send_sem, recv_sem, device):
        copy = pltpu.make_async_remote_copy(
            src_ref=source, dst_ref=target, send_sem=send_sem, recv_sem=recv_sem,
            device_id=device, device_id_type=pl.DeviceIdType.MESH,
        )
        copy.start()
        return copy

    lane = lax.broadcasted_iota(jnp.int32, (8, LANES), 1)
    sublane = lax.broadcasted_iota(jnp.int32, (8, LANES), 0)
    lane_block = lane // PORTALS
    lane_class = lane % PORTALS

    loads[0].wait()
    loads[1].wait()
    ground[:, 0:TILE] = heights[...]
    ground[:, TILE : 2 * TILE] = blocked[...]
    wide = lax.broadcasted_iota(jnp.int32, (STRIP, LANES), 1)
    west = jnp.zeros((STRIP, LANES), jnp.int32)
    east = jnp.zeros((STRIP, LANES), jnp.int32)
    for part in range(4):
        here = ground[part * STRIP : (part + 1) * STRIP]
        base = part * 32
        in_height = (wide >= base) & (wide < base + 16)
        in_block = (wide >= base + 16) & (wide < base + 32)
        west = jnp.where(in_height, pltpu.roll(here, base % LANES, 1), west)
        west = jnp.where(in_block, pltpu.roll(here, (base + 16 - 64) % LANES, 1), west)
        east = jnp.where(in_height, pltpu.roll(here, (base - 48) % LANES, 1), east)
        east = jnp.where(in_block, pltpu.roll(here, (base + 16 - 112) % LANES, 1), east)
    strips[0] = west
    strips[1] = east

    pl.semaphore_wait(barrier, len(met))

    top, bottom = ground.at[0:STRIP], ground.at[TILE - STRIP : TILE]
    ground_source = {-1: top, 1: bottom}
    ground_copies = []
    for at, (dr, dc) in enumerate(AROUND):
        if dr:
            source = ground_source[dr]
        else:
            source = strips.at[0 if dc < 0 else 1]
        slot = AROUND.index((-dr, -dc))
        ground_copies.append(
            send(source, ground_in.at[slot], ground_send.at[at], ground_recv.at[slot], around[at])
        )

    loads[2].wait()
    own = jnp.broadcast_to(portal[0, 0:1, :], (8, PORTALS))
    portal_cells = jnp.concatenate([own] * BLOCKS, axis=1)
    loads[3].wait()
    loads[4].wait()
    loads[5].wait()
    low = lane < 2 * PORTALS
    even = lane_block % 2 == 0
    swapped_blocks = lane_class + (lane_block + 1 - 2 * (lane_block % 2)) * PORTALS

    def transposed(a):
        t = [None] * 4
        for at in range(2):
            turned = pltpu.roll(jnp.where(low, a[at + 2], a[at]), 2 * PORTALS, 1)
            t[at], t[at + 2] = jnp.where(low, a[at], turned), jnp.where(low, turned, a[at + 2])
        out = [None] * 4
        for at in (0, 2):
            turned = lane_take(jnp.where(even, t[at + 1], t[at]), swapped_blocks)
            out[at], out[at + 1] = jnp.where(even, t[at], turned), jnp.where(even, turned, t[at + 1])
        return out

    def estimates(part, group):
        values = estimate[part * 16 : (part + 1) * 16, group * LANES : (group + 1) * LANES]
        values = values.astype(jnp.float32)
        return values[0:8], values[8:16]

    def prepare(part):
        for first in range(4):
            halves = [estimates(part, first + 4 * at) for at in range(4)]
            for half in range(2):
                row = part * 16 + half * 8
                cell = (row + sublane) * TILE + lane_block * OWN
                for at, values in enumerate(transposed([pieces[half] for pieces in halves])):
                    group = 4 * first + at
                    field[group, HALO + row : HALO + row + 8, :] = jnp.where(
                        portal_cells == cell + group, 0.0, values
                    )

    def edges(part):
        columns = (0, 1, OWN - 2, OWN - 1)
        pieces = [estimates(part, group) for group in columns]
        for half in range(2):
            row = part * 16 + half * 8
            cell = (row + sublane) * TILE + lane_block
            w0, w1, e0, e1 = (
                jnp.where(portal_cells == cell + group * BLOCKS, 0.0, piece[half])
                for group, piece in zip(columns, pieces)
            )
            side_out[0, 0, row : row + 8, :] = jnp.where(even, w0, pltpu.roll(w1, 32, 1))
            side_out[0, 1, row : row + 8, :] = jnp.where(even, pltpu.roll(w0, 96, 1), w1)
            side_out[1, 0, row : row + 8, :] = jnp.where(even, pltpu.roll(e0, 64, 1), pltpu.roll(e1, 96, 1))
            side_out[1, 1, row : row + 8, :] = jnp.where(even, pltpu.roll(e0, 32, 1), pltpu.roll(e1, 64, 1))

    prepare(0)
    prepare(3)
    for part in range(4):
        edges(part)

    field_copies = []
    for at, (dr, dc) in enumerate(AROUND):
        row_from, row_to, row_len = {
            -1: (0, HALO + TILE, HALO), 0: (0, HALO, TILE), 1: (TILE - HALO, 0, HALO)
        }[dr]
        if dc:
            side = 0 if dc < 0 else 1
            source = side_out.at[side, :, pl.ds(row_from, row_len), :]
            target = side_in.at[side, :, pl.ds(row_to, row_len), :]
        else:
            source = field.at[:, pl.ds(HALO + row_from, row_len), :]
            target = field.at[:, pl.ds(row_to, row_len), :]
        slot = AROUND.index((-dr, -dc))
        field_copies.append(send(source, target, field_send.at[at], field_recv.at[slot], around[at]))

    prepare(1)
    prepare(2)

    for copy in ground_copies:
        copy.wait_recv()
    slots = {step: at for at, step in enumerate(AROUND)}

    def lay(row, west_height, middle, east_height, west_block, east_block):
        height = jnp.where(wide < 16, west_height, jnp.where(wide < 80, pltpu.roll(middle, 16, 1), east_height))
        block = jnp.where(wide < 16, west_block, jnp.where(wide < 80, pltpu.roll(middle, 80, 1), east_block))
        high[0, row : row + STRIP, :] = height.astype(jnp.float32)
        high[1, row : row + STRIP, :] = block.astype(jnp.float32)

    for dr, row in ((-1, 0), (1, STRIP + TILE)):
        west_in, middle, east_in = (ground_in[slots[(dr, dc)]] for dc in (-1, 0, 1))
        lay(
            row, pltpu.roll(west_in, 80, 1), middle, pltpu.roll(east_in, 80, 1),
            pltpu.roll(west_in, 16, 1), pltpu.roll(east_in, 16, 1),
        )
    west_in, east_in = ground_in[slots[(0, -1)]], ground_in[slots[(0, 1)]]
    for part in range(4):
        base = part * 32
        lay(
            STRIP + part * STRIP,
            pltpu.roll(west_in, (-base) % LANES, 1),
            ground[part * STRIP : (part + 1) * STRIP],
            pltpu.roll(east_in, (80 - base) % LANES, 1),
            pltpu.roll(west_in, (-base - 16) % LANES, 1),
            pltpu.roll(east_in, (64 - base) % LANES, 1),
        )

    @pl.when(row_index == 0)
    def _():
        high[0, STRIP - 1 : STRIP, :] = high[0, STRIP : STRIP + 1, :]

    @pl.when(row_index == row_count - 1)
    def _():
        high[0, STRIP + TILE : STRIP + TILE + 1, :] = high[0, STRIP + TILE - 1 : STRIP + TILE, :]

    shift = STRIP - HALO
    near = high[0, shift : shift + EXT, :]
    up = high[0, shift - 1 : shift - 1 + EXT, :]
    down = high[0, shift + 1 : shift + 1 + EXT, :]
    col = lax.broadcasted_iota(jnp.int32, (EXT, LANES), 1) - STRIP
    row = lax.broadcasted_iota(jnp.int32, (EXT, LANES), 0) - HALO
    grid_col = col_index * TILE + col
    grid_row = row_index * TILE + row
    before = jnp.where(grid_col == 0, near, pltpu.roll(near, 1, 1))
    after = jnp.where(grid_col == col_count * TILE - 1, near, pltpu.roll(near, LANES - 1, 1))
    grad_x = (after - before) * 0.01
    grad_y = (down - up) * 0.01
    grad_sq = grad_x * grad_x + grad_y * grad_y
    step_cost = (
        1.0 + 2.0 * grad_sq + 0.5 * grad_y / jnp.sqrt(1.0 + grad_sq)
        + 30.0 * high[1, shift : shift + EXT, :]
    )
    inside = (
        (grid_row >= 0) & (grid_row < row_count * TILE)
        & (grid_col >= 0) & (grid_col < col_count * TILE)
    )
    cost_rows[...] = jnp.where(inside, step_cost, FAR)
    first_column = STRIP + lane_block * OWN
    halo_shift = jnp.where(low, TILE + 4 * lane_block, 4 * lane_block - 16) - lane_block * OWN
    for at in range(STEP):
        values = cost_rows[pl.ds(at, 8, stride=STEP), :]
        for group in range(GROUPS):
            cost[group, at] = lane_take(values, first_column + (group if group < OWN else group - OWN + halo_shift))

    for copy in field_copies:
        copy.wait_recv()

    def start(group, at, distance):
        here = cost[group, at]
        dist[group, at] = jnp.where(here >= FAR, FAR, distance + 0.5 * here)

    for at in range(STEP):
        for group in range(OWN):
            start(group, at, field[group, pl.ds(at, 8, stride=STEP), :])
        for piece in range(2):
            from_east = side_in[0, piece, pl.ds(at, 8, stride=STEP), :]
            from_west = side_in[1, piece, pl.ds(at, 8, stride=STEP), :]
            start(OWN + piece, at, jnp.where(low, from_east, from_west))
            start(OWN + piece + 2, at, pltpu.roll(jnp.where(low, from_west, from_east), 64, 1))

    first_block, last_block = lane_block == 0, lane_block == BLOCKS - 1

    def sweep(_, carry):
        def pairs_of(here, east_of):
            below = east_of[1:] + [pltpu.roll(east_of[0], 7, 0)]
            return [jnp.minimum(a, b) for a, b in zip(here, below)]

        def column(group):
            return [dist[group, at] for at in range(STEP)]

        own_first, halo_first = column(0), column(OWN)
        own_pairs = pairs_of(
            column(OWN - 1),
            [pltpu.roll(jnp.where(first_block, a, b), LANES - PORTALS, 1) for a, b in zip(halo_first, own_first)],
        )
        halo_pairs = pairs_of(
            column(GROUPS - 1),
            [pltpu.roll(jnp.where(first_block, a, b), LANES - PORTALS, 1) for a, b in zip(own_first, halo_first)],
        )
        own_west = [pltpu.roll(jnp.where(last_block, a, b), PORTALS, 1) for a, b in zip(halo_pairs, own_pairs)]
        halo_west = [pltpu.roll(jnp.where(last_block, a, b), PORTALS, 1) for a, b in zip(own_pairs, halo_pairs)]
        for begin, end, west_of, end_pairs in ((0, OWN, own_west, own_pairs), (OWN, GROUPS, halo_west, halo_pairs)):
            now = own_first if begin == 0 else column(begin)
            for group in range(begin, end):
                if group < end - 1:
                    later = column(group + 1)
                    pairs = pairs_of(now, later)
                else:
                    pairs = end_pairs
                north = [pltpu.roll(pairs[STEP - 1], 1, 0)] + pairs[:-1]
                for at in range(STEP):
                    nearest = cost[group, at] + jnp.minimum(north[at], west_of[at])
                    dist[group, at] = jnp.minimum(now[at], nearest)
                west_of, now = pairs, later
        return carry

    lax.fori_loop(0, SWEEPS, sweep, 0)

    for copy in field_copies:
        copy.wait_send()
    for group in range(OWN):
        for at in range(STEP):
            field[group, pl.ds(at, 8, stride=STEP), :] = dist[group, at] - 0.5 * cost[group, at]

    loads[6].wait()
    for at in range(PORTALS):
        cell = portal_smem[0, 0, at]
        column_at = cell % TILE
        rows[at : at + 1, :] = field[column_at % OWN, pl.ds(HALO + cell // TILE, 1), :]
        shifts[at : at + 1, :] = jnp.full((1, LANES), column_at // OWN * PORTALS, jnp.int32)
    first = jnp.zeros((8, LANES), jnp.float32)
    for part in range(4):
        index = shifts[part * 8 : part * 8 + 8, :] + lane_class
        first = jnp.where(lane_block == part, lane_take(rows[part * 8 : part * 8 + 8, :], index), first)
    table[0] = first

    table_copies = []

    def exchange(level):
        copies = [
            send(
                table.at[level], table_in.at[3 * level + at],
                table_send.at[3 * level + at], table_recv.at[3 * level + at], device,
            )
            for at, device in reversed(tuple(enumerate(partners[level])))
        ]
        table_copies.extend(copies)
        return copies

    def left_of(values):
        return [lane_take(values, lane_block * PORTALS + at) for at in range(PORTALS)]

    def right_of(values, slot):
        for part in range(4):
            right_rows[slot, part * 8 : part * 8 + 8, :] = lane_take(values, lane_class + part * PORTALS)
        return [
            jnp.broadcast_to(right_rows[slot, at : at + 1, :], (8, LANES)) for at in range(PORTALS)
        ]

    def minplus(left, right):
        sums = [a + b for a, b in zip(left, right)]
        while len(sums) > 1:
            sums = [jnp.minimum(a, b) for a, b in zip(sums[::2], sums[1::2])]
        return sums[0]

    def pair(near_table, near_left, near_right, far_right):
        through = minplus(near_left, far_right)
        return jnp.minimum(near_table, minplus(left_of(through), near_right))

    def relax_out(part):
        for first_at in range(4):
            for_rows = [
                transposed(
                    [
                        field[4 * first_at + at, HALO + part * 16 + half * 8 : HALO + part * 16 + half * 8 + 8, :]
                        for at in range(4)
                    ]
                )
                for half in range(2)
            ]
            for at in range(4):
                group = first_at + 4 * at
                values = jnp.concatenate([for_rows[0][at], for_rows[1][at]], axis=0)
                relaxed[part * 16 : part * 16 + 16, group * LANES : (group + 1) * LANES] = values.astype(jnp.bfloat16)

    now = first
    for level in range(2):
        copies = exchange(level)
        now_left, now_right = left_of(now), right_of(now, 6 * level)
        relax_out(2 * level)
        relax_out(2 * level + 1)
        for copy in copies:
            copy.wait_recv()
        by_row, by_col, by_both = (table_in[3 * level + at] for at in range(3))
        here = pair(now, now_left, now_right, right_of(by_row, 6 * level + 1))
        there = pair(by_col, left_of(by_col), right_of(by_col, 6 * level + 2), right_of(by_both, 6 * level + 3))
        now = pair(here, left_of(here), right_of(here, 6 * level + 4), right_of(there, 6 * level + 5))
        if level == 0:
            table[1] = now
    now = now * 0.0625
    for part in range(4):
        merged[0, 0, part * 8 : part * 8 + 8, :] = now[:, part * PORTALS : (part + 1) * PORTALS]

    for copy in ground_copies + table_copies:
        copy.wait_send()


def hand_out(relaxed_in, merged_in, relaxed, merged, sem):
    copies = [
        pltpu.make_async_copy(relaxed_in, relaxed, sem.at[0]),
        pltpu.make_async_copy(merged_in, merged, sem.at[1]),
    ]
    for copy in copies:
        copy.start()
    for copy in copies:
        copy.wait()


def body(heights, blocked, estimate, portal_index):
    in_hbm = pl.BlockSpec(memory_space=pltpu.HBM)
    in_vmem = pl.BlockSpec(memory_space=pltpu.VMEM)
    outs = (
        jax.ShapeDtypeStruct(estimate.shape, jnp.bfloat16),
        jax.ShapeDtypeStruct((1, 1, PORTALS, PORTALS), jnp.float32),
    )
    results = pl.pallas_call(
        kernel,
        out_shape=outs,
        in_specs=[in_hbm] * 4,
        out_specs=(in_vmem, in_vmem),
        scratch_shapes=[
            pltpu.VMEM((TILE, TILE), jnp.int32),
            pltpu.VMEM((TILE, TILE), jnp.int32),
            pltpu.VMEM((TILE, TILE * PORTALS), jnp.bfloat16),
            pltpu.VMEM((1, 1, PORTALS), jnp.int32),
            pltpu.SMEM((1, 1, PORTALS), jnp.int32),
            pltpu.VMEM((TILE, LANES), jnp.int32),
            pltpu.VMEM((2, STRIP, LANES), jnp.int32),
            pltpu.VMEM((8, STRIP, LANES), jnp.int32),
            pltpu.VMEM((2, TILE + 2 * STRIP, LANES), jnp.float32),
            pltpu.VMEM((EXT, LANES), jnp.float32),
            pltpu.VMEM((OWN, EXT, LANES), jnp.float32),
            pltpu.VMEM((2, 2, TILE, LANES), jnp.float32),
            pltpu.VMEM((2, 2, EXT, LANES), jnp.float32),
            pltpu.VMEM((GROUPS, STEP, 8, LANES), jnp.float32),
            pltpu.VMEM((GROUPS, STEP, 8, LANES), jnp.float32),
            pltpu.VMEM((PORTALS, LANES), jnp.float32),
            pltpu.VMEM((PORTALS, LANES), jnp.int32),
            pltpu.VMEM((2, 8, LANES), jnp.float32),
            pltpu.VMEM((6, 8, LANES), jnp.float32),
            pltpu.VMEM((12, PORTALS, LANES), jnp.float32),
            pltpu.SemaphoreType.DMA((7,)),
            pltpu.SemaphoreType.DMA((8,)),
            pltpu.SemaphoreType.DMA((8,)),
            pltpu.SemaphoreType.DMA((8,)),
            pltpu.SemaphoreType.DMA((8,)),
            pltpu.SemaphoreType.DMA((6,)),
            pltpu.SemaphoreType.DMA((6,)),
        ],
        compiler_params=pltpu.CompilerParams(
            collective_id=0, has_side_effects=True, vmem_limit_bytes=16 * 2**20
        ),
    )(*(pltpu.with_memory_space_constraint(x, pltpu.HBM) for x in (heights, blocked, estimate, portal_index)))
    return pl.pallas_call(
        hand_out,
        out_shape=tuple(pltpu.HBM(x.shape, x.dtype) for x in outs),
        in_specs=[in_vmem] * 2,
        out_specs=[in_hbm] * 2,
        scratch_shapes=[pltpu.SemaphoreType.DMA((2,))],
        compiler_params=pltpu.CompilerParams(vmem_limit_bytes=2**20),
    )(*(pltpu.with_memory_space_constraint(x, pltpu.VMEM) for x in results))


def solution(mesh):
    placed = (P("row", "col"), P("row", "col"), P("row", "col"), P("row", "col", None))
    return jax.shard_map(
        body,
        mesh=mesh,
        in_specs=placed,
        out_specs=(P("row", "col"), P("row", "col", None, None)),
        check_vma=False,
    )
```

```python
import functools

import jax
import jax.numpy as jnp
from jax import lax
from jax.experimental import pallas as pl
from jax.experimental.pallas import tpu as pltpu
from jax.sharding import PartitionSpec as P

TILE = 64
PORTALS = 32
SWEEPS = 8
HALO = 8
EXT = TILE + 2 * HALO
LANES = 128
BLOCKS = LANES // PORTALS
OWN = TILE // BLOCKS
GROUPS = EXT // BLOCKS
STEP = EXT // 8
STRIP = 16
FAR = 1000000.0


AROUND = ((-1, -1), (-1, 1), (1, -1), (1, 1), (-1, 0), (1, 0), (0, -1), (0, 1))


def lane_take(values, index):
    return jnp.take_along_axis(values, index, axis=1, mode="promise_in_bounds")


def kernel(
    heights_hbm, blocked_hbm, estimate_hbm, portal_hbm,
    relaxed, merged,
    heights, blocked, estimate, portal, portal_smem,
    ground, strips, ground_in, high, cost_rows,
    field, side_out, side_in, cost, dist, rows, shifts, table, table_in, right_rows,
    load_sem, ground_send, ground_recv, field_send, field_recv, table_send, table_recv,
):
    row_index, col_index = lax.axis_index("row"), lax.axis_index("col")
    row_count, col_count = lax.axis_size("row"), lax.axis_size("col")
    around = [
        (lax.rem(row_index + dr + row_count, row_count), lax.rem(col_index + dc + col_count, col_count))
        for dr, dc in AROUND
    ]

    def other(index, bit):
        return index + bit - 2 * bit * lax.rem(index // bit, 2)

    partners = []
    for level in range(2):
        bit = 1 << level
        partners.append(
            [
                (other(row_index, bit), col_index),
                (row_index, other(col_index, bit)),
                (other(row_index, bit), other(col_index, bit)),
            ]
        )

    loads = [
        pltpu.make_async_copy(source, target, load_sem.at[at])
        for at, (source, target) in enumerate(
            (
                (heights_hbm, heights),
                (blocked_hbm, blocked),
                (portal_hbm, portal),
                (estimate_hbm.at[0:16], estimate.at[0:16]),
                (estimate_hbm.at[48:64], estimate.at[48:64]),
                (estimate_hbm.at[16:48], estimate.at[16:48]),
                (portal_hbm, portal_smem),
            )
        )
    ]
    for load in loads:
        load.start()

    barrier = pltpu.get_barrier_semaphore()
    met = around + partners[1]
    for device in met:
        pl.semaphore_signal(barrier, inc=1, device_id=device, device_id_type=pl.DeviceIdType.MESH)

    def send(source, target, send_sem, recv_sem, device):
        copy = pltpu.make_async_remote_copy(
            src_ref=source, dst_ref=target, send_sem=send_sem, recv_sem=recv_sem,
            device_id=device, device_id_type=pl.DeviceIdType.MESH,
        )
        copy.start()
        return copy

    lane = lax.broadcasted_iota(jnp.int32, (8, LANES), 1)
    sublane = lax.broadcasted_iota(jnp.int32, (8, LANES), 0)
    lane_block = lane // PORTALS
    lane_class = lane % PORTALS

    loads[0].wait()
    loads[1].wait()
    ground[:, 0:TILE] = heights[...]
    ground[:, TILE : 2 * TILE] = blocked[...]
    wide = lax.broadcasted_iota(jnp.int32, (STRIP, LANES), 1)
    west = jnp.zeros((STRIP, LANES), jnp.int32)
    east = jnp.zeros((STRIP, LANES), jnp.int32)
    for part in range(4):
        here = ground[part * STRIP : (part + 1) * STRIP]
        base = part * 32
        in_height = (wide >= base) & (wide < base + 16)
        in_block = (wide >= base + 16) & (wide < base + 32)
        west = jnp.where(in_height, pltpu.roll(here, base % LANES, 1), west)
        west = jnp.where(in_block, pltpu.roll(here, (base + 16 - 64) % LANES, 1), west)
        east = jnp.where(in_height, pltpu.roll(here, (base - 48) % LANES, 1), east)
        east = jnp.where(in_block, pltpu.roll(here, (base + 16 - 112) % LANES, 1), east)
    strips[0] = west
    strips[1] = east

    pl.semaphore_wait(barrier, len(met))

    top, bottom = ground.at[0:STRIP], ground.at[TILE - STRIP : TILE]
    ground_source = {-1: top, 1: bottom}
    ground_copies = []
    for at, (dr, dc) in enumerate(AROUND):
        if dr:
            source = ground_source[dr]
        else:
            source = strips.at[0 if dc < 0 else 1]
        slot = AROUND.index((-dr, -dc))
        ground_copies.append(
            send(source, ground_in.at[slot], ground_send.at[at], ground_recv.at[slot], around[at])
        )

    loads[2].wait()
    own = jnp.broadcast_to(portal[0, 0:1, :], (8, PORTALS))
    portal_cells = jnp.concatenate([own] * BLOCKS, axis=1)
    loads[3].wait()
    loads[4].wait()
    loads[5].wait()
    low = lane < 2 * PORTALS
    even = lane_block % 2 == 0
    swapped_blocks = lane_class + (lane_block + 1 - 2 * (lane_block % 2)) * PORTALS

    def transposed(a):
        t = [None] * 4
        for at in range(2):
            turned = pltpu.roll(jnp.where(low, a[at + 2], a[at]), 2 * PORTALS, 1)
            t[at], t[at + 2] = jnp.where(low, a[at], turned), jnp.where(low, turned, a[at + 2])
        out = [None] * 4
        for at in (0, 2):
            turned = lane_take(jnp.where(even, t[at + 1], t[at]), swapped_blocks)
            out[at], out[at + 1] = jnp.where(even, t[at], turned), jnp.where(even, turned, t[at + 1])
        return out

    def estimates(part, group):
        values = estimate[part * 16 : (part + 1) * 16, group * LANES : (group + 1) * LANES]
        values = values.astype(jnp.float32)
        return values[0:8], values[8:16]

    def prepare(part):
        for first in range(4):
            halves = [estimates(part, first + 4 * at) for at in range(4)]
            for half in range(2):
                row = part * 16 + half * 8
                cell = (row + sublane) * TILE + lane_block * OWN
                for at, values in enumerate(transposed([pieces[half] for pieces in halves])):
                    group = 4 * first + at
                    field[group, HALO + row : HALO + row + 8, :] = jnp.where(
                        portal_cells == cell + group, 0.0, values
                    )

    def edges(part):
        columns = (0, 1, OWN - 2, OWN - 1)
        pieces = [estimates(part, group) for group in columns]
        for half in range(2):
            row = part * 16 + half * 8
            cell = (row + sublane) * TILE + lane_block
            w0, w1, e0, e1 = (
                jnp.where(portal_cells == cell + group * BLOCKS, 0.0, piece[half])
                for group, piece in zip(columns, pieces)
            )
            side_out[0, 0, row : row + 8, :] = jnp.where(even, w0, pltpu.roll(w1, 32, 1))
            side_out[0, 1, row : row + 8, :] = jnp.where(even, pltpu.roll(w0, 96, 1), w1)
            side_out[1, 0, row : row + 8, :] = jnp.where(even, pltpu.roll(e0, 64, 1), pltpu.roll(e1, 96, 1))
            side_out[1, 1, row : row + 8, :] = jnp.where(even, pltpu.roll(e0, 32, 1), pltpu.roll(e1, 64, 1))

    prepare(0)
    prepare(3)
    for part in range(4):
        edges(part)

    field_copies = []
    for at, (dr, dc) in enumerate(AROUND):
        row_from, row_to, row_len = {
            -1: (0, HALO + TILE, HALO), 0: (0, HALO, TILE), 1: (TILE - HALO, 0, HALO)
        }[dr]
        if dc:
            side = 0 if dc < 0 else 1
            source = side_out.at[side, :, pl.ds(row_from, row_len), :]
            target = side_in.at[side, :, pl.ds(row_to, row_len), :]
        else:
            source = field.at[:, pl.ds(HALO + row_from, row_len), :]
            target = field.at[:, pl.ds(row_to, row_len), :]
        slot = AROUND.index((-dr, -dc))
        field_copies.append(send(source, target, field_send.at[at], field_recv.at[slot], around[at]))

    prepare(1)
    prepare(2)

    for copy in ground_copies:
        copy.wait_recv()
    slots = {step: at for at, step in enumerate(AROUND)}

    def lay(row, west_height, middle, east_height, west_block, east_block):
        height = jnp.where(wide < 16, west_height, jnp.where(wide < 80, pltpu.roll(middle, 16, 1), east_height))
        block = jnp.where(wide < 16, west_block, jnp.where(wide < 80, pltpu.roll(middle, 80, 1), east_block))
        high[0, row : row + STRIP, :] = height.astype(jnp.float32)
        high[1, row : row + STRIP, :] = block.astype(jnp.float32)

    for dr, row in ((-1, 0), (1, STRIP + TILE)):
        west_in, middle, east_in = (ground_in[slots[(dr, dc)]] for dc in (-1, 0, 1))
        lay(
            row, pltpu.roll(west_in, 80, 1), middle, pltpu.roll(east_in, 80, 1),
            pltpu.roll(west_in, 16, 1), pltpu.roll(east_in, 16, 1),
        )
    west_in, east_in = ground_in[slots[(0, -1)]], ground_in[slots[(0, 1)]]
    for part in range(4):
        base = part * 32
        lay(
            STRIP + part * STRIP,
            pltpu.roll(west_in, (-base) % LANES, 1),
            ground[part * STRIP : (part + 1) * STRIP],
            pltpu.roll(east_in, (80 - base) % LANES, 1),
            pltpu.roll(west_in, (-base - 16) % LANES, 1),
            pltpu.roll(east_in, (64 - base) % LANES, 1),
        )

    @pl.when(row_index == 0)
    def _():
        high[0, STRIP - 1 : STRIP, :] = high[0, STRIP : STRIP + 1, :]

    @pl.when(row_index == row_count - 1)
    def _():
        high[0, STRIP + TILE : STRIP + TILE + 1, :] = high[0, STRIP + TILE - 1 : STRIP + TILE, :]

    shift = STRIP - HALO
    near = high[0, shift : shift + EXT, :]
    up = high[0, shift - 1 : shift - 1 + EXT, :]
    down = high[0, shift + 1 : shift + 1 + EXT, :]
    col = lax.broadcasted_iota(jnp.int32, (EXT, LANES), 1) - STRIP
    row = lax.broadcasted_iota(jnp.int32, (EXT, LANES), 0) - HALO
    grid_col = col_index * TILE + col
    grid_row = row_index * TILE + row
    before = jnp.where(grid_col == 0, near, pltpu.roll(near, 1, 1))
    after = jnp.where(grid_col == col_count * TILE - 1, near, pltpu.roll(near, LANES - 1, 1))
    grad_x = (after - before) * 0.01
    grad_y = (down - up) * 0.01
    grad_sq = grad_x * grad_x + grad_y * grad_y
    step_cost = (
        1.0 + 2.0 * grad_sq + 0.5 * grad_y / jnp.sqrt(1.0 + grad_sq)
        + 30.0 * high[1, shift : shift + EXT, :]
    )
    inside = (
        (grid_row >= 0) & (grid_row < row_count * TILE)
        & (grid_col >= 0) & (grid_col < col_count * TILE)
    )
    cost_rows[...] = jnp.where(inside, step_cost, FAR)
    first_column = STRIP + lane_block * OWN
    halo_shift = jnp.where(low, TILE + 4 * lane_block, 4 * lane_block - 16) - lane_block * OWN
    for at in range(STEP):
        values = cost_rows[pl.ds(at, 8, stride=STEP), :]
        for group in range(GROUPS):
            cost[group, at] = lane_take(values, first_column + (group if group < OWN else group - OWN + halo_shift))

    loads[6].wait()
    cells = [portal_smem[0, 0, at] for at in range(PORTALS)]
    for at, cell in enumerate(cells):
        shifts[at : at + 1, :] = jnp.full((1, LANES), ((cell >> 4) & (BLOCKS - 1)) * PORTALS, jnp.int32)

    for copy in field_copies:
        copy.wait_recv()

    def half_cost(group, at):
        here = cost[group, at]
        return jnp.where(here >= FAR, FAR, 0.5 * here)

    def start(group, at, distance):
        dist[group, at] = jnp.minimum(distance + half_cost(group, at), FAR)

    for at in range(STEP):
        for group in range(OWN):
            start(group, at, field[group, pl.ds(at, 8, stride=STEP), :])
        for piece in range(2):
            from_east = side_in[0, piece, pl.ds(at, 8, stride=STEP), :]
            from_west = side_in[1, piece, pl.ds(at, 8, stride=STEP), :]
            start(OWN + piece, at, jnp.where(low, from_east, from_west))
            start(OWN + piece + 2, at, pltpu.roll(jnp.where(low, from_west, from_east), 64, 1))

    first_block, last_block = lane_block == 0, lane_block == BLOCKS - 1

    def sweep(_, carry):
        def pairs_of(here, east_of):
            below = east_of[1:] + [pltpu.roll(east_of[0], 7, 0)]
            return [jnp.minimum(a, b) for a, b in zip(here, below)]

        def column(group):
            return [dist[group, at] for at in range(STEP)]

        own_first, halo_first = column(0), column(OWN)
        own_pairs = pairs_of(
            column(OWN - 1),
            [pltpu.roll(jnp.where(first_block, a, b), LANES - PORTALS, 1) for a, b in zip(halo_first, own_first)],
        )
        halo_pairs = pairs_of(
            column(GROUPS - 1),
            [pltpu.roll(jnp.where(first_block, a, b), LANES - PORTALS, 1) for a, b in zip(own_first, halo_first)],
        )
        own_west = [pltpu.roll(jnp.where(last_block, a, b), PORTALS, 1) for a, b in zip(halo_pairs, own_pairs)]
        halo_west = [pltpu.roll(jnp.where(last_block, a, b), PORTALS, 1) for a, b in zip(own_pairs, halo_pairs)]
        for begin, end, west_of, end_pairs in ((0, OWN, own_west, own_pairs), (OWN, GROUPS, halo_west, halo_pairs)):
            now = own_first if begin == 0 else column(begin)
            for group in range(begin, end):
                if group < end - 1:
                    later = column(group + 1)
                    pairs = pairs_of(now, later)
                else:
                    pairs = end_pairs
                north = [pltpu.roll(pairs[STEP - 1], 1, 0)] + pairs[:-1]
                for at in range(STEP):
                    nearest = cost[group, at] + jnp.minimum(north[at], west_of[at])
                    dist[group, at] = jnp.minimum(now[at], nearest)
                west_of, now = pairs, later
        return carry

    lax.fori_loop(0, SWEEPS, sweep, 0)

    for copy in field_copies:
        copy.wait_send()
    for group in range(OWN):
        for at in range(STEP):
            field[group, pl.ds(at, 8, stride=STEP), :] = dist[group, at] - 0.5 * cost[group, at]

    for at, cell in enumerate(cells):
        rows[at : at + 1, :] = field[cell & (OWN - 1), pl.ds(HALO + (cell >> 6), 1), :]
    first = jnp.zeros((8, LANES), jnp.float32)
    for part in range(4):
        index = shifts[part * 8 : part * 8 + 8, :] + lane_class
        first = jnp.where(lane_block == part, lane_take(rows[part * 8 : part * 8 + 8, :], index), first)
    table[0] = first

    table_copies = []

    def exchange(level):
        copies = [
            send(
                table.at[level], table_in.at[3 * level + at],
                table_send.at[3 * level + at], table_recv.at[3 * level + at], device,
            )
            for at, device in reversed(tuple(enumerate(partners[level])))
        ]
        table_copies.extend(reversed(copies))

    def left_of(values):
        return [lane_take(values, lane_block * PORTALS + at) for at in range(PORTALS)]

    def right_of(values, slot):
        for part in range(4):
            right_rows[slot, part * 8 : part * 8 + 8, :] = lane_take(values, lane_class + part * PORTALS)
        return [
            jnp.broadcast_to(right_rows[slot, at : at + 1, :], (8, LANES)) for at in range(PORTALS)
        ]

    def minplus(left, right):
        sums = [a + b for a, b in zip(left, right)]
        while len(sums) > 1:
            sums = [jnp.minimum(a, b) for a, b in zip(sums[::2], sums[1::2])]
        return sums[0]

    def pair(near_table, near_left, near_right, far_right):
        through = minplus(near_left, far_right)
        return jnp.minimum(near_table, minplus(left_of(through), near_right))

    def relax_out(part):
        for first_at in range(4):
            for_rows = [
                transposed(
                    [
                        field[4 * first_at + at, HALO + part * 16 + half * 8 : HALO + part * 16 + half * 8 + 8, :]
                        for at in range(4)
                    ]
                )
                for half in range(2)
            ]
            for at in range(4):
                group = first_at + 4 * at
                values = jnp.concatenate([for_rows[0][at], for_rows[1][at]], axis=0)
                relaxed[part * 16 : part * 16 + 16, group * LANES : (group + 1) * LANES] = values.astype(jnp.bfloat16)

    now = first
    for level in range(2):
        exchange(level)
        now_left, now_right = left_of(now), right_of(now, 6 * level)
        relax_out(2 * level)
        relax_out(2 * level + 1)
        def arrived(at):
            table_copies[3 * level + at].wait_recv()
            return table_in[3 * level + at]

        by_col = arrived(1)
        col_left, col_right = left_of(by_col), right_of(by_col, 6 * level + 2)
        by_row = arrived(0)
        here = pair(now, now_left, now_right, right_of(by_row, 6 * level + 1))
        here_left, here_right = left_of(here), right_of(here, 6 * level + 4)
        there = pair(by_col, col_left, col_right, right_of(arrived(2), 6 * level + 3))
        now = pair(here, here_left, here_right, right_of(there, 6 * level + 5))
        if level == 0:
            table[1] = now
    now = now * 0.0625
    for part in range(4):
        merged[0, 0, part * 8 : part * 8 + 8, :] = now[:, part * PORTALS : (part + 1) * PORTALS]

    for copy in ground_copies + table_copies:
        copy.wait_send()


def hand_out(relaxed_in, merged_in, relaxed, merged, sem):
    copies = [
        pltpu.make_async_copy(relaxed_in, relaxed, sem.at[0]),
        pltpu.make_async_copy(merged_in, merged, sem.at[1]),
    ]
    for copy in copies:
        copy.start()
    for copy in copies:
        copy.wait()


def body(heights, blocked, estimate, portal_index):
    in_hbm = pl.BlockSpec(memory_space=pltpu.HBM)
    in_vmem = pl.BlockSpec(memory_space=pltpu.VMEM)
    outs = (
        jax.ShapeDtypeStruct(estimate.shape, jnp.bfloat16),
        jax.ShapeDtypeStruct((1, 1, PORTALS, PORTALS), jnp.float32),
    )
    results = pl.pallas_call(
        kernel,
        out_shape=outs,
        in_specs=[in_hbm] * 4,
        out_specs=(in_vmem, in_vmem),
        scratch_shapes=[
            pltpu.VMEM((TILE, TILE), jnp.int32),
            pltpu.VMEM((TILE, TILE), jnp.int32),
            pltpu.VMEM((TILE, TILE * PORTALS), jnp.bfloat16),
            pltpu.VMEM((1, 1, PORTALS), jnp.int32),
            pltpu.SMEM((1, 1, PORTALS), jnp.int32),
            pltpu.VMEM((TILE, LANES), jnp.int32),
            pltpu.VMEM((2, STRIP, LANES), jnp.int32),
            pltpu.VMEM((8, STRIP, LANES), jnp.int32),
            pltpu.VMEM((2, TILE + 2 * STRIP, LANES), jnp.float32),
            pltpu.VMEM((EXT, LANES), jnp.float32),
            pltpu.VMEM((OWN, EXT, LANES), jnp.float32),
            pltpu.VMEM((2, 2, TILE, LANES), jnp.float32),
            pltpu.VMEM((2, 2, EXT, LANES), jnp.float32),
            pltpu.VMEM((GROUPS, STEP, 8, LANES), jnp.float32),
            pltpu.VMEM((GROUPS, STEP, 8, LANES), jnp.float32),
            pltpu.VMEM((PORTALS, LANES), jnp.float32),
            pltpu.VMEM((PORTALS, LANES), jnp.int32),
            pltpu.VMEM((2, 8, LANES), jnp.float32),
            pltpu.VMEM((6, 8, LANES), jnp.float32),
            pltpu.VMEM((12, PORTALS, LANES), jnp.float32),
            pltpu.SemaphoreType.DMA((7,)),
            pltpu.SemaphoreType.DMA((8,)),
            pltpu.SemaphoreType.DMA((8,)),
            pltpu.SemaphoreType.DMA((8,)),
            pltpu.SemaphoreType.DMA((8,)),
            pltpu.SemaphoreType.DMA((6,)),
            pltpu.SemaphoreType.DMA((6,)),
        ],
        compiler_params=pltpu.CompilerParams(
            collective_id=0, has_side_effects=True, vmem_limit_bytes=16 * 2**20
        ),
    )(*(pltpu.with_memory_space_constraint(x, pltpu.HBM) for x in (heights, blocked, estimate, portal_index)))
    return pl.pallas_call(
        hand_out,
        out_shape=tuple(pltpu.HBM(x.shape, x.dtype) for x in outs),
        in_specs=[in_vmem] * 2,
        out_specs=[in_hbm] * 2,
        scratch_shapes=[pltpu.SemaphoreType.DMA((2,))],
        compiler_params=pltpu.CompilerParams(vmem_limit_bytes=2**20),
    )(*(pltpu.with_memory_space_constraint(x, pltpu.VMEM) for x in results))


def solution(mesh):
    placed = (P("row", "col"), P("row", "col"), P("row", "col"), P("row", "col", None))
    return jax.shard_map(
        body,
        mesh=mesh,
        in_specs=placed,
        out_specs=(P("row", "col"), P("row", "col", None, None)),
        check_vma=False,
    )
```

```python
import functools

import jax
import jax.numpy as jnp
from jax import lax
from jax.experimental import pallas as pl
from jax.experimental.pallas import tpu as pltpu
from jax.sharding import PartitionSpec as P

TILE = 64
PORTALS = 32
SWEEPS = 8
HALO = 8
EXT = TILE + 2 * HALO
LANES = 128
BLOCKS = LANES // PORTALS
OWN = TILE // BLOCKS
GROUPS = EXT // BLOCKS
STEP = EXT // 8
STRIP = 16
FAR = 1000000.0


AROUND = ((-1, -1), (-1, 1), (1, -1), (1, 1), (-1, 0), (1, 0), (0, -1), (0, 1))


def lane_take(values, index):
    return jnp.take_along_axis(values, index, axis=1, mode="promise_in_bounds")


def kernel(
    heights_hbm, blocked_hbm, estimate_hbm, portal_hbm,
    relaxed, merged,
    heights, blocked, estimate, portal, portal_smem,
    ground, strips, ground_in, high, cost_rows,
    field, side_out, side_in, cost, dist, rows, shifts, table, table_in, right_rows,
    load_sem, ground_send, ground_recv, field_send, field_recv, table_send, table_recv,
):
    row_index, col_index = lax.axis_index("row"), lax.axis_index("col")
    row_count, col_count = lax.axis_size("row"), lax.axis_size("col")
    around = [
        (lax.rem(row_index + dr + row_count, row_count), lax.rem(col_index + dc + col_count, col_count))
        for dr, dc in AROUND
    ]

    def other(index, bit):
        return index + bit - 2 * bit * lax.rem(index // bit, 2)

    def partner(index, step):
        for bit in (1, 2):
            if step & bit:
                index = other(index, bit)
        return index

    steps = [(a, b) for a in range(4) for b in range(4) if a or b]
    blocks = {(a, b): 2 * (a // 2) + b // 2 for a, b in steps}
    steps.sort(key=lambda step: (0, 3, 2, 1).index(blocks[step]))
    partners = {(a, b): (partner(row_index, a), partner(col_index, b)) for a, b in steps}

    loads = [
        pltpu.make_async_copy(source, target, load_sem.at[at])
        for at, (source, target) in enumerate(
            (
                (heights_hbm, heights),
                (blocked_hbm, blocked),
                (portal_hbm, portal),
                (estimate_hbm.at[0:16], estimate.at[0:16]),
                (estimate_hbm.at[48:64], estimate.at[48:64]),
                (estimate_hbm.at[16:48], estimate.at[16:48]),
                (portal_hbm, portal_smem),
            )
        )
    ]
    for load in loads:
        load.start()

    barrier = pltpu.get_barrier_semaphore()
    met = around + [partners[step] for step in steps if max(step) > 1]
    for device in met:
        pl.semaphore_signal(barrier, inc=1, device_id=device, device_id_type=pl.DeviceIdType.MESH)

    def send(source, target, send_sem, recv_sem, device):
        copy = pltpu.make_async_remote_copy(
            src_ref=source, dst_ref=target, send_sem=send_sem, recv_sem=recv_sem,
            device_id=device, device_id_type=pl.DeviceIdType.MESH,
        )
        copy.start()
        return copy

    lane = lax.broadcasted_iota(jnp.int32, (8, LANES), 1)
    sublane = lax.broadcasted_iota(jnp.int32, (8, LANES), 0)
    lane_block = lane // PORTALS
    lane_class = lane % PORTALS

    loads[0].wait()
    loads[1].wait()
    ground[:, 0:TILE] = heights[...]
    ground[:, TILE : 2 * TILE] = blocked[...]
    wide = lax.broadcasted_iota(jnp.int32, (STRIP, LANES), 1)
    west = jnp.zeros((STRIP, LANES), jnp.int32)
    east = jnp.zeros((STRIP, LANES), jnp.int32)
    for part in range(4):
        here = ground[part * STRIP : (part + 1) * STRIP]
        base = part * 32
        in_height = (wide >= base) & (wide < base + 16)
        in_block = (wide >= base + 16) & (wide < base + 32)
        west = jnp.where(in_height, pltpu.roll(here, base % LANES, 1), west)
        west = jnp.where(in_block, pltpu.roll(here, (base + 16 - 64) % LANES, 1), west)
        east = jnp.where(in_height, pltpu.roll(here, (base - 48) % LANES, 1), east)
        east = jnp.where(in_block, pltpu.roll(here, (base + 16 - 112) % LANES, 1), east)
    strips[0] = west
    strips[1] = east

    pl.semaphore_wait(barrier, len(met))

    top, bottom = ground.at[0:STRIP], ground.at[TILE - STRIP : TILE]
    ground_source = {-1: top, 1: bottom}
    ground_copies = []
    for at, (dr, dc) in enumerate(AROUND):
        if dr:
            source = ground_source[dr]
        else:
            source = strips.at[0 if dc < 0 else 1]
        slot = AROUND.index((-dr, -dc))
        ground_copies.append(
            send(source, ground_in.at[slot], ground_send.at[at], ground_recv.at[slot], around[at])
        )

    loads[2].wait()
    own = jnp.broadcast_to(portal[0, 0:1, :], (8, PORTALS))
    portal_cells = jnp.concatenate([own] * BLOCKS, axis=1)
    loads[3].wait()
    loads[4].wait()
    loads[5].wait()
    low = lane < 2 * PORTALS
    even = lane_block % 2 == 0
    swapped_blocks = lane_class + (lane_block + 1 - 2 * (lane_block % 2)) * PORTALS

    def transposed(a):
        t = [None] * 4
        for at in range(2):
            turned = pltpu.roll(jnp.where(low, a[at + 2], a[at]), 2 * PORTALS, 1)
            t[at], t[at + 2] = jnp.where(low, a[at], turned), jnp.where(low, turned, a[at + 2])
        out = [None] * 4
        for at in (0, 2):
            turned = lane_take(jnp.where(even, t[at + 1], t[at]), swapped_blocks)
            out[at], out[at + 1] = jnp.where(even, t[at], turned), jnp.where(even, turned, t[at + 1])
        return out

    def estimates(part, group):
        values = estimate[part * 16 : (part + 1) * 16, group * LANES : (group + 1) * LANES]
        values = values.astype(jnp.float32)
        return values[0:8], values[8:16]

    def prepare(part):
        for first in range(4):
            halves = [estimates(part, first + 4 * at) for at in range(4)]
            for half in range(2):
                row = part * 16 + half * 8
                cell = (row + sublane) * TILE + lane_block * OWN
                for at, values in enumerate(transposed([pieces[half] for pieces in halves])):
                    group = 4 * first + at
                    field[group, HALO + row : HALO + row + 8, :] = jnp.where(
                        portal_cells == cell + group, 0.0, values
                    )

    def edges(part):
        columns = (0, 1, OWN - 2, OWN - 1)
        pieces = [estimates(part, group) for group in columns]
        for half in range(2):
            row = part * 16 + half * 8
            cell = (row + sublane) * TILE + lane_block
            w0, w1, e0, e1 = (
                jnp.where(portal_cells == cell + group * BLOCKS, 0.0, piece[half])
                for group, piece in zip(columns, pieces)
            )
            side_out[0, 0, row : row + 8, :] = jnp.where(even, w0, pltpu.roll(w1, 32, 1))
            side_out[0, 1, row : row + 8, :] = jnp.where(even, pltpu.roll(w0, 96, 1), w1)
            side_out[1, 0, row : row + 8, :] = jnp.where(even, pltpu.roll(e0, 64, 1), pltpu.roll(e1, 96, 1))
            side_out[1, 1, row : row + 8, :] = jnp.where(even, pltpu.roll(e0, 32, 1), pltpu.roll(e1, 64, 1))

    prepare(0)
    prepare(3)
    for part in range(4):
        edges(part)

    field_copies = []
    for at, (dr, dc) in enumerate(AROUND):
        row_from, row_to, row_len = {
            -1: (0, HALO + TILE, HALO), 0: (0, HALO, TILE), 1: (TILE - HALO, 0, HALO)
        }[dr]
        if dc:
            side = 0 if dc < 0 else 1
            source = side_out.at[side, :, pl.ds(row_from, row_len), :]
            target = side_in.at[side, :, pl.ds(row_to, row_len), :]
        else:
            source = field.at[:, pl.ds(HALO + row_from, row_len), :]
            target = field.at[:, pl.ds(row_to, row_len), :]
        slot = AROUND.index((-dr, -dc))
        field_copies.append(send(source, target, field_send.at[at], field_recv.at[slot], around[at]))

    prepare(1)
    prepare(2)

    for copy in ground_copies:
        copy.wait_recv()
    slots = {step: at for at, step in enumerate(AROUND)}

    def lay(row, west_height, middle, east_height, west_block, east_block):
        height = jnp.where(wide < 16, west_height, jnp.where(wide < 80, pltpu.roll(middle, 16, 1), east_height))
        block = jnp.where(wide < 16, west_block, jnp.where(wide < 80, pltpu.roll(middle, 80, 1), east_block))
        high[0, row : row + STRIP, :] = height.astype(jnp.float32)
        high[1, row : row + STRIP, :] = block.astype(jnp.float32)

    for dr, row in ((-1, 0), (1, STRIP + TILE)):
        west_in, middle, east_in = (ground_in[slots[(dr, dc)]] for dc in (-1, 0, 1))
        lay(
            row, pltpu.roll(west_in, 80, 1), middle, pltpu.roll(east_in, 80, 1),
            pltpu.roll(west_in, 16, 1), pltpu.roll(east_in, 16, 1),
        )
    west_in, east_in = ground_in[slots[(0, -1)]], ground_in[slots[(0, 1)]]
    for part in range(4):
        base = part * 32
        lay(
            STRIP + part * STRIP,
            pltpu.roll(west_in, (-base) % LANES, 1),
            ground[part * STRIP : (part + 1) * STRIP],
            pltpu.roll(east_in, (80 - base) % LANES, 1),
            pltpu.roll(west_in, (-base - 16) % LANES, 1),
            pltpu.roll(east_in, (64 - base) % LANES, 1),
        )

    @pl.when(row_index == 0)
    def _():
        high[0, STRIP - 1 : STRIP, :] = high[0, STRIP : STRIP + 1, :]

    @pl.when(row_index == row_count - 1)
    def _():
        high[0, STRIP + TILE : STRIP + TILE + 1, :] = high[0, STRIP + TILE - 1 : STRIP + TILE, :]

    shift = STRIP - HALO
    near = high[0, shift : shift + EXT, :]
    up = high[0, shift - 1 : shift - 1 + EXT, :]
    down = high[0, shift + 1 : shift + 1 + EXT, :]
    col = lax.broadcasted_iota(jnp.int32, (EXT, LANES), 1) - STRIP
    row = lax.broadcasted_iota(jnp.int32, (EXT, LANES), 0) - HALO
    grid_col = col_index * TILE + col
    grid_row = row_index * TILE + row
    before = jnp.where(grid_col == 0, near, pltpu.roll(near, 1, 1))
    after = jnp.where(grid_col == col_count * TILE - 1, near, pltpu.roll(near, LANES - 1, 1))
    grad_x = (after - before) * 0.01
    grad_y = (down - up) * 0.01
    grad_sq = grad_x * grad_x + grad_y * grad_y
    step_cost = (
        1.0 + 2.0 * grad_sq + 0.5 * grad_y / jnp.sqrt(1.0 + grad_sq)
        + 30.0 * high[1, shift : shift + EXT, :]
    )
    inside = (
        (grid_row >= 0) & (grid_row < row_count * TILE)
        & (grid_col >= 0) & (grid_col < col_count * TILE)
    )
    cost_rows[...] = jnp.where(inside, step_cost, FAR)
    first_column = STRIP + lane_block * OWN
    halo_shift = jnp.where(low, TILE + 4 * lane_block, 4 * lane_block - 16) - lane_block * OWN
    for at in range(STEP):
        values = cost_rows[pl.ds(at, 8, stride=STEP), :]
        for group in range(GROUPS):
            here = lane_take(values, first_column + (group if group < OWN else group - OWN + halo_shift))
            cost[group, at] = here
            dist[group, at] = jnp.where(here >= FAR, FAR, 0.5 * here)

    loads[6].wait()
    cells = [portal_smem[0, 0, at] for at in range(PORTALS)]
    for at, cell in enumerate(cells):
        shifts[at : at + 1, :] = jnp.full((1, LANES), ((cell >> 4) & (BLOCKS - 1)) * PORTALS, jnp.int32)

    for copy in field_copies:
        copy.wait_recv()

    def start(group, at, distance):
        dist[group, at] = jnp.minimum(distance + dist[group, at], FAR)

    for at in range(STEP):
        for group in range(OWN):
            start(group, at, field[group, pl.ds(at, 8, stride=STEP), :])
        for piece in range(2):
            from_east = side_in[0, piece, pl.ds(at, 8, stride=STEP), :]
            from_west = side_in[1, piece, pl.ds(at, 8, stride=STEP), :]
            start(OWN + piece, at, jnp.where(low, from_east, from_west))
            start(OWN + piece + 2, at, pltpu.roll(jnp.where(low, from_west, from_east), 64, 1))

    first_block, last_block = lane_block == 0, lane_block == BLOCKS - 1

    def sweep(_, carry):
        def pairs_of(here, east_of):
            below = east_of[1:] + [pltpu.roll(east_of[0], 7, 0)]
            return [jnp.minimum(a, b) for a, b in zip(here, below)]

        def column(group):
            return [dist[group, at] for at in range(STEP)]

        own_first, halo_first = column(0), column(OWN)
        own_pairs = pairs_of(
            column(OWN - 1),
            [pltpu.roll(jnp.where(first_block, a, b), LANES - PORTALS, 1) for a, b in zip(halo_first, own_first)],
        )
        halo_pairs = pairs_of(
            column(GROUPS - 1),
            [pltpu.roll(jnp.where(first_block, a, b), LANES - PORTALS, 1) for a, b in zip(own_first, halo_first)],
        )
        own_west = [pltpu.roll(jnp.where(last_block, a, b), PORTALS, 1) for a, b in zip(halo_pairs, own_pairs)]
        halo_west = [pltpu.roll(jnp.where(last_block, a, b), PORTALS, 1) for a, b in zip(own_pairs, halo_pairs)]
        for begin, end, west_of, end_pairs in ((0, OWN, own_west, own_pairs), (OWN, GROUPS, halo_west, halo_pairs)):
            now = own_first if begin == 0 else column(begin)
            for group in range(begin, end):
                if group < end - 1:
                    later = column(group + 1)
                    pairs = pairs_of(now, later)
                else:
                    pairs = end_pairs
                north = [pltpu.roll(pairs[STEP - 1], 1, 0)] + pairs[:-1]
                for at in range(STEP):
                    nearest = cost[group, at] + jnp.minimum(north[at], west_of[at])
                    dist[group, at] = jnp.minimum(now[at], nearest)
                west_of, now = pairs, later
        return carry

    lax.fori_loop(0, SWEEPS, sweep, 0)

    for copy in field_copies:
        copy.wait_send()
    for group in range(OWN):
        for at in range(STEP):
            field[group, pl.ds(at, 8, stride=STEP), :] = dist[group, at] - 0.5 * cost[group, at]

    for at, cell in enumerate(cells):
        rows[at : at + 1, :] = field[cell & (OWN - 1), pl.ds(HALO + (cell >> 6), 1), :]
    first = jnp.zeros((8, LANES), jnp.float32)
    for part in range(4):
        index = shifts[part * 8 : part * 8 + 8, :] + lane_class
        first = jnp.where(lane_block == part, lane_take(rows[part * 8 : part * 8 + 8, :], index), first)
    table[...] = first

    table_copies = {
        (a, b): send(
            table, table_in.at[4 * a + b], table_send.at[4 * a + b], table_recv.at[4 * a + b], partners[a, b]
        )
        for a, b in steps
    }

    def left_of(values):
        return [lane_take(values, lane_block * PORTALS + at) for at in range(PORTALS)]

    slots_used = []

    def right_of(values):
        slot = len(slots_used)
        slots_used.append(slot)
        for part in range(4):
            right_rows[slot, part * 8 : part * 8 + 8, :] = lane_take(values, lane_class + part * PORTALS)
        return [
            jnp.broadcast_to(right_rows[slot, at : at + 1, :], (8, LANES)) for at in range(PORTALS)
        ]

    def minplus(left, right):
        sums = [a + b for a, b in zip(left, right)]
        while len(sums) > 1:
            sums = [jnp.minimum(a, b) for a, b in zip(sums[::2], sums[1::2])]
        return sums[0]

    def sides(values):
        return values, left_of(values), right_of(values)

    def pair(near, far_table):
        values, near_left, near_right = near
        through = minplus(near_left, right_of(far_table))
        return jnp.minimum(values, minplus(left_of(through), near_right))

    def relax_out(part):
        for first_at in range(4):
            for_rows = [
                transposed(
                    [
                        field[4 * first_at + at, HALO + part * 16 + half * 8 : HALO + part * 16 + half * 8 + 8, :]
                        for at in range(4)
                    ]
                )
                for half in range(2)
            ]
            for at in range(4):
                group = first_at + 4 * at
                values = jnp.concatenate([for_rows[0][at], for_rows[1][at]], axis=0)
                relaxed[part * 16 : part * 16 + 16, group * LANES : (group + 1) * LANES] = values.astype(jnp.bfloat16)

    def arrived(a, b):
        table_copies[a, b].wait_recv()
        return table_in[4 * a + b]

    def block(a, b):
        near, beside = sides(arrived(a, b)), sides(arrived(a, b + 1))
        below, across = arrived(a + 1, b), arrived(a + 1, b + 1)
        return pair(sides(pair(near, below)), pair(beside, across))

    near = sides(first)
    for part in range(4):
        relax_out(part)
    beside = sides(arrived(0, 1))
    beside = pair(beside, arrived(1, 1))
    second = sides(pair(sides(pair(near, arrived(1, 0))), beside))
    third = sides(pair(second, block(2, 0)))
    beside = sides(block(0, 2))
    now = pair(third, pair(beside, block(2, 2)))
    now = now * 0.0625
    for part in range(4):
        merged[0, 0, part * 8 : part * 8 + 8, :] = now[:, part * PORTALS : (part + 1) * PORTALS]

    for copy in ground_copies + list(table_copies.values()):
        copy.wait_send()


def hand_out(relaxed_in, merged_in, relaxed, merged, sem):
    copies = [
        pltpu.make_async_copy(relaxed_in, relaxed, sem.at[0]),
        pltpu.make_async_copy(merged_in, merged, sem.at[1]),
    ]
    for copy in copies:
        copy.start()
    for copy in copies:
        copy.wait()


def body(heights, blocked, estimate, portal_index):
    in_hbm = pl.BlockSpec(memory_space=pltpu.HBM)
    in_vmem = pl.BlockSpec(memory_space=pltpu.VMEM)
    outs = (
        jax.ShapeDtypeStruct(estimate.shape, jnp.bfloat16),
        jax.ShapeDtypeStruct((1, 1, PORTALS, PORTALS), jnp.float32),
    )
    results = pl.pallas_call(
        kernel,
        out_shape=outs,
        in_specs=[in_hbm] * 4,
        out_specs=(in_vmem, in_vmem),
        scratch_shapes=[
            pltpu.VMEM((TILE, TILE), jnp.int32),
            pltpu.VMEM((TILE, TILE), jnp.int32),
            pltpu.VMEM((TILE, TILE * PORTALS), jnp.bfloat16),
            pltpu.VMEM((1, 1, PORTALS), jnp.int32),
            pltpu.SMEM((1, 1, PORTALS), jnp.int32),
            pltpu.VMEM((TILE, LANES), jnp.int32),
            pltpu.VMEM((2, STRIP, LANES), jnp.int32),
            pltpu.VMEM((8, STRIP, LANES), jnp.int32),
            pltpu.VMEM((2, TILE + 2 * STRIP, LANES), jnp.float32),
            pltpu.VMEM((EXT, LANES), jnp.float32),
            pltpu.VMEM((OWN, EXT, LANES), jnp.float32),
            pltpu.VMEM((2, 2, TILE, LANES), jnp.float32),
            pltpu.VMEM((2, 2, EXT, LANES), jnp.float32),
            pltpu.VMEM((GROUPS, STEP, 8, LANES), jnp.float32),
            pltpu.VMEM((GROUPS, STEP, 8, LANES), jnp.float32),
            pltpu.VMEM((PORTALS, LANES), jnp.float32),
            pltpu.VMEM((PORTALS, LANES), jnp.int32),
            pltpu.VMEM((8, LANES), jnp.float32),
            pltpu.VMEM((16, 8, LANES), jnp.float32),
            pltpu.VMEM((32, PORTALS, LANES), jnp.float32),
            pltpu.SemaphoreType.DMA((7,)),
            pltpu.SemaphoreType.DMA((8,)),
            pltpu.SemaphoreType.DMA((8,)),
            pltpu.SemaphoreType.DMA((8,)),
            pltpu.SemaphoreType.DMA((8,)),
            pltpu.SemaphoreType.DMA((16,)),
            pltpu.SemaphoreType.DMA((16,)),
        ],
        compiler_params=pltpu.CompilerParams(
            collective_id=0, has_side_effects=True, vmem_limit_bytes=16 * 2**20
        ),
    )(*(pltpu.with_memory_space_constraint(x, pltpu.HBM) for x in (heights, blocked, estimate, portal_index)))
    return pl.pallas_call(
        hand_out,
        out_shape=tuple(pltpu.HBM(x.shape, x.dtype) for x in outs),
        in_specs=[in_vmem] * 2,
        out_specs=[in_hbm] * 2,
        scratch_shapes=[pltpu.SemaphoreType.DMA((2,))],
        compiler_params=pltpu.CompilerParams(vmem_limit_bytes=2**20),
    )(*(pltpu.with_memory_space_constraint(x, pltpu.VMEM) for x in results))


def solution(mesh):
    placed = (P("row", "col"), P("row", "col"), P("row", "col"), P("row", "col", None))
    return jax.shard_map(
        body,
        mesh=mesh,
        in_specs=placed,
        out_specs=(P("row", "col"), P("row", "col", None, None)),
        check_vma=False,
    )
```

```python
import functools

import jax
import jax.numpy as jnp
from jax import lax
from jax.experimental import pallas as pl
from jax.experimental.pallas import tpu as pltpu
from jax.sharding import PartitionSpec as P

TILE = 64
PORTALS = 32
SWEEPS = 8
HALO = 8
EXT = TILE + 2 * HALO
LANES = 128
BLOCKS = LANES // PORTALS
OWN = TILE // BLOCKS
GROUPS = EXT // BLOCKS
STEP = EXT // 8
STRIP = 16
FAR = 1000000.0


AROUND = ((-1, -1), (-1, 1), (1, -1), (1, 1), (-1, 0), (1, 0), (0, -1), (0, 1))


def lane_take(values, index):
    return jnp.take_along_axis(values, index, axis=1, mode="promise_in_bounds")


def kernel(
    heights_hbm, blocked_hbm, estimate_hbm, portal_hbm,
    relaxed, merged,
    heights, blocked, estimate, portal, portal_smem,
    ground, strips, ground_in, high, cost_rows,
    field, side_out, side_in, cost, dist, rows, shifts, table, table_in, right_rows,
    load_sem, ground_send, ground_recv, field_send, field_recv, table_send, table_recv,
):
    row_index, col_index = lax.axis_index("row"), lax.axis_index("col")
    row_count, col_count = lax.axis_size("row"), lax.axis_size("col")
    around = [
        (lax.rem(row_index + dr + row_count, row_count), lax.rem(col_index + dc + col_count, col_count))
        for dr, dc in AROUND
    ]

    def other(index, bit):
        return index + bit - 2 * bit * lax.rem(index // bit, 2)

    partners = []
    for level in range(2):
        bit = 1 << level
        partners.append(
            [
                (other(row_index, bit), col_index),
                (row_index, other(col_index, bit)),
                (other(row_index, bit), other(col_index, bit)),
            ]
        )

    barrier = pltpu.get_barrier_semaphore()
    met = around
    for device in met:
        pl.semaphore_signal(barrier, inc=1, device_id=device, device_id_type=pl.DeviceIdType.MESH)

    loads = [
        pltpu.make_async_copy(source, target, load_sem.at[at])
        for at, (source, target) in enumerate(
            (
                (heights_hbm, heights),
                (blocked_hbm, blocked),
                (portal_hbm, portal),
                (estimate_hbm.at[0:16], estimate.at[0:16]),
                (estimate_hbm.at[48:64], estimate.at[48:64]),
                (estimate_hbm.at[16:48], estimate.at[16:48]),
                (portal_hbm, portal_smem),
            )
        )
    ]
    for load in loads:
        load.start()

    def send(source, target, send_sem, recv_sem, device):
        copy = pltpu.make_async_remote_copy(
            src_ref=source, dst_ref=target, send_sem=send_sem, recv_sem=recv_sem,
            device_id=device, device_id_type=pl.DeviceIdType.MESH,
        )
        copy.start()
        return copy

    lane = lax.broadcasted_iota(jnp.int32, (8, LANES), 1)
    sublane = lax.broadcasted_iota(jnp.int32, (8, LANES), 0)
    lane_block = lane // PORTALS
    lane_class = lane % PORTALS

    loads[0].wait()
    loads[1].wait()
    ground[:, 0:TILE] = heights[...]
    ground[:, TILE : 2 * TILE] = blocked[...]
    wide = lax.broadcasted_iota(jnp.int32, (STRIP, LANES), 1)
    west = jnp.zeros((STRIP, LANES), jnp.int32)
    east = jnp.zeros((STRIP, LANES), jnp.int32)
    for part in range(4):
        here = ground[part * STRIP : (part + 1) * STRIP]
        base = part * 32
        in_height = (wide >= base) & (wide < base + 16)
        in_block = (wide >= base + 16) & (wide < base + 32)
        west = jnp.where(in_height, pltpu.roll(here, base % LANES, 1), west)
        west = jnp.where(in_block, pltpu.roll(here, (base + 16 - 64) % LANES, 1), west)
        east = jnp.where(in_height, pltpu.roll(here, (base - 48) % LANES, 1), east)
        east = jnp.where(in_block, pltpu.roll(here, (base + 16 - 112) % LANES, 1), east)
    strips[0] = west
    strips[1] = east

    loads[2].wait()
    own = jnp.broadcast_to(portal[0, 0:1, :], (8, PORTALS))
    portal_cells = jnp.concatenate([own] * BLOCKS, axis=1)
    loads[3].wait()
    loads[4].wait()
    loads[5].wait()
    low = lane < 2 * PORTALS
    even = lane_block % 2 == 0
    swapped_blocks = lane_class + (lane_block + 1 - 2 * (lane_block % 2)) * PORTALS

    def transposed(a):
        t = [None] * 4
        for at in range(2):
            turned = pltpu.roll(jnp.where(low, a[at + 2], a[at]), 2 * PORTALS, 1)
            t[at], t[at + 2] = jnp.where(low, a[at], turned), jnp.where(low, turned, a[at + 2])
        out = [None] * 4
        for at in (0, 2):
            turned = lane_take(jnp.where(even, t[at + 1], t[at]), swapped_blocks)
            out[at], out[at + 1] = jnp.where(even, t[at], turned), jnp.where(even, turned, t[at + 1])
        return out

    def estimates(part, group):
        values = estimate[part * 16 : (part + 1) * 16, group * LANES : (group + 1) * LANES]
        values = values.astype(jnp.float32)
        return values[0:8], values[8:16]

    def prepare(part):
        for first in range(4):
            halves = [estimates(part, first + 4 * at) for at in range(4)]
            for half in range(2):
                row = part * 16 + half * 8
                cell = (row + sublane) * TILE + lane_block * OWN
                for at, values in enumerate(transposed([pieces[half] for pieces in halves])):
                    group = 4 * first + at
                    field[group, HALO + row : HALO + row + 8, :] = jnp.where(
                        portal_cells == cell + group, 0.0, values
                    )

    def edges(part):
        columns = (0, 1, OWN - 2, OWN - 1)
        pieces = [estimates(part, group) for group in columns]
        for half in range(2):
            row = part * 16 + half * 8
            cell = (row + sublane) * TILE + lane_block
            w0, w1, e0, e1 = (
                jnp.where(portal_cells == cell + group * BLOCKS, 0.0, piece[half])
                for group, piece in zip(columns, pieces)
            )
            side_out[0, 0, row : row + 8, :] = jnp.where(even, w0, pltpu.roll(w1, 32, 1))
            side_out[0, 1, row : row + 8, :] = jnp.where(even, pltpu.roll(w0, 96, 1), w1)
            side_out[1, 0, row : row + 8, :] = jnp.where(even, pltpu.roll(e0, 64, 1), pltpu.roll(e1, 96, 1))
            side_out[1, 1, row : row + 8, :] = jnp.where(even, pltpu.roll(e0, 32, 1), pltpu.roll(e1, 64, 1))

    prepare(0)
    prepare(3)
    for part in range(4):
        edges(part)

    pl.semaphore_wait(barrier, len(met))

    top, bottom = ground.at[0:STRIP], ground.at[TILE - STRIP : TILE]
    ground_source = {-1: top, 1: bottom}
    ground_copies = []
    for at, (dr, dc) in enumerate(AROUND):
        if dr:
            source = ground_source[dr]
        else:
            source = strips.at[0 if dc < 0 else 1]
        slot = AROUND.index((-dr, -dc))
        ground_copies.append(
            send(source, ground_in.at[slot], ground_send.at[at], ground_recv.at[slot], around[at])
        )

    field_copies = []
    for at, (dr, dc) in enumerate(AROUND):
        row_from, row_to, row_len = {
            -1: (0, HALO + TILE, HALO), 0: (0, HALO, TILE), 1: (TILE - HALO, 0, HALO)
        }[dr]
        if dc:
            side = 0 if dc < 0 else 1
            source = side_out.at[side, :, pl.ds(row_from, row_len), :]
            target = side_in.at[side, :, pl.ds(row_to, row_len), :]
        else:
            source = field.at[:, pl.ds(HALO + row_from, row_len), :]
            target = field.at[:, pl.ds(row_to, row_len), :]
        slot = AROUND.index((-dr, -dc))
        field_copies.append(send(source, target, field_send.at[at], field_recv.at[slot], around[at]))

    prepare(1)
    prepare(2)

    for copy in ground_copies:
        copy.wait_recv()
    slots = {step: at for at, step in enumerate(AROUND)}

    def lay(row, west_height, middle, east_height, west_block, east_block):
        height = jnp.where(wide < 16, west_height, jnp.where(wide < 80, pltpu.roll(middle, 16, 1), east_height))
        block = jnp.where(wide < 16, west_block, jnp.where(wide < 80, pltpu.roll(middle, 80, 1), east_block))
        high[0, row : row + STRIP, :] = height.astype(jnp.float32)
        high[1, row : row + STRIP, :] = block.astype(jnp.float32)

    for dr, row in ((-1, 0), (1, STRIP + TILE)):
        west_in, middle, east_in = (ground_in[slots[(dr, dc)]] for dc in (-1, 0, 1))
        lay(
            row, pltpu.roll(west_in, 80, 1), middle, pltpu.roll(east_in, 80, 1),
            pltpu.roll(west_in, 16, 1), pltpu.roll(east_in, 16, 1),
        )
    west_in, east_in = ground_in[slots[(0, -1)]], ground_in[slots[(0, 1)]]
    for part in range(4):
        base = part * 32
        lay(
            STRIP + part * STRIP,
            pltpu.roll(west_in, (-base) % LANES, 1),
            ground[part * STRIP : (part + 1) * STRIP],
            pltpu.roll(east_in, (80 - base) % LANES, 1),
            pltpu.roll(west_in, (-base - 16) % LANES, 1),
            pltpu.roll(east_in, (64 - base) % LANES, 1),
        )

    @pl.when(row_index == 0)
    def _():
        high[0, STRIP - 1 : STRIP, :] = high[0, STRIP : STRIP + 1, :]

    @pl.when(row_index == row_count - 1)
    def _():
        high[0, STRIP + TILE : STRIP + TILE + 1, :] = high[0, STRIP + TILE - 1 : STRIP + TILE, :]

    shift = STRIP - HALO
    near = high[0, shift : shift + EXT, :]
    up = high[0, shift - 1 : shift - 1 + EXT, :]
    down = high[0, shift + 1 : shift + 1 + EXT, :]
    col = lax.broadcasted_iota(jnp.int32, (EXT, LANES), 1) - STRIP
    row = lax.broadcasted_iota(jnp.int32, (EXT, LANES), 0) - HALO
    grid_col = col_index * TILE + col
    grid_row = row_index * TILE + row
    before = jnp.where(grid_col == 0, near, pltpu.roll(near, 1, 1))
    after = jnp.where(grid_col == col_count * TILE - 1, near, pltpu.roll(near, LANES - 1, 1))
    grad_x = (after - before) * 0.01
    grad_y = (down - up) * 0.01
    grad_sq = grad_x * grad_x + grad_y * grad_y
    step_cost = (
        1.0 + 2.0 * grad_sq + 0.5 * grad_y / jnp.sqrt(1.0 + grad_sq)
        + 30.0 * high[1, shift : shift + EXT, :]
    )
    inside = (
        (grid_row >= 0) & (grid_row < row_count * TILE)
        & (grid_col >= 0) & (grid_col < col_count * TILE)
    )
    cost_rows[...] = jnp.where(inside, step_cost, FAR)
    first_column = STRIP + lane_block * OWN
    halo_shift = jnp.where(low, TILE + 4 * lane_block, 4 * lane_block - 16) - lane_block * OWN
    for at in range(STEP):
        values = cost_rows[pl.ds(at, 8, stride=STEP), :]
        for group in range(GROUPS):
            cost[group, at] = lane_take(values, first_column + (group if group < OWN else group - OWN + halo_shift))

    loads[6].wait()
    cells = [portal_smem[0, 0, at] for at in range(PORTALS)]
    for at, cell in enumerate(cells):
        shifts[at : at + 1, :] = jnp.full((1, LANES), ((cell >> 4) & (BLOCKS - 1)) * PORTALS, jnp.int32)

    for copy in field_copies:
        copy.wait_recv()

    def half_cost(group, at):
        here = cost[group, at]
        return jnp.where(here >= FAR, FAR, 0.5 * here)

    def start(group, at, distance):
        dist[group, at] = jnp.minimum(distance + half_cost(group, at), FAR)

    for at in range(STEP):
        for group in range(OWN):
            start(group, at, field[group, pl.ds(at, 8, stride=STEP), :])
        for piece in range(2):
            from_east = side_in[0, piece, pl.ds(at, 8, stride=STEP), :]
            from_west = side_in[1, piece, pl.ds(at, 8, stride=STEP), :]
            start(OWN + piece, at, jnp.where(low, from_east, from_west))
            start(OWN + piece + 2, at, pltpu.roll(jnp.where(low, from_west, from_east), 64, 1))

    first_block, last_block = lane_block == 0, lane_block == BLOCKS - 1

    def sweep(_, carry):
        def pairs_of(here, east_of):
            below = east_of[1:] + [pltpu.roll(east_of[0], 7, 0)]
            return [jnp.minimum(a, b) for a, b in zip(here, below)]

        def column(group):
            return [dist[group, at] for at in range(STEP)]

        own_first, halo_first = column(0), column(OWN)
        own_pairs = pairs_of(
            column(OWN - 1),
            [pltpu.roll(jnp.where(first_block, a, b), LANES - PORTALS, 1) for a, b in zip(halo_first, own_first)],
        )
        halo_pairs = pairs_of(
            column(GROUPS - 1),
            [pltpu.roll(jnp.where(first_block, a, b), LANES - PORTALS, 1) for a, b in zip(own_first, halo_first)],
        )
        own_west = [pltpu.roll(jnp.where(last_block, a, b), PORTALS, 1) for a, b in zip(halo_pairs, own_pairs)]
        halo_west = [pltpu.roll(jnp.where(last_block, a, b), PORTALS, 1) for a, b in zip(own_pairs, halo_pairs)]
        for begin, end, west_of, end_pairs in ((0, OWN, own_west, own_pairs), (OWN, GROUPS, halo_west, halo_pairs)):
            now = own_first if begin == 0 else column(begin)
            for group in range(begin, end):
                if group < end - 1:
                    later = column(group + 1)
                    pairs = pairs_of(now, later)
                else:
                    pairs = end_pairs
                north = [pltpu.roll(pairs[STEP - 1], 1, 0)] + pairs[:-1]
                for at in range(STEP):
                    nearest = cost[group, at] + jnp.minimum(north[at], west_of[at])
                    dist[group, at] = jnp.minimum(now[at], nearest)
                west_of, now = pairs, later
        return carry

    lax.fori_loop(0, SWEEPS, sweep, 0)

    for copy in field_copies:
        copy.wait_send()
    for group in range(OWN):
        for at in range(STEP):
            field[group, pl.ds(at, 8, stride=STEP), :] = dist[group, at] - 0.5 * cost[group, at]

    for at, cell in enumerate(cells):
        rows[at : at + 1, :] = field[cell & (OWN - 1), pl.ds(HALO + (cell >> 6), 1), :]
    first = jnp.zeros((8, LANES), jnp.float32)
    for part in range(4):
        index = shifts[part * 8 : part * 8 + 8, :] + lane_class
        first = jnp.where(lane_block == part, lane_take(rows[part * 8 : part * 8 + 8, :], index), first)
    table[0] = first

    table_copies = []

    def exchange(level):
        copies = [
            send(
                table.at[level], table_in.at[3 * level + at],
                table_send.at[3 * level + at], table_recv.at[3 * level + at], device,
            )
            for at, device in reversed(tuple(enumerate(partners[level])))
        ]
        table_copies.extend(reversed(copies))

    def left_of(values):
        return [lane_take(values, lane_block * PORTALS + at) for at in range(PORTALS)]

    def right_of(values, slot):
        for part in range(4):
            right_rows[slot, part * 8 : part * 8 + 8, :] = lane_take(values, lane_class + part * PORTALS)
        return [
            jnp.broadcast_to(right_rows[slot, at : at + 1, :], (8, LANES)) for at in range(PORTALS)
        ]

    def minplus(left, right):
        sums = [a + b for a, b in zip(left, right)]
        while len(sums) > 1:
            sums = [jnp.minimum(a, b) for a, b in zip(sums[::2], sums[1::2])]
        return sums[0]

    def pair(near_table, near_left, near_right, far_right):
        through = minplus(near_left, far_right)
        return jnp.minimum(near_table, minplus(left_of(through), near_right))

    def relax_out(part):
        for first_at in range(4):
            for_rows = [
                transposed(
                    [
                        field[4 * first_at + at, HALO + part * 16 + half * 8 : HALO + part * 16 + half * 8 + 8, :]
                        for at in range(4)
                    ]
                )
                for half in range(2)
            ]
            for at in range(4):
                group = first_at + 4 * at
                values = jnp.concatenate([for_rows[0][at], for_rows[1][at]], axis=0)
                relaxed[part * 16 : part * 16 + 16, group * LANES : (group + 1) * LANES] = values.astype(jnp.bfloat16)

    now = first
    for level in range(2):
        exchange(level)
        now_left, now_right = left_of(now), right_of(now, 6 * level)
        relax_out(2 * level)
        relax_out(2 * level + 1)
        def arrived(at):
            table_copies[3 * level + at].wait_recv()
            return table_in[3 * level + at]

        by_col = arrived(1)
        col_left, col_right = left_of(by_col), right_of(by_col, 6 * level + 2)
        by_row = arrived(0)
        here = pair(now, now_left, now_right, right_of(by_row, 6 * level + 1))
        here_left, here_right = left_of(here), right_of(here, 6 * level + 4)
        there = pair(by_col, col_left, col_right, right_of(arrived(2), 6 * level + 3))
        now = pair(here, here_left, here_right, right_of(there, 6 * level + 5))
        if level == 0:
            table[1] = now
    now = now * 0.0625
    for part in range(4):
        merged[0, 0, part * 8 : part * 8 + 8, :] = now[:, part * PORTALS : (part + 1) * PORTALS]

    for copy in ground_copies + table_copies:
        copy.wait_send()


def hand_out(relaxed_in, merged_in, relaxed, merged, sem):
    copies = [
        pltpu.make_async_copy(relaxed_in, relaxed, sem.at[0]),
        pltpu.make_async_copy(merged_in, merged, sem.at[1]),
    ]
    for copy in copies:
        copy.start()
    for copy in copies:
        copy.wait()


def body(heights, blocked, estimate, portal_index):
    in_hbm = pl.BlockSpec(memory_space=pltpu.HBM)
    in_vmem = pl.BlockSpec(memory_space=pltpu.VMEM)
    outs = (
        jax.ShapeDtypeStruct(estimate.shape, jnp.bfloat16),
        jax.ShapeDtypeStruct((1, 1, PORTALS, PORTALS), jnp.float32),
    )
    results = pl.pallas_call(
        kernel,
        out_shape=outs,
        in_specs=[in_hbm] * 4,
        out_specs=(in_vmem, in_vmem),
        scratch_shapes=[
            pltpu.VMEM((TILE, TILE), jnp.int32),
            pltpu.VMEM((TILE, TILE), jnp.int32),
            pltpu.VMEM((TILE, TILE * PORTALS), jnp.bfloat16),
            pltpu.VMEM((1, 1, PORTALS), jnp.int32),
            pltpu.SMEM((1, 1, PORTALS), jnp.int32),
            pltpu.VMEM((TILE, LANES), jnp.int32),
            pltpu.VMEM((2, STRIP, LANES), jnp.int32),
            pltpu.VMEM((8, STRIP, LANES), jnp.int32),
            pltpu.VMEM((2, TILE + 2 * STRIP, LANES), jnp.float32),
            pltpu.VMEM((EXT, LANES), jnp.float32),
            pltpu.VMEM((OWN, EXT, LANES), jnp.float32),
            pltpu.VMEM((2, 2, TILE, LANES), jnp.float32),
            pltpu.VMEM((2, 2, EXT, LANES), jnp.float32),
            pltpu.VMEM((GROUPS, STEP, 8, LANES), jnp.float32),
            pltpu.VMEM((GROUPS, STEP, 8, LANES), jnp.float32),
            pltpu.VMEM((PORTALS, LANES), jnp.float32),
            pltpu.VMEM((PORTALS, LANES), jnp.int32),
            pltpu.VMEM((2, 8, LANES), jnp.float32),
            pltpu.VMEM((6, 8, LANES), jnp.float32),
            pltpu.VMEM((12, PORTALS, LANES), jnp.float32),
            pltpu.SemaphoreType.DMA((7,)),
            pltpu.SemaphoreType.DMA((8,)),
            pltpu.SemaphoreType.DMA((8,)),
            pltpu.SemaphoreType.DMA((8,)),
            pltpu.SemaphoreType.DMA((8,)),
            pltpu.SemaphoreType.DMA((6,)),
            pltpu.SemaphoreType.DMA((6,)),
        ],
        compiler_params=pltpu.CompilerParams(
            collective_id=0, has_side_effects=True, vmem_limit_bytes=16 * 2**20
        ),
    )(*(pltpu.with_memory_space_constraint(x, pltpu.HBM) for x in (heights, blocked, estimate, portal_index)))
    return pl.pallas_call(
        hand_out,
        out_shape=tuple(pltpu.HBM(x.shape, x.dtype) for x in outs),
        in_specs=[in_vmem] * 2,
        out_specs=[in_hbm] * 2,
        scratch_shapes=[pltpu.SemaphoreType.DMA((2,))],
        compiler_params=pltpu.CompilerParams(vmem_limit_bytes=2**20),
    )(*(pltpu.with_memory_space_constraint(x, pltpu.VMEM) for x in results))


def solution(mesh):
    placed = (P("row", "col"), P("row", "col"), P("row", "col"), P("row", "col", None))
    return jax.shard_map(
        body,
        mesh=mesh,
        in_specs=placed,
        out_specs=(P("row", "col"), P("row", "col", None, None)),
        check_vma=False,
    )
```

```python
import functools

import jax
import jax.numpy as jnp
from jax import lax
from jax.experimental import pallas as pl
from jax.experimental.pallas import tpu as pltpu
from jax.sharding import PartitionSpec as P

TILE = 64
PORTALS = 32
SWEEPS = 8
HALO = 8
EXT = TILE + 2 * HALO
LANES = 128
BLOCKS = LANES // PORTALS
OWN = TILE // BLOCKS
GROUPS = EXT // BLOCKS
STEP = EXT // 8
STRIP = 16
FAR = 1000000.0


AROUND = ((-1, -1), (-1, 1), (1, -1), (1, 1), (-1, 0), (1, 0), (0, -1), (0, 1))


def lane_take(values, index):
    return jnp.take_along_axis(values, index, axis=1, mode="promise_in_bounds")


def kernel(
    heights_hbm, blocked_hbm, estimate_hbm, portal_hbm,
    relaxed, merged,
    heights, blocked, estimate, portal, portal_smem,
    ground, strips, ground_in, high, cost_rows,
    field, side_out, side_in, cost, dist, rows, shifts, table, table_in, right_rows,
    load_sem, ground_send, ground_recv, field_send, field_recv, table_send, table_recv,
):
    row_index, col_index = lax.axis_index("row"), lax.axis_index("col")
    row_count, col_count = lax.axis_size("row"), lax.axis_size("col")
    around = [
        (lax.rem(row_index + dr + row_count, row_count), lax.rem(col_index + dc + col_count, col_count))
        for dr, dc in AROUND
    ]

    def other(index, bit):
        return index + bit - 2 * bit * lax.rem(index // bit, 2)

    partners = []
    for level in range(2):
        bit = 1 << level
        partners.append(
            [
                (other(row_index, bit), col_index),
                (row_index, other(col_index, bit)),
                (other(row_index, bit), other(col_index, bit)),
            ]
        )

    barrier = pltpu.get_barrier_semaphore()
    met = around
    for device in met:
        pl.semaphore_signal(barrier, inc=1, device_id=device, device_id_type=pl.DeviceIdType.MESH)

    loads = [
        pltpu.make_async_copy(source, target, load_sem.at[at])
        for at, (source, target) in enumerate(
            (
                (heights_hbm, heights),
                (blocked_hbm, blocked),
                (portal_hbm, portal),
                (estimate_hbm.at[0:16], estimate.at[0:16]),
                (estimate_hbm.at[48:64], estimate.at[48:64]),
                (estimate_hbm.at[16:48], estimate.at[16:48]),
                (portal_hbm, portal_smem),
            )
        )
    ]
    for load in loads:
        load.start()

    def send(source, target, send_sem, recv_sem, device):
        copy = pltpu.make_async_remote_copy(
            src_ref=source, dst_ref=target, send_sem=send_sem, recv_sem=recv_sem,
            device_id=device, device_id_type=pl.DeviceIdType.MESH,
        )
        copy.start()
        return copy

    lane = lax.broadcasted_iota(jnp.int32, (8, LANES), 1)
    sublane = lax.broadcasted_iota(jnp.int32, (8, LANES), 0)
    lane_block = lane // PORTALS
    lane_class = lane % PORTALS

    loads[0].wait()
    loads[1].wait()
    ground[:, 0:TILE] = heights[...]
    ground[:, TILE : 2 * TILE] = blocked[...]
    wide = lax.broadcasted_iota(jnp.int32, (STRIP, LANES), 1)
    west = jnp.zeros((STRIP, LANES), jnp.int32)
    east = jnp.zeros((STRIP, LANES), jnp.int32)
    for part in range(4):
        here = ground[part * STRIP : (part + 1) * STRIP]
        base = part * 32
        in_height = (wide >= base) & (wide < base + 16)
        in_block = (wide >= base + 16) & (wide < base + 32)
        west = jnp.where(in_height, pltpu.roll(here, base % LANES, 1), west)
        west = jnp.where(in_block, pltpu.roll(here, (base + 16 - 64) % LANES, 1), west)
        east = jnp.where(in_height, pltpu.roll(here, (base - 48) % LANES, 1), east)
        east = jnp.where(in_block, pltpu.roll(here, (base + 16 - 112) % LANES, 1), east)
    strips[0] = west
    strips[1] = east

    loads[2].wait()
    own = jnp.broadcast_to(portal[0, 0:1, :], (8, PORTALS))
    portal_cells = jnp.concatenate([own] * BLOCKS, axis=1)
    loads[3].wait()
    loads[4].wait()
    loads[5].wait()
    low = lane < 2 * PORTALS
    even = lane_block % 2 == 0
    swapped_blocks = lane_class + (lane_block + 1 - 2 * (lane_block % 2)) * PORTALS

    def transposed(a):
        t = [None] * 4
        for at in range(2):
            turned = pltpu.roll(jnp.where(low, a[at + 2], a[at]), 2 * PORTALS, 1)
            t[at], t[at + 2] = jnp.where(low, a[at], turned), jnp.where(low, turned, a[at + 2])
        out = [None] * 4
        for at in (0, 2):
            turned = lane_take(jnp.where(even, t[at + 1], t[at]), swapped_blocks)
            out[at], out[at + 1] = jnp.where(even, t[at], turned), jnp.where(even, turned, t[at + 1])
        return out

    def estimates(part, group):
        values = estimate[part * 16 : (part + 1) * 16, group * LANES : (group + 1) * LANES]
        values = values.astype(jnp.float32)
        return values[0:8], values[8:16]

    def prepare(part):
        for first in range(4):
            halves = [estimates(part, first + 4 * at) for at in range(4)]
            for half in range(2):
                row = part * 16 + half * 8
                cell = (row + sublane) * TILE + lane_block * OWN
                for at, values in enumerate(transposed([pieces[half] for pieces in halves])):
                    group = 4 * first + at
                    field[group, HALO + row : HALO + row + 8, :] = jnp.where(
                        portal_cells == cell + group, 0.0, values
                    )

    def edges(part):
        columns = (0, 1, OWN - 2, OWN - 1)
        pieces = [estimates(part, group) for group in columns]
        for half in range(2):
            row = part * 16 + half * 8
            cell = (row + sublane) * TILE + lane_block
            w0, w1, e0, e1 = (
                jnp.where(portal_cells == cell + group * BLOCKS, 0.0, piece[half])
                for group, piece in zip(columns, pieces)
            )
            side_out[0, 0, row : row + 8, :] = jnp.where(even, w0, pltpu.roll(w1, 32, 1))
            side_out[0, 1, row : row + 8, :] = jnp.where(even, pltpu.roll(w0, 96, 1), w1)
            side_out[1, 0, row : row + 8, :] = jnp.where(even, pltpu.roll(e0, 64, 1), pltpu.roll(e1, 96, 1))
            side_out[1, 1, row : row + 8, :] = jnp.where(even, pltpu.roll(e0, 32, 1), pltpu.roll(e1, 64, 1))

    prepare(0)
    prepare(3)
    for part in range(4):
        edges(part)

    pl.semaphore_wait(barrier, len(met))

    top, bottom = ground.at[0:STRIP], ground.at[TILE - STRIP : TILE]
    ground_source = {-1: top, 1: bottom}
    ground_copies = []
    for at, (dr, dc) in enumerate(AROUND):
        if dr:
            source = ground_source[dr]
        else:
            source = strips.at[0 if dc < 0 else 1]
        slot = AROUND.index((-dr, -dc))
        ground_copies.append(
            send(source, ground_in.at[slot], ground_send.at[at], ground_recv.at[slot], around[at])
        )

    field_copies = []
    for at, (dr, dc) in enumerate(AROUND):
        row_from, row_to, row_len = {
            -1: (0, HALO + TILE, HALO), 0: (0, HALO, TILE), 1: (TILE - HALO, 0, HALO)
        }[dr]
        if dc:
            side = 0 if dc < 0 else 1
            source = side_out.at[side, :, pl.ds(row_from, row_len), :]
            target = side_in.at[side, :, pl.ds(row_to, row_len), :]
        else:
            source = field.at[:, pl.ds(HALO + row_from, row_len), :]
            target = field.at[:, pl.ds(row_to, row_len), :]
        slot = AROUND.index((-dr, -dc))
        field_copies.append(send(source, target, field_send.at[at], field_recv.at[slot], around[at]))

    prepare(1)
    prepare(2)

    for copy in ground_copies:
        copy.wait_recv()
    slots = {step: at for at, step in enumerate(AROUND)}

    def lay(row, west_height, middle, east_height, west_block, east_block):
        height = jnp.where(wide < 16, west_height, jnp.where(wide < 80, pltpu.roll(middle, 16, 1), east_height))
        block = jnp.where(wide < 16, west_block, jnp.where(wide < 80, pltpu.roll(middle, 80, 1), east_block))
        high[0, row : row + STRIP, :] = height.astype(jnp.float32)
        high[1, row : row + STRIP, :] = block.astype(jnp.float32)

    for dr, row in ((-1, 0), (1, STRIP + TILE)):
        west_in, middle, east_in = (ground_in[slots[(dr, dc)]] for dc in (-1, 0, 1))
        lay(
            row, pltpu.roll(west_in, 80, 1), middle, pltpu.roll(east_in, 80, 1),
            pltpu.roll(west_in, 16, 1), pltpu.roll(east_in, 16, 1),
        )
    west_in, east_in = ground_in[slots[(0, -1)]], ground_in[slots[(0, 1)]]
    for part in range(4):
        base = part * 32
        lay(
            STRIP + part * STRIP,
            pltpu.roll(west_in, (-base) % LANES, 1),
            ground[part * STRIP : (part + 1) * STRIP],
            pltpu.roll(east_in, (80 - base) % LANES, 1),
            pltpu.roll(west_in, (-base - 16) % LANES, 1),
            pltpu.roll(east_in, (64 - base) % LANES, 1),
        )

    @pl.when(row_index == 0)
    def _():
        high[0, STRIP - 1 : STRIP, :] = high[0, STRIP : STRIP + 1, :]

    @pl.when(row_index == row_count - 1)
    def _():
        high[0, STRIP + TILE : STRIP + TILE + 1, :] = high[0, STRIP + TILE - 1 : STRIP + TILE, :]

    shift = STRIP - HALO
    near = high[0, shift : shift + EXT, :]
    up = high[0, shift - 1 : shift - 1 + EXT, :]
    down = high[0, shift + 1 : shift + 1 + EXT, :]
    col = lax.broadcasted_iota(jnp.int32, (EXT, LANES), 1) - STRIP
    row = lax.broadcasted_iota(jnp.int32, (EXT, LANES), 0) - HALO
    grid_col = col_index * TILE + col
    grid_row = row_index * TILE + row
    before = jnp.where(grid_col == 0, near, pltpu.roll(near, 1, 1))
    after = jnp.where(grid_col == col_count * TILE - 1, near, pltpu.roll(near, LANES - 1, 1))
    grad_x = (after - before) * 0.01
    grad_y = (down - up) * 0.01
    grad_sq = grad_x * grad_x + grad_y * grad_y
    step_cost = (
        1.0 + 2.0 * grad_sq + 0.5 * grad_y / jnp.sqrt(1.0 + grad_sq)
        + 30.0 * high[1, shift : shift + EXT, :]
    )
    inside = (
        (grid_row >= 0) & (grid_row < row_count * TILE)
        & (grid_col >= 0) & (grid_col < col_count * TILE)
    )
    cost_rows[...] = jnp.where(inside, step_cost, 2.0 * FAR)
    first_column = STRIP + lane_block * OWN
    halo_shift = jnp.where(low, TILE + 4 * lane_block, 4 * lane_block - 16) - lane_block * OWN
    for at in range(STEP):
        values = cost_rows[pl.ds(at, 8, stride=STEP), :]
        for group in range(GROUPS):
            cost[group, at] = lane_take(values, first_column + (group if group < OWN else group - OWN + halo_shift))

    loads[6].wait()
    cells = [portal_smem[0, 0, at] for at in range(PORTALS)]
    for at, cell in enumerate(cells):
        shifts[at : at + 1, :] = jnp.full((1, LANES), ((cell >> 4) & (BLOCKS - 1)) * PORTALS, jnp.int32)

    for copy in field_copies:
        copy.wait_recv()

    def started(group, at, distance):
        return jnp.minimum(distance + 0.5 * cost[group, at], FAR)

    for at in range(STEP):
        for piece in range(2):
            from_east = side_in[0, piece, pl.ds(at, 8, stride=STEP), :]
            from_west = side_in[1, piece, pl.ds(at, 8, stride=STEP), :]
            for group, values in (
                (OWN + piece, jnp.where(low, from_east, from_west)),
                (OWN + piece + 2, pltpu.roll(jnp.where(low, from_west, from_east), 64, 1)),
            ):
                dist[group, at] = started(group, at, values)

    first_block, last_block = lane_block == 0, lane_block == BLOCKS - 1

    def sweep(first, last):
        def pairs_of(here, east_of):
            below = east_of[1:] + [pltpu.roll(east_of[0], 7, 0)]
            return [jnp.minimum(a, b) for a, b in zip(here, below)]

        def column(group):
            if first and group < OWN:
                return [started(group, at, field[group, pl.ds(at, 8, stride=STEP), :]) for at in range(STEP)]
            return [dist[group, at] for at in range(STEP)]

        own_first, halo_first = column(0), column(OWN)
        own_pairs = pairs_of(
            column(OWN - 1),
            [pltpu.roll(jnp.where(first_block, a, b), LANES - PORTALS, 1) for a, b in zip(halo_first, own_first)],
        )
        halo_pairs = pairs_of(
            column(GROUPS - 1),
            [pltpu.roll(jnp.where(first_block, a, b), LANES - PORTALS, 1) for a, b in zip(own_first, halo_first)],
        )
        own_west = [pltpu.roll(jnp.where(last_block, a, b), PORTALS, 1) for a, b in zip(halo_pairs, own_pairs)]
        halo_west = [pltpu.roll(jnp.where(last_block, a, b), PORTALS, 1) for a, b in zip(own_pairs, halo_pairs)]
        for begin, end, west_of, end_pairs in ((0, OWN, own_west, own_pairs), (OWN, GROUPS, halo_west, halo_pairs)):
            if last and begin == OWN:
                continue
            now = own_first if begin == 0 else column(begin)
            for group in range(begin, end):
                if group < end - 1:
                    later = column(group + 1)
                    pairs = pairs_of(now, later)
                else:
                    pairs = end_pairs
                north = [pltpu.roll(pairs[STEP - 1], 1, 0)] + pairs[:-1]
                for at in range(STEP):
                    here = cost[group, at]
                    shortest = jnp.minimum(now[at], here + jnp.minimum(north[at], west_of[at]))
                    if last:
                        field[group, pl.ds(at, 8, stride=STEP), :] = shortest - 0.5 * here
                    else:
                        dist[group, at] = shortest
                west_of, now = pairs, later

    sweep(True, False)
    def middle(_, carry):
        sweep(False, False)
        return carry

    lax.fori_loop(0, SWEEPS - 2, middle, 0)
    for copy in field_copies:
        copy.wait_send()
    sweep(False, True)

    for at, cell in enumerate(cells):
        rows[at : at + 1, :] = field[cell & (OWN - 1), pl.ds(HALO + (cell >> 6), 1), :]
    first = jnp.zeros((8, LANES), jnp.float32)
    for part in range(4):
        index = shifts[part * 8 : part * 8 + 8, :] + lane_class
        first = jnp.where(lane_block == part, lane_take(rows[part * 8 : part * 8 + 8, :], index), first)
    table[0] = first

    table_copies = []

    def exchange(level):
        copies = [
            send(
                table.at[level], table_in.at[3 * level + at],
                table_send.at[3 * level + at], table_recv.at[3 * level + at], device,
            )
            for at, device in reversed(tuple(enumerate(partners[level])))
        ]
        table_copies.extend(reversed(copies))

    def left_of(values):
        return [lane_take(values, lane_block * PORTALS + at) for at in range(PORTALS)]

    def right_of(values, slot):
        for part in range(4):
            right_rows[slot, part * 8 : part * 8 + 8, :] = lane_take(values, lane_class + part * PORTALS)
        return [
            jnp.broadcast_to(right_rows[slot, at : at + 1, :], (8, LANES)) for at in range(PORTALS)
        ]

    def minplus(left, right):
        sums = [a + b for a, b in zip(left, right)]
        while len(sums) > 1:
            sums = [jnp.minimum(a, b) for a, b in zip(sums[::2], sums[1::2])]
        return sums[0]

    def pair(near_table, near_left, near_right, far_right):
        through = minplus(near_left, far_right)
        return jnp.minimum(near_table, minplus(left_of(through), near_right))

    def relax_out(part):
        for first_at in range(4):
            for_rows = [
                transposed(
                    [
                        field[4 * first_at + at, HALO + part * 16 + half * 8 : HALO + part * 16 + half * 8 + 8, :]
                        for at in range(4)
                    ]
                )
                for half in range(2)
            ]
            for at in range(4):
                group = first_at + 4 * at
                values = jnp.concatenate([for_rows[0][at], for_rows[1][at]], axis=0)
                relaxed[part * 16 : part * 16 + 16, group * LANES : (group + 1) * LANES] = values.astype(jnp.bfloat16)

    now = first
    for level in range(2):
        exchange(level)
        now_left, now_right = left_of(now), right_of(now, 6 * level)
        relax_out(2 * level)
        relax_out(2 * level + 1)
        def arrived(at):
            table_copies[3 * level + at].wait_recv()
            return table_in[3 * level + at]

        by_col = arrived(1)
        col_left, col_right = left_of(by_col), right_of(by_col, 6 * level + 2)
        by_row = arrived(0)
        here = pair(now, now_left, now_right, right_of(by_row, 6 * level + 1))
        here_left, here_right = left_of(here), right_of(here, 6 * level + 4)
        there = pair(by_col, col_left, col_right, right_of(arrived(2), 6 * level + 3))
        now = pair(here, here_left, here_right, right_of(there, 6 * level + 5))
        if level == 0:
            table[1] = now
    now = now * 0.0625
    for part in range(4):
        merged[0, 0, part * 8 : part * 8 + 8, :] = now[:, part * PORTALS : (part + 1) * PORTALS]

    for copy in ground_copies + table_copies:
        copy.wait_send()


def hand_out(relaxed_in, merged_in, relaxed, merged, sem):
    copies = [
        pltpu.make_async_copy(relaxed_in, relaxed, sem.at[0]),
        pltpu.make_async_copy(merged_in, merged, sem.at[1]),
    ]
    for copy in copies:
        copy.start()
    for copy in copies:
        copy.wait()


def body(heights, blocked, estimate, portal_index):
    in_hbm = pl.BlockSpec(memory_space=pltpu.HBM)
    in_vmem = pl.BlockSpec(memory_space=pltpu.VMEM)
    outs = (
        jax.ShapeDtypeStruct(estimate.shape, jnp.bfloat16),
        jax.ShapeDtypeStruct((1, 1, PORTALS, PORTALS), jnp.float32),
    )
    results = pl.pallas_call(
        kernel,
        out_shape=outs,
        in_specs=[in_hbm] * 4,
        out_specs=(in_vmem, in_vmem),
        scratch_shapes=[
            pltpu.VMEM((TILE, TILE), jnp.int32),
            pltpu.VMEM((TILE, TILE), jnp.int32),
            pltpu.VMEM((TILE, TILE * PORTALS), jnp.bfloat16),
            pltpu.VMEM((1, 1, PORTALS), jnp.int32),
            pltpu.SMEM((1, 1, PORTALS), jnp.int32),
            pltpu.VMEM((TILE, LANES), jnp.int32),
            pltpu.VMEM((2, STRIP, LANES), jnp.int32),
            pltpu.VMEM((8, STRIP, LANES), jnp.int32),
            pltpu.VMEM((2, TILE + 2 * STRIP, LANES), jnp.float32),
            pltpu.VMEM((EXT, LANES), jnp.float32),
            pltpu.VMEM((OWN, EXT, LANES), jnp.float32),
            pltpu.VMEM((2, 2, TILE, LANES), jnp.float32),
            pltpu.VMEM((2, 2, EXT, LANES), jnp.float32),
            pltpu.VMEM((GROUPS, STEP, 8, LANES), jnp.float32),
            pltpu.VMEM((GROUPS, STEP, 8, LANES), jnp.float32),
            pltpu.VMEM((PORTALS, LANES), jnp.float32),
            pltpu.VMEM((PORTALS, LANES), jnp.int32),
            pltpu.VMEM((2, 8, LANES), jnp.float32),
            pltpu.VMEM((6, 8, LANES), jnp.float32),
            pltpu.VMEM((12, PORTALS, LANES), jnp.float32),
            pltpu.SemaphoreType.DMA((7,)),
            pltpu.SemaphoreType.DMA((8,)),
            pltpu.SemaphoreType.DMA((8,)),
            pltpu.SemaphoreType.DMA((8,)),
            pltpu.SemaphoreType.DMA((8,)),
            pltpu.SemaphoreType.DMA((6,)),
            pltpu.SemaphoreType.DMA((6,)),
        ],
        compiler_params=pltpu.CompilerParams(
            collective_id=0, has_side_effects=True, vmem_limit_bytes=16 * 2**20
        ),
    )(*(pltpu.with_memory_space_constraint(x, pltpu.HBM) for x in (heights, blocked, estimate, portal_index)))
    return pl.pallas_call(
        hand_out,
        out_shape=tuple(pltpu.HBM(x.shape, x.dtype) for x in outs),
        in_specs=[in_vmem] * 2,
        out_specs=[in_hbm] * 2,
        scratch_shapes=[pltpu.SemaphoreType.DMA((2,))],
        compiler_params=pltpu.CompilerParams(vmem_limit_bytes=2**20),
    )(*(pltpu.with_memory_space_constraint(x, pltpu.VMEM) for x in results))


def solution(mesh):
    placed = (P("row", "col"), P("row", "col"), P("row", "col"), P("row", "col", None))
    return jax.shard_map(
        body,
        mesh=mesh,
        in_specs=placed,
        out_specs=(P("row", "col"), P("row", "col", None, None)),
        check_vma=False,
    )
```

```python
import functools

import jax
import jax.numpy as jnp
from jax import lax
from jax.experimental import pallas as pl
from jax.experimental.pallas import tpu as pltpu
from jax.sharding import PartitionSpec as P

TILE = 64
PORTALS = 32
SWEEPS = 8
HALO = 8
EXT = TILE + 2 * HALO
LANES = 128
BLOCKS = LANES // PORTALS
OWN = TILE // BLOCKS
GROUPS = EXT // BLOCKS
STEP = EXT // 8
STRIP = 16
FAR = 1000000.0


AROUND = ((-1, -1), (-1, 1), (1, -1), (1, 1), (-1, 0), (1, 0), (0, -1), (0, 1))


def lane_take(values, index):
    return jnp.take_along_axis(values, index, axis=1, mode="promise_in_bounds")


def kernel(
    heights_hbm, blocked_hbm, estimate_hbm, portal_hbm,
    relaxed, merged,
    heights, blocked, estimate, portal, portal_smem,
    ground, strips, ground_in, high, cost_rows,
    field, side_out, side_in, cost, dist, rows, shifts, table, table_in, right_rows,
    load_sem, ground_send, ground_recv, field_send, field_recv, table_send, table_recv,
):
    row_index, col_index = lax.axis_index("row"), lax.axis_index("col")
    row_count, col_count = lax.axis_size("row"), lax.axis_size("col")
    around = [
        (lax.rem(row_index + dr + row_count, row_count), lax.rem(col_index + dc + col_count, col_count))
        for dr, dc in AROUND
    ]

    def other(index, bit):
        return index + bit - 2 * bit * lax.rem(index // bit, 2)

    partners = []
    for level in range(2):
        bit = 1 << level
        partners.append(
            [
                (other(row_index, bit), col_index),
                (row_index, other(col_index, bit)),
                (other(row_index, bit), other(col_index, bit)),
            ]
        )

    barrier = pltpu.get_barrier_semaphore()
    met = around
    for device in met:
        pl.semaphore_signal(barrier, inc=1, device_id=device, device_id_type=pl.DeviceIdType.MESH)

    loads = [
        pltpu.make_async_copy(source, target, load_sem.at[at])
        for at, (source, target) in enumerate(
            (
                (heights_hbm, heights),
                (blocked_hbm, blocked),
                (portal_hbm, portal),
                (estimate_hbm.at[0:16], estimate.at[0:16]),
                (estimate_hbm.at[48:64], estimate.at[48:64]),
                (estimate_hbm.at[16:48], estimate.at[16:48]),
                (portal_hbm, portal_smem),
            )
        )
    ]
    for load in loads:
        load.start()

    def send(source, target, send_sem, recv_sem, device):
        copy = pltpu.make_async_remote_copy(
            src_ref=source, dst_ref=target, send_sem=send_sem, recv_sem=recv_sem,
            device_id=device, device_id_type=pl.DeviceIdType.MESH,
        )
        copy.start()
        return copy

    lane = lax.broadcasted_iota(jnp.int32, (8, LANES), 1)
    sublane = lax.broadcasted_iota(jnp.int32, (8, LANES), 0)
    lane_block = lane // PORTALS
    lane_class = lane % PORTALS

    loads[0].wait()
    loads[1].wait()
    ground[:, 0:TILE] = heights[...]
    ground[:, TILE : 2 * TILE] = blocked[...]
    wide = lax.broadcasted_iota(jnp.int32, (STRIP, LANES), 1)
    west = jnp.zeros((STRIP, LANES), jnp.int32)
    east = jnp.zeros((STRIP, LANES), jnp.int32)
    for part in range(4):
        here = ground[part * STRIP : (part + 1) * STRIP]
        base = part * 32
        in_height = (wide >= base) & (wide < base + 16)
        in_block = (wide >= base + 16) & (wide < base + 32)
        west = jnp.where(in_height, pltpu.roll(here, base % LANES, 1), west)
        west = jnp.where(in_block, pltpu.roll(here, (base + 16 - 64) % LANES, 1), west)
        east = jnp.where(in_height, pltpu.roll(here, (base - 48) % LANES, 1), east)
        east = jnp.where(in_block, pltpu.roll(here, (base + 16 - 112) % LANES, 1), east)
    strips[0] = west
    strips[1] = east

    loads[2].wait()
    own = jnp.broadcast_to(portal[0, 0:1, :], (8, PORTALS))
    portal_cells = jnp.concatenate([own] * BLOCKS, axis=1)
    loads[3].wait()
    loads[4].wait()
    loads[5].wait()
    low = lane < 2 * PORTALS
    even = lane_block % 2 == 0
    swapped_blocks = lane_class + (lane_block + 1 - 2 * (lane_block % 2)) * PORTALS

    def transposed(a):
        t = [None] * 4
        for at in range(2):
            turned = pltpu.roll(jnp.where(low, a[at + 2], a[at]), 2 * PORTALS, 1)
            t[at], t[at + 2] = jnp.where(low, a[at], turned), jnp.where(low, turned, a[at + 2])
        out = [None] * 4
        for at in (0, 2):
            turned = lane_take(jnp.where(even, t[at + 1], t[at]), swapped_blocks)
            out[at], out[at + 1] = jnp.where(even, t[at], turned), jnp.where(even, turned, t[at + 1])
        return out

    def estimates(part, group):
        values = estimate[part * 16 : (part + 1) * 16, group * LANES : (group + 1) * LANES]
        values = values.astype(jnp.float32)
        return values[0:8], values[8:16]

    def prepare(part):
        for first in range(4):
            halves = [estimates(part, first + 4 * at) for at in range(4)]
            for half in range(2):
                row = part * 16 + half * 8
                cell = (row + sublane) * TILE + lane_block * OWN
                for at, values in enumerate(transposed([pieces[half] for pieces in halves])):
                    group = 4 * first + at
                    field[group, HALO + row : HALO + row + 8, :] = jnp.where(
                        portal_cells == cell + group, 0.0, values
                    )

    def edges(part):
        columns = (0, 1, OWN - 2, OWN - 1)
        pieces = [estimates(part, group) for group in columns]
        for half in range(2):
            row = part * 16 + half * 8
            cell = (row + sublane) * TILE + lane_block
            w0, w1, e0, e1 = (
                jnp.where(portal_cells == cell + group * BLOCKS, 0.0, piece[half])
                for group, piece in zip(columns, pieces)
            )
            side_out[0, 0, row : row + 8, :] = jnp.where(even, w0, pltpu.roll(w1, 32, 1))
            side_out[0, 1, row : row + 8, :] = jnp.where(even, pltpu.roll(w0, 96, 1), w1)
            side_out[1, 0, row : row + 8, :] = jnp.where(even, pltpu.roll(e0, 64, 1), pltpu.roll(e1, 96, 1))
            side_out[1, 1, row : row + 8, :] = jnp.where(even, pltpu.roll(e0, 32, 1), pltpu.roll(e1, 64, 1))

    prepare(0)
    prepare(3)
    for part in range(4):
        edges(part)

    pl.semaphore_wait(barrier, len(met))

    top, bottom = ground.at[0:STRIP], ground.at[TILE - STRIP : TILE]
    ground_source = {-1: top, 1: bottom}
    ground_copies = []
    for at, (dr, dc) in enumerate(AROUND):
        if dr:
            source = ground_source[dr]
        else:
            source = strips.at[0 if dc < 0 else 1]
        slot = AROUND.index((-dr, -dc))
        ground_copies.append(
            send(source, ground_in.at[slot], ground_send.at[at], ground_recv.at[slot], around[at])
        )

    field_copies = []
    for at, (dr, dc) in enumerate(AROUND):
        row_from, row_to, row_len = {
            -1: (0, HALO + TILE, HALO), 0: (0, HALO, TILE), 1: (TILE - HALO, 0, HALO)
        }[dr]
        if dc:
            side = 0 if dc < 0 else 1
            source = side_out.at[side, :, pl.ds(row_from, row_len), :]
            target = side_in.at[side, :, pl.ds(row_to, row_len), :]
        else:
            source = field.at[:, pl.ds(HALO + row_from, row_len), :]
            target = field.at[:, pl.ds(row_to, row_len), :]
        slot = AROUND.index((-dr, -dc))
        field_copies.append(send(source, target, field_send.at[at], field_recv.at[slot], around[at]))

    prepare(1)
    prepare(2)

    for copy in ground_copies:
        copy.wait_recv()
    slots = {step: at for at, step in enumerate(AROUND)}

    def lay(row, west_height, middle, east_height, west_block, east_block):
        height = jnp.where(wide < 16, west_height, jnp.where(wide < 80, pltpu.roll(middle, 16, 1), east_height))
        block = jnp.where(wide < 16, west_block, jnp.where(wide < 80, pltpu.roll(middle, 80, 1), east_block))
        high[0, row : row + STRIP, :] = height.astype(jnp.float32)
        high[1, row : row + STRIP, :] = block.astype(jnp.float32)

    for dr, row in ((-1, 0), (1, STRIP + TILE)):
        west_in, middle, east_in = (ground_in[slots[(dr, dc)]] for dc in (-1, 0, 1))
        lay(
            row, pltpu.roll(west_in, 80, 1), middle, pltpu.roll(east_in, 80, 1),
            pltpu.roll(west_in, 16, 1), pltpu.roll(east_in, 16, 1),
        )
    west_in, east_in = ground_in[slots[(0, -1)]], ground_in[slots[(0, 1)]]
    for part in range(4):
        base = part * 32
        lay(
            STRIP + part * STRIP,
            pltpu.roll(west_in, (-base) % LANES, 1),
            ground[part * STRIP : (part + 1) * STRIP],
            pltpu.roll(east_in, (80 - base) % LANES, 1),
            pltpu.roll(west_in, (-base - 16) % LANES, 1),
            pltpu.roll(east_in, (64 - base) % LANES, 1),
        )

    @pl.when(row_index == 0)
    def _():
        high[0, STRIP - 1 : STRIP, :] = high[0, STRIP : STRIP + 1, :]

    @pl.when(row_index == row_count - 1)
    def _():
        high[0, STRIP + TILE : STRIP + TILE + 1, :] = high[0, STRIP + TILE - 1 : STRIP + TILE, :]

    shift = STRIP - HALO
    near = high[0, shift : shift + EXT, :]
    up = high[0, shift - 1 : shift - 1 + EXT, :]
    down = high[0, shift + 1 : shift + 1 + EXT, :]
    col = lax.broadcasted_iota(jnp.int32, (EXT, LANES), 1) - STRIP
    row = lax.broadcasted_iota(jnp.int32, (EXT, LANES), 0) - HALO
    grid_col = col_index * TILE + col
    grid_row = row_index * TILE + row
    before = jnp.where(grid_col == 0, near, pltpu.roll(near, 1, 1))
    after = jnp.where(grid_col == col_count * TILE - 1, near, pltpu.roll(near, LANES - 1, 1))
    grad_x = (after - before) * 0.01
    grad_y = (down - up) * 0.01
    grad_sq = grad_x * grad_x + grad_y * grad_y
    step_cost = (
        1.0 + 2.0 * grad_sq + 0.5 * grad_y / jnp.sqrt(1.0 + grad_sq)
        + 30.0 * high[1, shift : shift + EXT, :]
    )
    inside = (
        (grid_row >= 0) & (grid_row < row_count * TILE)
        & (grid_col >= 0) & (grid_col < col_count * TILE)
    )
    cost_rows[...] = jnp.where(inside, step_cost, 2.0 * FAR)
    first_column = STRIP + lane_block * OWN
    halo_shift = jnp.where(low, TILE + 4 * lane_block, 4 * lane_block - 16) - lane_block * OWN
    for at in range(STEP):
        values = cost_rows[pl.ds(at, 8, stride=STEP), :]
        for group in range(GROUPS):
            cost[group, at] = lane_take(values, first_column + (group if group < OWN else group - OWN + halo_shift))

    loads[6].wait()
    cells = [portal_smem[0, 0, at] for at in range(PORTALS)]
    for at, cell in enumerate(cells):
        shifts[at : at + 1, :] = jnp.full((1, LANES), ((cell >> 4) & (BLOCKS - 1)) * PORTALS, jnp.int32)

    for copy, (_, dc) in zip(field_copies, AROUND):
        if dc:
            copy.wait_recv()

    def started(group, at, distance):
        return jnp.minimum(distance + 0.5 * cost[group, at], FAR)

    for at in range(STEP):
        for piece in range(2):
            from_east = side_in[0, piece, pl.ds(at, 8, stride=STEP), :]
            from_west = side_in[1, piece, pl.ds(at, 8, stride=STEP), :]
            for group, values in (
                (OWN + piece, jnp.where(low, from_east, from_west)),
                (OWN + piece + 2, pltpu.roll(jnp.where(low, from_west, from_east), 64, 1)),
            ):
                dist[group, at] = started(group, at, values)

    for copy, (_, dc) in zip(field_copies, AROUND):
        if not dc:
            copy.wait_recv()

    first_block, last_block = lane_block == 0, lane_block == BLOCKS - 1

    def sweep(first, last):
        def pairs_of(here, east_of):
            below = east_of[1:] + [pltpu.roll(east_of[0], 7, 0)]
            return [jnp.minimum(a, b) for a, b in zip(here, below)]

        def column(group):
            if first and group < OWN:
                return [started(group, at, field[group, pl.ds(at, 8, stride=STEP), :]) for at in range(STEP)]
            return [dist[group, at] for at in range(STEP)]

        own_first, halo_first = column(0), column(OWN)
        own_pairs = pairs_of(
            column(OWN - 1),
            [pltpu.roll(jnp.where(first_block, a, b), LANES - PORTALS, 1) for a, b in zip(halo_first, own_first)],
        )
        halo_pairs = pairs_of(
            column(GROUPS - 1),
            [pltpu.roll(jnp.where(first_block, a, b), LANES - PORTALS, 1) for a, b in zip(own_first, halo_first)],
        )
        own_west = [pltpu.roll(jnp.where(last_block, a, b), PORTALS, 1) for a, b in zip(halo_pairs, own_pairs)]
        halo_west = [pltpu.roll(jnp.where(last_block, a, b), PORTALS, 1) for a, b in zip(own_pairs, halo_pairs)]
        for begin, end, west_of, end_pairs in ((0, OWN, own_west, own_pairs), (OWN, GROUPS, halo_west, halo_pairs)):
            if last and begin == OWN:
                continue
            now = own_first if begin == 0 else column(begin)
            for group in range(begin, end):
                if group < end - 1:
                    later = column(group + 1)
                    pairs = pairs_of(now, later)
                else:
                    pairs = end_pairs
                north = [pltpu.roll(pairs[STEP - 1], 1, 0)] + pairs[:-1]
                for at in range(STEP):
                    here = cost[group, at]
                    shortest = jnp.minimum(now[at], here + jnp.minimum(north[at], west_of[at]))
                    if last:
                        field[group, pl.ds(at, 8, stride=STEP), :] = shortest - 0.5 * here
                    else:
                        dist[group, at] = shortest
                west_of, now = pairs, later

    sweep(True, False)
    def middle(_, carry):
        sweep(False, False)
        return carry

    lax.fori_loop(0, SWEEPS - 2, middle, 0)
    for copy in field_copies:
        copy.wait_send()
    sweep(False, True)

    for at, cell in enumerate(cells):
        rows[at : at + 1, :] = field[cell & (OWN - 1), pl.ds(HALO + (cell >> 6), 1), :]
    first = jnp.zeros((8, LANES), jnp.float32)
    for part in range(4):
        index = shifts[part * 8 : part * 8 + 8, :] + lane_class
        first = jnp.where(lane_block == part, lane_take(rows[part * 8 : part * 8 + 8, :], index), first)
    table[0] = first

    table_copies = []

    def exchange(level):
        copies = [
            send(
                table.at[level], table_in.at[3 * level + at],
                table_send.at[3 * level + at], table_recv.at[3 * level + at], device,
            )
            for at, device in reversed(tuple(enumerate(partners[level])))
        ]
        table_copies.extend(reversed(copies))

    def left_of(values):
        return [lane_take(values, lane_block * PORTALS + at) for at in range(PORTALS)]

    def right_of(values, slot):
        for part in range(4):
            right_rows[slot, part * 8 : part * 8 + 8, :] = lane_take(values, lane_class + part * PORTALS)
        return [
            jnp.broadcast_to(right_rows[slot, at : at + 1, :], (8, LANES)) for at in range(PORTALS)
        ]

    def minplus(left, right):
        sums = [a + b for a, b in zip(left, right)]
        while len(sums) > 1:
            sums = [jnp.minimum(a, b) for a, b in zip(sums[::2], sums[1::2])]
        return sums[0]

    def pair(near_table, near_left, near_right, far_right):
        through = minplus(near_left, far_right)
        return jnp.minimum(near_table, minplus(left_of(through), near_right))

    def relax_out(part):
        for first_at in range(4):
            for_rows = [
                transposed(
                    [
                        field[4 * first_at + at, HALO + part * 16 + half * 8 : HALO + part * 16 + half * 8 + 8, :]
                        for at in range(4)
                    ]
                )
                for half in range(2)
            ]
            for at in range(4):
                group = first_at + 4 * at
                values = jnp.concatenate([for_rows[0][at], for_rows[1][at]], axis=0)
                relaxed[part * 16 : part * 16 + 16, group * LANES : (group + 1) * LANES] = values.astype(jnp.bfloat16)

    now = first
    for level in range(2):
        exchange(level)
        now_left, now_right = left_of(now), right_of(now, 6 * level)
        relax_out(2 * level)
        relax_out(2 * level + 1)
        def arrived(at):
            table_copies[3 * level + at].wait_recv()
            return table_in[3 * level + at]

        by_col = arrived(1)
        col_left, col_right = left_of(by_col), right_of(by_col, 6 * level + 2)
        if level == 0:
            there = pair(by_col, col_left, col_right, right_of(arrived(2), 6 * level + 3))
            there_right = right_of(there, 6 * level + 5)
        by_row = arrived(0)
        here = pair(now, now_left, now_right, right_of(by_row, 6 * level + 1))
        here_left, here_right = left_of(here), right_of(here, 6 * level + 4)
        if level == 1:
            there = pair(by_col, col_left, col_right, right_of(arrived(2), 6 * level + 3))
            there_right = right_of(there, 6 * level + 5)
        now = pair(here, here_left, here_right, there_right)
        if level == 0:
            table[1] = now
    now = now * 0.0625
    for part in range(4):
        merged[0, 0, part * 8 : part * 8 + 8, :] = now[:, part * PORTALS : (part + 1) * PORTALS]

    for copy in ground_copies + table_copies:
        copy.wait_send()


def hand_out(relaxed_in, merged_in, relaxed, merged, sem):
    copies = [
        pltpu.make_async_copy(relaxed_in, relaxed, sem.at[0]),
        pltpu.make_async_copy(merged_in, merged, sem.at[1]),
    ]
    for copy in copies:
        copy.start()
    for copy in copies:
        copy.wait()


def body(heights, blocked, estimate, portal_index):
    in_hbm = pl.BlockSpec(memory_space=pltpu.HBM)
    in_vmem = pl.BlockSpec(memory_space=pltpu.VMEM)
    outs = (
        jax.ShapeDtypeStruct(estimate.shape, jnp.bfloat16),
        jax.ShapeDtypeStruct((1, 1, PORTALS, PORTALS), jnp.float32),
    )
    results = pl.pallas_call(
        kernel,
        out_shape=outs,
        in_specs=[in_hbm] * 4,
        out_specs=(in_vmem, in_vmem),
        scratch_shapes=[
            pltpu.VMEM((TILE, TILE), jnp.int32),
            pltpu.VMEM((TILE, TILE), jnp.int32),
            pltpu.VMEM((TILE, TILE * PORTALS), jnp.bfloat16),
            pltpu.VMEM((1, 1, PORTALS), jnp.int32),
            pltpu.SMEM((1, 1, PORTALS), jnp.int32),
            pltpu.VMEM((TILE, LANES), jnp.int32),
            pltpu.VMEM((2, STRIP, LANES), jnp.int32),
            pltpu.VMEM((8, STRIP, LANES), jnp.int32),
            pltpu.VMEM((2, TILE + 2 * STRIP, LANES), jnp.float32),
            pltpu.VMEM((EXT, LANES), jnp.float32),
            pltpu.VMEM((OWN, EXT, LANES), jnp.float32),
            pltpu.VMEM((2, 2, TILE, LANES), jnp.float32),
            pltpu.VMEM((2, 2, EXT, LANES), jnp.float32),
            pltpu.VMEM((GROUPS, STEP, 8, LANES), jnp.float32),
            pltpu.VMEM((GROUPS, STEP, 8, LANES), jnp.float32),
            pltpu.VMEM((PORTALS, LANES), jnp.float32),
            pltpu.VMEM((PORTALS, LANES), jnp.int32),
            pltpu.VMEM((2, 8, LANES), jnp.float32),
            pltpu.VMEM((6, 8, LANES), jnp.float32),
            pltpu.VMEM((12, PORTALS, LANES), jnp.float32),
            pltpu.SemaphoreType.DMA((7,)),
            pltpu.SemaphoreType.DMA((8,)),
            pltpu.SemaphoreType.DMA((8,)),
            pltpu.SemaphoreType.DMA((8,)),
            pltpu.SemaphoreType.DMA((8,)),
            pltpu.SemaphoreType.DMA((6,)),
            pltpu.SemaphoreType.DMA((6,)),
        ],
        compiler_params=pltpu.CompilerParams(
            collective_id=0, has_side_effects=True, vmem_limit_bytes=16 * 2**20
        ),
    )(*(pltpu.with_memory_space_constraint(x, pltpu.HBM) for x in (heights, blocked, estimate, portal_index)))
    return pl.pallas_call(
        hand_out,
        out_shape=tuple(pltpu.HBM(x.shape, x.dtype) for x in outs),
        in_specs=[in_vmem] * 2,
        out_specs=[in_hbm] * 2,
        scratch_shapes=[pltpu.SemaphoreType.DMA((2,))],
        compiler_params=pltpu.CompilerParams(vmem_limit_bytes=2**20),
    )(*(pltpu.with_memory_space_constraint(x, pltpu.VMEM) for x in results))


def solution(mesh):
    placed = (P("row", "col"), P("row", "col"), P("row", "col"), P("row", "col", None))
    return jax.shard_map(
        body,
        mesh=mesh,
        in_specs=placed,
        out_specs=(P("row", "col"), P("row", "col", None, None)),
        check_vma=False,
    )
```

```python
import functools

import jax
import jax.numpy as jnp
from jax import lax
from jax.experimental import pallas as pl
from jax.experimental.pallas import tpu as pltpu
from jax.sharding import PartitionSpec as P

TILE = 64
PORTALS = 32
SWEEPS = 8
HALO = 8
EXT = TILE + 2 * HALO
LANES = 128
BLOCKS = LANES // PORTALS
OWN = TILE // BLOCKS
GROUPS = EXT // BLOCKS
STEP = EXT // 8
STRIP = 16
FAR = 1000000.0


AROUND = ((-1, -1), (-1, 1), (1, -1), (1, 1), (-1, 0), (1, 0), (0, -1), (0, 1))


def lane_take(values, index):
    return jnp.take_along_axis(values, index, axis=1, mode="promise_in_bounds")


def kernel(
    heights_hbm, blocked_hbm, estimate_hbm, portal_hbm,
    relaxed, merged,
    heights, blocked, estimate, portal, portal_smem,
    ground, strips, ground_in, high, cost_rows,
    field, side_out, side_in, cost, dist, rows, shifts, table, table_in, right_rows,
    load_sem, ground_send, ground_recv, field_send, field_recv, table_send, table_recv,
):
    row_index, col_index = lax.axis_index("row"), lax.axis_index("col")
    row_count, col_count = lax.axis_size("row"), lax.axis_size("col")
    around = [
        (lax.rem(row_index + dr + row_count, row_count), lax.rem(col_index + dc + col_count, col_count))
        for dr, dc in AROUND
    ]

    def other(index, bit):
        return index + bit - 2 * bit * lax.rem(index // bit, 2)

    partners = []
    for level in range(2):
        bit = 1 << level
        partners.append(
            [
                (other(row_index, bit), col_index),
                (row_index, other(col_index, bit)),
                (other(row_index, bit), other(col_index, bit)),
            ]
        )

    barrier = pltpu.get_barrier_semaphore()
    met = around
    for device in met:
        pl.semaphore_signal(barrier, inc=1, device_id=device, device_id_type=pl.DeviceIdType.MESH)

    loads = [
        pltpu.make_async_copy(source, target, load_sem.at[at])
        for at, (source, target) in enumerate(
            (
                (heights_hbm, heights),
                (blocked_hbm, blocked),
                (portal_hbm, portal),
                (estimate_hbm.at[0:16], estimate.at[0:16]),
                (estimate_hbm.at[48:64], estimate.at[48:64]),
                (estimate_hbm.at[16:48], estimate.at[16:48]),
                (portal_hbm, portal_smem),
            )
        )
    ]
    for load in loads:
        load.start()

    def send(source, target, send_sem, recv_sem, device):
        copy = pltpu.make_async_remote_copy(
            src_ref=source, dst_ref=target, send_sem=send_sem, recv_sem=recv_sem,
            device_id=device, device_id_type=pl.DeviceIdType.MESH,
        )
        copy.start()
        return copy

    lane = lax.broadcasted_iota(jnp.int32, (8, LANES), 1)
    sublane = lax.broadcasted_iota(jnp.int32, (8, LANES), 0)
    lane_block = lane // PORTALS
    lane_class = lane % PORTALS

    loads[0].wait()
    loads[1].wait()
    ground[:, 0:TILE] = heights[...]
    ground[:, TILE : 2 * TILE] = blocked[...]
    wide = lax.broadcasted_iota(jnp.int32, (STRIP, LANES), 1)
    west = jnp.zeros((STRIP, LANES), jnp.int32)
    east = jnp.zeros((STRIP, LANES), jnp.int32)
    for part in range(4):
        here = ground[part * STRIP : (part + 1) * STRIP]
        base = part * 32
        in_height = (wide >= base) & (wide < base + 16)
        in_block = (wide >= base + 16) & (wide < base + 32)
        west = jnp.where(in_height, pltpu.roll(here, base % LANES, 1), west)
        west = jnp.where(in_block, pltpu.roll(here, (base + 16 - 64) % LANES, 1), west)
        east = jnp.where(in_height, pltpu.roll(here, (base - 48) % LANES, 1), east)
        east = jnp.where(in_block, pltpu.roll(here, (base + 16 - 112) % LANES, 1), east)
    strips[0] = west
    strips[1] = east

    loads[2].wait()
    own = jnp.broadcast_to(portal[0, 0:1, :], (8, PORTALS))
    portal_cells = jnp.concatenate([own] * BLOCKS, axis=1)
    loads[3].wait()
    loads[4].wait()
    loads[5].wait()
    low = lane < 2 * PORTALS
    even = lane_block % 2 == 0
    swapped_blocks = lane_class + (lane_block + 1 - 2 * (lane_block % 2)) * PORTALS

    def transposed(a):
        t = [None] * 4
        for at in range(2):
            turned = pltpu.roll(jnp.where(low, a[at + 2], a[at]), 2 * PORTALS, 1)
            t[at], t[at + 2] = jnp.where(low, a[at], turned), jnp.where(low, turned, a[at + 2])
        out = [None] * 4
        for at in (0, 2):
            turned = lane_take(jnp.where(even, t[at + 1], t[at]), swapped_blocks)
            out[at], out[at + 1] = jnp.where(even, t[at], turned), jnp.where(even, turned, t[at + 1])
        return out

    def estimates(part, group):
        values = estimate[part * 16 : (part + 1) * 16, group * LANES : (group + 1) * LANES]
        values = values.astype(jnp.float32)
        return values[0:8], values[8:16]

    def prepare(part):
        for first in range(4):
            halves = [estimates(part, first + 4 * at) for at in range(4)]
            for half in range(2):
                row = part * 16 + half * 8
                cell = (row + sublane) * TILE + lane_block * OWN
                for at, values in enumerate(transposed([pieces[half] for pieces in halves])):
                    group = 4 * first + at
                    field[group, HALO + row : HALO + row + 8, :] = jnp.where(
                        portal_cells == cell + group, 0.0, values
                    )

    def edges(part):
        columns = (0, 1, OWN - 2, OWN - 1)
        pieces = [estimates(part, group) for group in columns]
        for half in range(2):
            row = part * 16 + half * 8
            cell = (row + sublane) * TILE + lane_block
            w0, w1, e0, e1 = (
                jnp.where(portal_cells == cell + group * BLOCKS, 0.0, piece[half])
                for group, piece in zip(columns, pieces)
            )
            side_out[0, 0, row : row + 8, :] = jnp.where(even, w0, pltpu.roll(w1, 32, 1))
            side_out[0, 1, row : row + 8, :] = jnp.where(even, pltpu.roll(w0, 96, 1), w1)
            side_out[1, 0, row : row + 8, :] = jnp.where(even, pltpu.roll(e0, 64, 1), pltpu.roll(e1, 96, 1))
            side_out[1, 1, row : row + 8, :] = jnp.where(even, pltpu.roll(e0, 32, 1), pltpu.roll(e1, 64, 1))

    prepare(0)
    prepare(3)
    for part in range(4):
        edges(part)

    pl.semaphore_wait(barrier, len(met))

    top, bottom = ground.at[0:STRIP], ground.at[TILE - STRIP : TILE]
    ground_source = {-1: top, 1: bottom}
    ground_copies = []
    for at, (dr, dc) in enumerate(AROUND):
        if dr:
            source = ground_source[dr]
        else:
            source = strips.at[0 if dc < 0 else 1]
        slot = AROUND.index((-dr, -dc))
        ground_copies.append(
            send(source, ground_in.at[slot], ground_send.at[at], ground_recv.at[slot], around[at])
        )

    field_copies = []
    for at, (dr, dc) in enumerate(AROUND):
        row_from, row_to, row_len = {
            -1: (0, HALO + TILE, HALO), 0: (0, HALO, TILE), 1: (TILE - HALO, 0, HALO)
        }[dr]
        if dc:
            side = 0 if dc < 0 else 1
            source = side_out.at[side, :, pl.ds(row_from, row_len), :]
            target = side_in.at[side, :, pl.ds(row_to, row_len), :]
        else:
            source = field.at[:, pl.ds(HALO + row_from, row_len), :]
            target = field.at[:, pl.ds(row_to, row_len), :]
        slot = AROUND.index((-dr, -dc))
        field_copies.append(send(source, target, field_send.at[at], field_recv.at[slot], around[at]))

    prepare(1)
    prepare(2)

    for copy in ground_copies:
        copy.wait_recv()
    slots = {step: at for at, step in enumerate(AROUND)}

    def lay(row, west_height, middle, east_height, west_block, east_block):
        height = jnp.where(wide < 16, west_height, jnp.where(wide < 80, pltpu.roll(middle, 16, 1), east_height))
        block = jnp.where(wide < 16, west_block, jnp.where(wide < 80, pltpu.roll(middle, 80, 1), east_block))
        high[0, row : row + STRIP, :] = height.astype(jnp.float32)
        high[1, row : row + STRIP, :] = block.astype(jnp.float32)

    for dr, row in ((-1, 0), (1, STRIP + TILE)):
        west_in, middle, east_in = (ground_in[slots[(dr, dc)]] for dc in (-1, 0, 1))
        lay(
            row, pltpu.roll(west_in, 80, 1), middle, pltpu.roll(east_in, 80, 1),
            pltpu.roll(west_in, 16, 1), pltpu.roll(east_in, 16, 1),
        )
    west_in, east_in = ground_in[slots[(0, -1)]], ground_in[slots[(0, 1)]]
    for part in range(4):
        base = part * 32
        lay(
            STRIP + part * STRIP,
            pltpu.roll(west_in, (-base) % LANES, 1),
            ground[part * STRIP : (part + 1) * STRIP],
            pltpu.roll(east_in, (80 - base) % LANES, 1),
            pltpu.roll(west_in, (-base - 16) % LANES, 1),
            pltpu.roll(east_in, (64 - base) % LANES, 1),
        )

    @pl.when(row_index == 0)
    def _():
        high[0, STRIP - 1 : STRIP, :] = high[0, STRIP : STRIP + 1, :]

    @pl.when(row_index == row_count - 1)
    def _():
        high[0, STRIP + TILE : STRIP + TILE + 1, :] = high[0, STRIP + TILE - 1 : STRIP + TILE, :]

    shift = STRIP - HALO
    near = high[0, shift : shift + EXT, :]
    up = high[0, shift - 1 : shift - 1 + EXT, :]
    down = high[0, shift + 1 : shift + 1 + EXT, :]
    col = lax.broadcasted_iota(jnp.int32, (EXT, LANES), 1) - STRIP
    row = lax.broadcasted_iota(jnp.int32, (EXT, LANES), 0) - HALO
    grid_col = col_index * TILE + col
    grid_row = row_index * TILE + row
    before = jnp.where(grid_col == 0, near, pltpu.roll(near, 1, 1))
    after = jnp.where(grid_col == col_count * TILE - 1, near, pltpu.roll(near, LANES - 1, 1))
    grad_x = (after - before) * 0.01
    grad_y = (down - up) * 0.01
    grad_sq = grad_x * grad_x + grad_y * grad_y
    step_cost = (
        1.0 + 2.0 * grad_sq + 0.5 * grad_y / jnp.sqrt(1.0 + grad_sq)
        + 30.0 * high[1, shift : shift + EXT, :]
    )
    inside = (
        (grid_row >= 0) & (grid_row < row_count * TILE)
        & (grid_col >= 0) & (grid_col < col_count * TILE)
    )
    cost_rows[...] = jnp.where(inside, step_cost, 2.0 * FAR)
    first_column = STRIP + lane_block * OWN
    halo_shift = jnp.where(low, TILE + 4 * lane_block, 4 * lane_block - 16) - lane_block * OWN
    for at in range(STEP):
        values = cost_rows[pl.ds(at, 8, stride=STEP), :]
        for group in range(GROUPS):
            cost[group, at] = lane_take(values, first_column + (group if group < OWN else group - OWN + halo_shift))

    loads[6].wait()
    cells = [portal_smem[0, 0, at] for at in range(PORTALS)]
    for at, cell in enumerate(cells):
        shifts[at : at + 1, :] = jnp.full((1, LANES), ((cell >> 4) & (BLOCKS - 1)) * PORTALS, jnp.int32)

    for copy, (_, dc) in zip(field_copies, AROUND):
        if dc:
            copy.wait_recv()

    def started(group, at, distance):
        return jnp.minimum(distance + 0.5 * cost[group, at], FAR)

    for at in range(STEP):
        for piece in range(2):
            from_east = side_in[0, piece, pl.ds(at, 8, stride=STEP), :]
            from_west = side_in[1, piece, pl.ds(at, 8, stride=STEP), :]
            for group, values in (
                (OWN + piece, jnp.where(low, from_east, from_west)),
                (OWN + piece + 2, pltpu.roll(jnp.where(low, from_west, from_east), 64, 1)),
            ):
                dist[group, at] = started(group, at, values)

    for copy, (_, dc) in zip(field_copies, AROUND):
        if not dc:
            copy.wait_recv()

    first_block, last_block = lane_block == 0, lane_block == BLOCKS - 1

    def sweep(first, last):
        def pairs_of(here, east_of):
            below = east_of[1:] + [pltpu.roll(east_of[0], 7, 0)]
            return [jnp.minimum(a, b) for a, b in zip(here, below)]

        def column(group):
            if first and group < OWN:
                return [started(group, at, field[group, pl.ds(at, 8, stride=STEP), :]) for at in range(STEP)]
            return [dist[group, at] for at in range(STEP)]

        own_first, halo_first = column(0), column(OWN)
        own_pairs = pairs_of(
            column(OWN - 1),
            [pltpu.roll(jnp.where(first_block, a, b), LANES - PORTALS, 1) for a, b in zip(halo_first, own_first)],
        )
        halo_pairs = pairs_of(
            column(GROUPS - 1),
            [pltpu.roll(jnp.where(first_block, a, b), LANES - PORTALS, 1) for a, b in zip(own_first, halo_first)],
        )
        own_west = [pltpu.roll(jnp.where(last_block, a, b), PORTALS, 1) for a, b in zip(halo_pairs, own_pairs)]
        halo_west = [pltpu.roll(jnp.where(last_block, a, b), PORTALS, 1) for a, b in zip(own_pairs, halo_pairs)]
        for begin, end, west_of, end_pairs in ((0, OWN, own_west, own_pairs), (OWN, GROUPS, halo_west, halo_pairs)):
            if last and begin == OWN:
                continue
            now = own_first if begin == 0 else column(begin)
            for group in range(begin, end):
                if group < end - 1:
                    later = column(group + 1)
                    pairs = pairs_of(now, later)
                else:
                    pairs = end_pairs
                north = [pltpu.roll(pairs[STEP - 1], 1, 0)] + pairs[:-1]
                for at in range(STEP):
                    here = cost[group, at]
                    shortest = jnp.minimum(now[at], here + jnp.minimum(north[at], west_of[at]))
                    if last:
                        field[group, pl.ds(at, 8, stride=STEP), :] = shortest - 0.5 * here
                    else:
                        dist[group, at] = shortest
                west_of, now = pairs, later

    sweep(True, False)
    def middle(_, carry):
        sweep(False, False)
        return carry

    lax.fori_loop(0, SWEEPS - 2, middle, 0)
    for copy in field_copies:
        copy.wait_send()
    sweep(False, True)

    for at, cell in enumerate(cells):
        rows[at : at + 1, :] = field[cell & (OWN - 1), pl.ds(HALO + (cell >> 6), 1), :]
    first = jnp.zeros((8, LANES), jnp.float32)
    for part in range(4):
        index = shifts[part * 8 : part * 8 + 8, :] + lane_class
        first = jnp.where(lane_block == part, lane_take(rows[part * 8 : part * 8 + 8, :], index), first)
    table[0] = first

    table_copies = []

    def exchange(level):
        copies = [
            send(
                table.at[level], table_in.at[3 * level + at],
                table_send.at[3 * level + at], table_recv.at[3 * level + at], device,
            )
            for at, device in reversed(tuple(enumerate(partners[level])))
        ]
        table_copies.extend(reversed(copies))

    def left_of(values):
        return [lane_take(values, lane_block * PORTALS + at) for at in range(PORTALS)]

    def right_of(values, slot):
        for part in range(4):
            right_rows[slot, part * 8 : part * 8 + 8, :] = lane_take(values, lane_class + part * PORTALS)
        return [
            jnp.broadcast_to(right_rows[slot, at : at + 1, :], (8, LANES)) for at in range(PORTALS)
        ]

    def minplus(left, right):
        sums = [a + b for a, b in zip(left, right)]
        while len(sums) > 1:
            sums = [jnp.minimum(a, b) for a, b in zip(sums[::2], sums[1::2])]
        return sums[0]

    def pair(near_table, near_left, near_right, far_right):
        through = minplus(near_left, far_right)
        return jnp.minimum(near_table, minplus(left_of(through), near_right))

    def relax_out(part):
        for first_at in range(4):
            for_rows = [
                transposed(
                    [
                        field[4 * first_at + at, HALO + part * 16 + half * 8 : HALO + part * 16 + half * 8 + 8, :]
                        for at in range(4)
                    ]
                )
                for half in range(2)
            ]
            for at in range(4):
                group = first_at + 4 * at
                values = jnp.concatenate([for_rows[0][at], for_rows[1][at]], axis=0)
                relaxed[part * 16 : part * 16 + 16, group * LANES : (group + 1) * LANES] = values.astype(jnp.bfloat16)

    now = first
    for level in range(2):
        exchange(level)
        if level == 0:
            for copy in ground_copies:
                copy.wait_send()
        now_left, now_right = left_of(now), right_of(now, 6 * level)
        relax_out(2 * level)
        relax_out(2 * level + 1)
        def arrived(at):
            table_copies[3 * level + at].wait_recv()
            return table_in[3 * level + at]

        by_col = arrived(1)
        col_left, col_right = left_of(by_col), right_of(by_col, 6 * level + 2)
        if level == 0:
            there = pair(by_col, col_left, col_right, right_of(arrived(2), 6 * level + 3))
            there_left = left_of(there)
            here = pair(now, now_left, now_right, right_of(arrived(0), 6 * level + 1))
            around_here = minplus(there_left, right_of(here, 6 * level + 4))
            now = jnp.minimum(here, minplus(left_of(here), right_of(around_here, 6 * level + 5)))
        else:
            here = pair(now, now_left, now_right, right_of(arrived(0), 6 * level + 1))
            here_left, here_right = left_of(here), right_of(here, 6 * level + 4)
            there = pair(by_col, col_left, col_right, right_of(arrived(2), 6 * level + 3))
            now = pair(here, here_left, here_right, right_of(there, 6 * level + 5))
        if level == 0:
            table[1] = now
    now = now * 0.0625
    for part in range(4):
        merged[0, 0, part * 8 : part * 8 + 8, :] = now[:, part * PORTALS : (part + 1) * PORTALS]

    for copy in table_copies:
        copy.wait_send()


def hand_out(relaxed_in, merged_in, relaxed, merged, sem):
    copies = [
        pltpu.make_async_copy(relaxed_in, relaxed, sem.at[0]),
        pltpu.make_async_copy(merged_in, merged, sem.at[1]),
    ]
    for copy in copies:
        copy.start()
    for copy in copies:
        copy.wait()


def body(heights, blocked, estimate, portal_index):
    in_hbm = pl.BlockSpec(memory_space=pltpu.HBM)
    in_vmem = pl.BlockSpec(memory_space=pltpu.VMEM)
    outs = (
        jax.ShapeDtypeStruct(estimate.shape, jnp.bfloat16),
        jax.ShapeDtypeStruct((1, 1, PORTALS, PORTALS), jnp.float32),
    )
    results = pl.pallas_call(
        kernel,
        out_shape=outs,
        in_specs=[in_hbm] * 4,
        out_specs=(in_vmem, in_vmem),
        scratch_shapes=[
            pltpu.VMEM((TILE, TILE), jnp.int32),
            pltpu.VMEM((TILE, TILE), jnp.int32),
            pltpu.VMEM((TILE, TILE * PORTALS), jnp.bfloat16),
            pltpu.VMEM((1, 1, PORTALS), jnp.int32),
            pltpu.SMEM((1, 1, PORTALS), jnp.int32),
            pltpu.VMEM((TILE, LANES), jnp.int32),
            pltpu.VMEM((2, STRIP, LANES), jnp.int32),
            pltpu.VMEM((8, STRIP, LANES), jnp.int32),
            pltpu.VMEM((2, TILE + 2 * STRIP, LANES), jnp.float32),
            pltpu.VMEM((EXT, LANES), jnp.float32),
            pltpu.VMEM((OWN, EXT, LANES), jnp.float32),
            pltpu.VMEM((2, 2, TILE, LANES), jnp.float32),
            pltpu.VMEM((2, 2, EXT, LANES), jnp.float32),
            pltpu.VMEM((GROUPS, STEP, 8, LANES), jnp.float32),
            pltpu.VMEM((GROUPS, STEP, 8, LANES), jnp.float32),
            pltpu.VMEM((PORTALS, LANES), jnp.float32),
            pltpu.VMEM((PORTALS, LANES), jnp.int32),
            pltpu.VMEM((2, 8, LANES), jnp.float32),
            pltpu.VMEM((6, 8, LANES), jnp.float32),
            pltpu.VMEM((12, PORTALS, LANES), jnp.float32),
            pltpu.SemaphoreType.DMA((7,)),
            pltpu.SemaphoreType.DMA((8,)),
            pltpu.SemaphoreType.DMA((8,)),
            pltpu.SemaphoreType.DMA((8,)),
            pltpu.SemaphoreType.DMA((8,)),
            pltpu.SemaphoreType.DMA((6,)),
            pltpu.SemaphoreType.DMA((6,)),
        ],
        compiler_params=pltpu.CompilerParams(
            collective_id=0, has_side_effects=True, vmem_limit_bytes=16 * 2**20
        ),
    )(*(pltpu.with_memory_space_constraint(x, pltpu.HBM) for x in (heights, blocked, estimate, portal_index)))
    return pl.pallas_call(
        hand_out,
        out_shape=tuple(pltpu.HBM(x.shape, x.dtype) for x in outs),
        in_specs=[in_vmem] * 2,
        out_specs=[in_hbm] * 2,
        scratch_shapes=[pltpu.SemaphoreType.DMA((2,))],
        compiler_params=pltpu.CompilerParams(vmem_limit_bytes=2**20),
    )(*(pltpu.with_memory_space_constraint(x, pltpu.VMEM) for x in results))


def solution(mesh):
    placed = (P("row", "col"), P("row", "col"), P("row", "col"), P("row", "col", None))
    return jax.shard_map(
        body,
        mesh=mesh,
        in_specs=placed,
        out_specs=(P("row", "col"), P("row", "col", None, None)),
        check_vma=False,
    )
```

```python
import functools

import jax
import jax.numpy as jnp
from jax import lax
from jax.experimental import pallas as pl
from jax.experimental.pallas import tpu as pltpu
from jax.sharding import PartitionSpec as P

TILE = 64
PORTALS = 32
SWEEPS = 8
HALO = 8
EXT = TILE + 2 * HALO
LANES = 128
BLOCKS = LANES // PORTALS
OWN = TILE // BLOCKS
GROUPS = EXT // BLOCKS
STEP = EXT // 8
STRIP = 16
FAR = 1000000.0


AROUND = ((-1, -1), (-1, 1), (1, -1), (1, 1), (-1, 0), (1, 0), (0, -1), (0, 1))


def lane_take(values, index):
    return jnp.take_along_axis(values, index, axis=1, mode="promise_in_bounds")


def kernel(
    heights_hbm, blocked_hbm, estimate_hbm, portal_hbm,
    relaxed, merged,
    heights, blocked, estimate, portal, portal_smem,
    ground, strips, ground_in, high, cost_rows,
    field, side_out, side_in, cost, dist, rows, shifts, table, table_in, right_rows,
    load_sem, ground_send, ground_recv, field_send, field_recv, table_send, table_recv,
):
    row_index, col_index = lax.axis_index("row"), lax.axis_index("col")
    row_count, col_count = lax.axis_size("row"), lax.axis_size("col")
    around = [
        (lax.rem(row_index + dr + row_count, row_count), lax.rem(col_index + dc + col_count, col_count))
        for dr, dc in AROUND
    ]

    def other(index, bit):
        return index + bit - 2 * bit * lax.rem(index // bit, 2)

    partners = []
    for level in range(2):
        bit = 1 << level
        partners.append(
            [
                (other(row_index, bit), col_index),
                (row_index, other(col_index, bit)),
                (other(row_index, bit), other(col_index, bit)),
            ]
        )

    barrier = pltpu.get_barrier_semaphore()
    met = around
    for device in met:
        pl.semaphore_signal(barrier, inc=1, device_id=device, device_id_type=pl.DeviceIdType.MESH)

    loads = [
        pltpu.make_async_copy(source, target, load_sem.at[at])
        for at, (source, target) in enumerate(
            (
                (heights_hbm, heights),
                (blocked_hbm, blocked),
                (portal_hbm, portal),
                (estimate_hbm.at[0:16], estimate.at[0:16]),
                (estimate_hbm.at[48:64], estimate.at[48:64]),
                (estimate_hbm.at[16:48], estimate.at[16:48]),
                (portal_hbm, portal_smem),
            )
        )
    ]
    for load in loads:
        load.start()

    def send(source, target, send_sem, recv_sem, device):
        copy = pltpu.make_async_remote_copy(
            src_ref=source, dst_ref=target, send_sem=send_sem, recv_sem=recv_sem,
            device_id=device, device_id_type=pl.DeviceIdType.MESH,
        )
        copy.start()
        return copy

    lane = lax.broadcasted_iota(jnp.int32, (8, LANES), 1)
    sublane = lax.broadcasted_iota(jnp.int32, (8, LANES), 0)
    lane_block = lane // PORTALS
    lane_class = lane % PORTALS

    loads[0].wait()
    loads[1].wait()
    ground[:, 0:TILE] = heights[...]
    ground[:, TILE : 2 * TILE] = blocked[...]
    wide = lax.broadcasted_iota(jnp.int32, (STRIP, LANES), 1)
    west = jnp.zeros((STRIP, LANES), jnp.int32)
    east = jnp.zeros((STRIP, LANES), jnp.int32)
    for part in range(4):
        here = ground[part * STRIP : (part + 1) * STRIP]
        base = part * 32
        in_height = (wide >= base) & (wide < base + 16)
        in_block = (wide >= base + 16) & (wide < base + 32)
        west = jnp.where(in_height, pltpu.roll(here, base % LANES, 1), west)
        west = jnp.where(in_block, pltpu.roll(here, (base + 16 - 64) % LANES, 1), west)
        east = jnp.where(in_height, pltpu.roll(here, (base - 48) % LANES, 1), east)
        east = jnp.where(in_block, pltpu.roll(here, (base + 16 - 112) % LANES, 1), east)
    strips[0] = west
    strips[1] = east

    loads[2].wait()
    own = jnp.broadcast_to(portal[0, 0:1, :], (8, PORTALS))
    portal_cells = jnp.concatenate([own] * BLOCKS, axis=1)
    loads[3].wait()
    loads[4].wait()
    loads[5].wait()
    low = lane < 2 * PORTALS
    even = lane_block % 2 == 0
    swapped_blocks = lane_class + (lane_block + 1 - 2 * (lane_block % 2)) * PORTALS

    def transposed(a):
        t = [None] * 4
        for at in range(2):
            turned = pltpu.roll(jnp.where(low, a[at + 2], a[at]), 2 * PORTALS, 1)
            t[at], t[at + 2] = jnp.where(low, a[at], turned), jnp.where(low, turned, a[at + 2])
        out = [None] * 4
        for at in (0, 2):
            turned = lane_take(jnp.where(even, t[at + 1], t[at]), swapped_blocks)
            out[at], out[at + 1] = jnp.where(even, t[at], turned), jnp.where(even, turned, t[at + 1])
        return out

    def estimates(part, group):
        values = estimate[part * 16 : (part + 1) * 16, group * LANES : (group + 1) * LANES]
        values = values.astype(jnp.float32)
        return values[0:8], values[8:16]

    def prepare(part):
        for first in range(4):
            halves = [estimates(part, first + 4 * at) for at in range(4)]
            for half in range(2):
                row = part * 16 + half * 8
                cell = (row + sublane) * TILE + lane_block * OWN
                for at, values in enumerate(transposed([pieces[half] for pieces in halves])):
                    group = 4 * first + at
                    field[group, HALO + row : HALO + row + 8, :] = jnp.where(
                        portal_cells == cell + group, 0.0, values
                    )

    def edges(part):
        columns = (0, 1, OWN - 2, OWN - 1)
        pieces = [estimates(part, group) for group in columns]
        for half in range(2):
            row = part * 16 + half * 8
            cell = (row + sublane) * TILE + lane_block
            w0, w1, e0, e1 = (
                jnp.where(portal_cells == cell + group * BLOCKS, 0.0, piece[half])
                for group, piece in zip(columns, pieces)
            )
            side_out[0, 0, row : row + 8, :] = jnp.where(even, w0, pltpu.roll(w1, 32, 1))
            side_out[0, 1, row : row + 8, :] = jnp.where(even, pltpu.roll(w0, 96, 1), w1)
            side_out[1, 0, row : row + 8, :] = jnp.where(even, pltpu.roll(e0, 64, 1), pltpu.roll(e1, 96, 1))
            side_out[1, 1, row : row + 8, :] = jnp.where(even, pltpu.roll(e0, 32, 1), pltpu.roll(e1, 64, 1))

    prepare(0)
    prepare(3)
    for part in range(4):
        edges(part)

    pl.semaphore_wait(barrier, len(met))

    top, bottom = ground.at[0:STRIP], ground.at[TILE - STRIP : TILE]
    ground_source = {-1: top, 1: bottom}
    ground_copies = []
    for at, (dr, dc) in enumerate(AROUND):
        if dr:
            source = ground_source[dr]
        else:
            source = strips.at[0 if dc < 0 else 1]
        slot = AROUND.index((-dr, -dc))
        ground_copies.append(
            send(source, ground_in.at[slot], ground_send.at[at], ground_recv.at[slot], around[at])
        )

    field_copies = []
    for at, (dr, dc) in enumerate(AROUND):
        row_from, row_to, row_len = {
            -1: (0, HALO + TILE, HALO), 0: (0, HALO, TILE), 1: (TILE - HALO, 0, HALO)
        }[dr]
        if dc:
            side = 0 if dc < 0 else 1
            source = side_out.at[side, :, pl.ds(row_from, row_len), :]
            target = side_in.at[side, :, pl.ds(row_to, row_len), :]
        else:
            source = field.at[:, pl.ds(HALO + row_from, row_len), :]
            target = field.at[:, pl.ds(row_to, row_len), :]
        slot = AROUND.index((-dr, -dc))
        field_copies.append(send(source, target, field_send.at[at], field_recv.at[slot], around[at]))

    prepare(1)
    prepare(2)

    for copy in ground_copies:
        copy.wait_recv()
    slots = {step: at for at, step in enumerate(AROUND)}

    def lay(row, west_height, middle, east_height, west_block, east_block):
        height = jnp.where(wide < 16, west_height, jnp.where(wide < 80, pltpu.roll(middle, 16, 1), east_height))
        block = jnp.where(wide < 16, west_block, jnp.where(wide < 80, pltpu.roll(middle, 80, 1), east_block))
        high[0, row : row + STRIP, :] = height.astype(jnp.float32)
        high[1, row : row + STRIP, :] = block.astype(jnp.float32)

    for dr, row in ((-1, 0), (1, STRIP + TILE)):
        west_in, middle, east_in = (ground_in[slots[(dr, dc)]] for dc in (-1, 0, 1))
        lay(
            row, pltpu.roll(west_in, 80, 1), middle, pltpu.roll(east_in, 80, 1),
            pltpu.roll(west_in, 16, 1), pltpu.roll(east_in, 16, 1),
        )
    west_in, east_in = ground_in[slots[(0, -1)]], ground_in[slots[(0, 1)]]
    for part in range(4):
        base = part * 32
        lay(
            STRIP + part * STRIP,
            pltpu.roll(west_in, (-base) % LANES, 1),
            ground[part * STRIP : (part + 1) * STRIP],
            pltpu.roll(east_in, (80 - base) % LANES, 1),
            pltpu.roll(west_in, (-base - 16) % LANES, 1),
            pltpu.roll(east_in, (64 - base) % LANES, 1),
        )

    @pl.when(row_index == 0)
    def _():
        high[0, STRIP - 1 : STRIP, :] = high[0, STRIP : STRIP + 1, :]

    @pl.when(row_index == row_count - 1)
    def _():
        high[0, STRIP + TILE : STRIP + TILE + 1, :] = high[0, STRIP + TILE - 1 : STRIP + TILE, :]

    shift = STRIP - HALO
    near = high[0, shift : shift + EXT, :]
    up = high[0, shift - 1 : shift - 1 + EXT, :]
    down = high[0, shift + 1 : shift + 1 + EXT, :]
    col = lax.broadcasted_iota(jnp.int32, (EXT, LANES), 1) - STRIP
    row = lax.broadcasted_iota(jnp.int32, (EXT, LANES), 0) - HALO
    grid_col = col_index * TILE + col
    grid_row = row_index * TILE + row
    before = jnp.where(grid_col == 0, near, pltpu.roll(near, 1, 1))
    after = jnp.where(grid_col == col_count * TILE - 1, near, pltpu.roll(near, LANES - 1, 1))
    grad_x = (after - before) * 0.01
    grad_y = (down - up) * 0.01
    grad_sq = grad_x * grad_x + grad_y * grad_y
    step_cost = (
        1.0 + 2.0 * grad_sq + 0.5 * grad_y / jnp.sqrt(1.0 + grad_sq)
        + 30.0 * high[1, shift : shift + EXT, :]
    )
    inside = (
        (grid_row >= 0) & (grid_row < row_count * TILE)
        & (grid_col >= 0) & (grid_col < col_count * TILE)
    )
    cost_rows[...] = jnp.where(inside, step_cost, 2.0 * FAR)
    first_column = STRIP + lane_block * OWN
    halo_shift = jnp.where(low, TILE + 4 * lane_block, 4 * lane_block - 16) - lane_block * OWN
    for at in range(STEP):
        values = cost_rows[pl.ds(at, 8, stride=STEP), :]
        for group in range(GROUPS):
            cost[group, at] = lane_take(values, first_column + (group if group < OWN else group - OWN + halo_shift))

    loads[6].wait()
    cells = [portal_smem[0, 0, at] for at in range(PORTALS)]
    for at, cell in enumerate(cells):
        shifts[at : at + 1, :] = jnp.full((1, LANES), ((cell >> 4) & (BLOCKS - 1)) * PORTALS, jnp.int32)

    for copy, (_, dc) in zip(field_copies, AROUND):
        if dc:
            copy.wait_recv()

    def started(group, at, distance):
        return jnp.minimum(distance + 0.5 * cost[group, at], FAR)

    for at in range(STEP):
        for piece in range(2):
            from_east = side_in[0, piece, pl.ds(at, 8, stride=STEP), :]
            from_west = side_in[1, piece, pl.ds(at, 8, stride=STEP), :]
            for group, values in (
                (OWN + piece, jnp.where(low, from_east, from_west)),
                (OWN + piece + 2, pltpu.roll(jnp.where(low, from_west, from_east), 64, 1)),
            ):
                dist[group, at] = started(group, at, values)

    for copy, (_, dc) in zip(field_copies, AROUND):
        if not dc:
            copy.wait_recv()

    first_block, last_block = lane_block == 0, lane_block == BLOCKS - 1

    def sweep(first, last):
        def pairs_of(here, east_of):
            below = east_of[1:] + [pltpu.roll(east_of[0], 7, 0)]
            return [jnp.minimum(a, b) for a, b in zip(here, below)]

        def column(group):
            if first and group < OWN:
                return [started(group, at, field[group, pl.ds(at, 8, stride=STEP), :]) for at in range(STEP)]
            return [dist[group, at] for at in range(STEP)]

        own_first, halo_first = column(0), column(OWN)
        own_pairs = pairs_of(
            column(OWN - 1),
            [pltpu.roll(jnp.where(first_block, a, b), LANES - PORTALS, 1) for a, b in zip(halo_first, own_first)],
        )
        halo_pairs = pairs_of(
            column(GROUPS - 1),
            [pltpu.roll(jnp.where(first_block, a, b), LANES - PORTALS, 1) for a, b in zip(own_first, halo_first)],
        )
        own_west = [pltpu.roll(jnp.where(last_block, a, b), PORTALS, 1) for a, b in zip(halo_pairs, own_pairs)]
        halo_west = [pltpu.roll(jnp.where(last_block, a, b), PORTALS, 1) for a, b in zip(own_pairs, halo_pairs)]
        for begin, end, west_of, end_pairs in ((0, OWN, own_west, own_pairs), (OWN, GROUPS, halo_west, halo_pairs)):
            if last and begin == OWN:
                continue
            now = own_first if begin == 0 else column(begin)
            for group in range(begin, end):
                if group < end - 1:
                    later = column(group + 1)
                    pairs = pairs_of(now, later)
                else:
                    pairs = end_pairs
                north = [pltpu.roll(pairs[STEP - 1], 1, 0)] + pairs[:-1]
                for at in range(STEP):
                    here = cost[group, at]
                    shortest = jnp.minimum(now[at], here + jnp.minimum(north[at], west_of[at]))
                    if last:
                        field[group, pl.ds(at, 8, stride=STEP), :] = shortest - 0.5 * here
                    else:
                        dist[group, at] = shortest
                west_of, now = pairs, later

    sweep(True, False)
    def middle(_, carry):
        sweep(False, False)
        sweep(False, False)
        return carry

    lax.fori_loop(0, (SWEEPS - 2) // 2, middle, 0)
    for copy in field_copies:
        copy.wait_send()
    sweep(False, True)

    for at, cell in enumerate(cells):
        rows[at : at + 1, :] = field[cell & (OWN - 1), pl.ds(HALO + (cell >> 6), 1), :]
    first = jnp.zeros((8, LANES), jnp.float32)
    for part in range(4):
        index = shifts[part * 8 : part * 8 + 8, :] + lane_class
        first = jnp.where(lane_block == part, lane_take(rows[part * 8 : part * 8 + 8, :], index), first)
    table[0] = first

    table_copies = []

    def exchange(level):
        copies = [
            send(
                table.at[level], table_in.at[3 * level + at],
                table_send.at[3 * level + at], table_recv.at[3 * level + at], device,
            )
            for at, device in reversed(tuple(enumerate(partners[level])))
        ]
        table_copies.extend(reversed(copies))

    def left_of(values):
        return [lane_take(values, lane_block * PORTALS + at) for at in range(PORTALS)]

    def right_of(values, slot):
        for part in range(4):
            right_rows[slot, part * 8 : part * 8 + 8, :] = lane_take(values, lane_class + part * PORTALS)
        return [
            jnp.broadcast_to(right_rows[slot, at : at + 1, :], (8, LANES)) for at in range(PORTALS)
        ]

    def minplus(left, right):
        sums = [a + b for a, b in zip(left, right)]
        while len(sums) > 1:
            sums = [jnp.minimum(a, b) for a, b in zip(sums[::2], sums[1::2])]
        return sums[0]

    def pair(near_table, near_left, near_right, far_right):
        through = minplus(near_left, far_right)
        return jnp.minimum(near_table, minplus(left_of(through), near_right))

    def relax_out(part):
        for first_at in range(4):
            for_rows = [
                transposed(
                    [
                        field[4 * first_at + at, HALO + part * 16 + half * 8 : HALO + part * 16 + half * 8 + 8, :]
                        for at in range(4)
                    ]
                )
                for half in range(2)
            ]
            for at in range(4):
                group = first_at + 4 * at
                values = jnp.concatenate([for_rows[0][at], for_rows[1][at]], axis=0)
                relaxed[part * 16 : part * 16 + 16, group * LANES : (group + 1) * LANES] = values.astype(jnp.bfloat16)

    now = first
    for level in range(2):
        exchange(level)
        if level == 0:
            for copy in ground_copies:
                copy.wait_send()
        now_left, now_right = left_of(now), right_of(now, 6 * level)
        relax_out(2 * level)
        relax_out(2 * level + 1)
        def arrived(at):
            table_copies[3 * level + at].wait_recv()
            return table_in[3 * level + at]

        by_col = arrived(1)
        col_left, col_right = left_of(by_col), right_of(by_col, 6 * level + 2)
        if level == 0:
            there = pair(by_col, col_left, col_right, right_of(arrived(2), 6 * level + 3))
            there_left = left_of(there)
            here = pair(now, now_left, now_right, right_of(arrived(0), 6 * level + 1))
            around_here = minplus(there_left, right_of(here, 6 * level + 4))
            now = jnp.minimum(here, minplus(left_of(here), right_of(around_here, 6 * level + 5)))
        else:
            here = pair(now, now_left, now_right, right_of(arrived(0), 6 * level + 1))
            here_left, here_right = left_of(here), right_of(here, 6 * level + 4)
            there = pair(by_col, col_left, col_right, right_of(arrived(2), 6 * level + 3))
            now = pair(here, here_left, here_right, right_of(there, 6 * level + 5))
        if level == 0:
            table[1] = now
    now = now * 0.0625
    for part in range(4):
        merged[0, 0, part * 8 : part * 8 + 8, :] = now[:, part * PORTALS : (part + 1) * PORTALS]

    for copy in table_copies:
        copy.wait_send()


def hand_out(relaxed_in, merged_in, relaxed, merged, sem):
    copies = [
        pltpu.make_async_copy(relaxed_in, relaxed, sem.at[0]),
        pltpu.make_async_copy(merged_in, merged, sem.at[1]),
    ]
    for copy in copies:
        copy.start()
    for copy in copies:
        copy.wait()


def body(heights, blocked, estimate, portal_index):
    in_hbm = pl.BlockSpec(memory_space=pltpu.HBM)
    in_vmem = pl.BlockSpec(memory_space=pltpu.VMEM)
    outs = (
        jax.ShapeDtypeStruct(estimate.shape, jnp.bfloat16),
        jax.ShapeDtypeStruct((1, 1, PORTALS, PORTALS), jnp.float32),
    )
    results = pl.pallas_call(
        kernel,
        out_shape=outs,
        in_specs=[in_hbm] * 4,
        out_specs=(in_vmem, in_vmem),
        scratch_shapes=[
            pltpu.VMEM((TILE, TILE), jnp.int32),
            pltpu.VMEM((TILE, TILE), jnp.int32),
            pltpu.VMEM((TILE, TILE * PORTALS), jnp.bfloat16),
            pltpu.VMEM((1, 1, PORTALS), jnp.int32),
            pltpu.SMEM((1, 1, PORTALS), jnp.int32),
            pltpu.VMEM((TILE, LANES), jnp.int32),
            pltpu.VMEM((2, STRIP, LANES), jnp.int32),
            pltpu.VMEM((8, STRIP, LANES), jnp.int32),
            pltpu.VMEM((2, TILE + 2 * STRIP, LANES), jnp.float32),
            pltpu.VMEM((EXT, LANES), jnp.float32),
            pltpu.VMEM((OWN, EXT, LANES), jnp.float32),
            pltpu.VMEM((2, 2, TILE, LANES), jnp.float32),
            pltpu.VMEM((2, 2, EXT, LANES), jnp.float32),
            pltpu.VMEM((GROUPS, STEP, 8, LANES), jnp.float32),
            pltpu.VMEM((GROUPS, STEP, 8, LANES), jnp.float32),
            pltpu.VMEM((PORTALS, LANES), jnp.float32),
            pltpu.VMEM((PORTALS, LANES), jnp.int32),
            pltpu.VMEM((2, 8, LANES), jnp.float32),
            pltpu.VMEM((6, 8, LANES), jnp.float32),
            pltpu.VMEM((12, PORTALS, LANES), jnp.float32),
            pltpu.SemaphoreType.DMA((7,)),
            pltpu.SemaphoreType.DMA((8,)),
            pltpu.SemaphoreType.DMA((8,)),
            pltpu.SemaphoreType.DMA((8,)),
            pltpu.SemaphoreType.DMA((8,)),
            pltpu.SemaphoreType.DMA((6,)),
            pltpu.SemaphoreType.DMA((6,)),
        ],
        compiler_params=pltpu.CompilerParams(
            collective_id=0, has_side_effects=True, vmem_limit_bytes=16 * 2**20
        ),
    )(*(pltpu.with_memory_space_constraint(x, pltpu.HBM) for x in (heights, blocked, estimate, portal_index)))
    return pl.pallas_call(
        hand_out,
        out_shape=tuple(pltpu.HBM(x.shape, x.dtype) for x in outs),
        in_specs=[in_vmem] * 2,
        out_specs=[in_hbm] * 2,
        scratch_shapes=[pltpu.SemaphoreType.DMA((2,))],
        compiler_params=pltpu.CompilerParams(vmem_limit_bytes=2**20),
    )(*(pltpu.with_memory_space_constraint(x, pltpu.VMEM) for x in results))


def solution(mesh):
    placed = (P("row", "col"), P("row", "col"), P("row", "col"), P("row", "col", None))
    return jax.shard_map(
        body,
        mesh=mesh,
        in_specs=placed,
        out_specs=(P("row", "col"), P("row", "col", None, None)),
        check_vma=False,
    )
```

```python
import functools

import jax
import jax.numpy as jnp
from jax import lax
from jax.experimental import pallas as pl
from jax.experimental.pallas import tpu as pltpu
from jax.sharding import PartitionSpec as P

TILE = 64
PORTALS = 32
SWEEPS = 8
HALO = 8
EXT = TILE + 2 * HALO
LANES = 128
BLOCKS = LANES // PORTALS
OWN = TILE // BLOCKS
GROUPS = EXT // BLOCKS
STEP = EXT // 8
STRIP = 16
FAR = 1000000.0


AROUND = ((-1, -1), (-1, 1), (1, -1), (1, 1), (-1, 0), (1, 0), (0, -1), (0, 1))


def lane_take(values, index):
    return jnp.take_along_axis(values, index, axis=1, mode="promise_in_bounds")


def kernel(
    heights_hbm, blocked_hbm, estimate_hbm, portal_hbm,
    relaxed, merged,
    heights, blocked, estimate, portal, portal_smem,
    ground, strips, ground_in, high, cost_rows,
    field, side_out, side_in, cost, dist, rows, shifts, table, table_in, right_rows,
    load_sem, ground_send, ground_recv, field_send, field_recv, table_send, table_recv,
):
    row_index, col_index = lax.axis_index("row"), lax.axis_index("col")
    row_count, col_count = lax.axis_size("row"), lax.axis_size("col")
    around = [
        (lax.rem(row_index + dr + row_count, row_count), lax.rem(col_index + dc + col_count, col_count))
        for dr, dc in AROUND
    ]

    def other(index, bit):
        return index + bit - 2 * bit * lax.rem(index // bit, 2)

    partners = []
    for level in range(2):
        bit = 1 << level
        partners.append(
            [
                (other(row_index, bit), col_index),
                (row_index, other(col_index, bit)),
                (other(row_index, bit), other(col_index, bit)),
            ]
        )

    barrier = pltpu.get_barrier_semaphore()
    met = around
    for device in met:
        pl.semaphore_signal(barrier, inc=1, device_id=device, device_id_type=pl.DeviceIdType.MESH)

    loads = [
        pltpu.make_async_copy(source, target, load_sem.at[at])
        for at, (source, target) in enumerate(
            (
                (heights_hbm, heights),
                (blocked_hbm, blocked),
                (portal_hbm, portal),
                (estimate_hbm.at[0:16], estimate.at[0:16]),
                (estimate_hbm.at[48:64], estimate.at[48:64]),
                (estimate_hbm.at[16:48], estimate.at[16:48]),
                (portal_hbm, portal_smem),
            )
        )
    ]
    for load in loads:
        load.start()

    def send(source, target, send_sem, recv_sem, device):
        copy = pltpu.make_async_remote_copy(
            src_ref=source, dst_ref=target, send_sem=send_sem, recv_sem=recv_sem,
            device_id=device, device_id_type=pl.DeviceIdType.MESH,
        )
        copy.start()
        return copy

    lane = lax.broadcasted_iota(jnp.int32, (8, LANES), 1)
    sublane = lax.broadcasted_iota(jnp.int32, (8, LANES), 0)
    lane_block = lane // PORTALS
    lane_class = lane % PORTALS

    loads[0].wait()
    loads[1].wait()
    ground[:, 0:TILE] = heights[...]
    ground[:, TILE : 2 * TILE] = blocked[...]
    wide = lax.broadcasted_iota(jnp.int32, (STRIP, LANES), 1)
    west = jnp.zeros((STRIP, LANES), jnp.int32)
    east = jnp.zeros((STRIP, LANES), jnp.int32)
    for part in range(4):
        here = ground[part * STRIP : (part + 1) * STRIP]
        base = part * 32
        in_height = (wide >= base) & (wide < base + 16)
        in_block = (wide >= base + 16) & (wide < base + 32)
        west = jnp.where(in_height, pltpu.roll(here, base % LANES, 1), west)
        west = jnp.where(in_block, pltpu.roll(here, (base + 16 - 64) % LANES, 1), west)
        east = jnp.where(in_height, pltpu.roll(here, (base - 48) % LANES, 1), east)
        east = jnp.where(in_block, pltpu.roll(here, (base + 16 - 112) % LANES, 1), east)
    strips[0] = west
    strips[1] = east

    loads[2].wait()
    own = jnp.broadcast_to(portal[0, 0:1, :], (8, PORTALS))
    portal_cells = jnp.concatenate([own] * BLOCKS, axis=1)
    loads[3].wait()
    loads[4].wait()
    loads[5].wait()
    low = lane < 2 * PORTALS
    even = lane_block % 2 == 0
    swapped_blocks = lane_class + (lane_block + 1 - 2 * (lane_block % 2)) * PORTALS

    def transposed(a):
        t = [None] * 4
        for at in range(2):
            turned = pltpu.roll(jnp.where(low, a[at + 2], a[at]), 2 * PORTALS, 1)
            t[at], t[at + 2] = jnp.where(low, a[at], turned), jnp.where(low, turned, a[at + 2])
        out = [None] * 4
        for at in (0, 2):
            turned = lane_take(jnp.where(even, t[at + 1], t[at]), swapped_blocks)
            out[at], out[at + 1] = jnp.where(even, t[at], turned), jnp.where(even, turned, t[at + 1])
        return out

    def estimates(part, group):
        values = estimate[part * 16 : (part + 1) * 16, group * LANES : (group + 1) * LANES]
        values = values.astype(jnp.float32)
        return values[0:8], values[8:16]

    def prepare(part):
        for first in range(4):
            halves = [estimates(part, first + 4 * at) for at in range(4)]
            for half in range(2):
                row = part * 16 + half * 8
                cell = (row + sublane) * TILE + lane_block * OWN
                for at, values in enumerate(transposed([pieces[half] for pieces in halves])):
                    group = 4 * first + at
                    field[group, HALO + row : HALO + row + 8, :] = jnp.where(
                        portal_cells == cell + group, 0.0, values
                    )

    def edges(part):
        columns = (0, 1, OWN - 2, OWN - 1)
        pieces = [estimates(part, group) for group in columns]
        for half in range(2):
            row = part * 16 + half * 8
            cell = (row + sublane) * TILE + lane_block
            w0, w1, e0, e1 = (
                jnp.where(portal_cells == cell + group * BLOCKS, 0.0, piece[half])
                for group, piece in zip(columns, pieces)
            )
            side_out[0, 0, row : row + 8, :] = jnp.where(even, w0, pltpu.roll(w1, 32, 1))
            side_out[0, 1, row : row + 8, :] = jnp.where(even, pltpu.roll(w0, 96, 1), w1)
            side_out[1, 0, row : row + 8, :] = jnp.where(even, pltpu.roll(e0, 64, 1), pltpu.roll(e1, 96, 1))
            side_out[1, 1, row : row + 8, :] = jnp.where(even, pltpu.roll(e0, 32, 1), pltpu.roll(e1, 64, 1))

    prepare(0)
    prepare(3)
    for part in range(4):
        edges(part)

    pl.semaphore_wait(barrier, len(met))

    top, bottom = ground.at[0:STRIP], ground.at[TILE - STRIP : TILE]
    ground_source = {-1: top, 1: bottom}
    ground_copies = []
    for at, (dr, dc) in enumerate(AROUND):
        if dr:
            source = ground_source[dr]
        else:
            source = strips.at[0 if dc < 0 else 1]
        slot = AROUND.index((-dr, -dc))
        ground_copies.append(
            send(source, ground_in.at[slot], ground_send.at[at], ground_recv.at[slot], around[at])
        )

    field_copies = []
    for at, (dr, dc) in enumerate(AROUND):
        row_from, row_to, row_len = {
            -1: (0, HALO + TILE, HALO), 0: (0, HALO, TILE), 1: (TILE - HALO, 0, HALO)
        }[dr]
        if dc:
            side = 0 if dc < 0 else 1
            source = side_out.at[side, :, pl.ds(row_from, row_len), :]
            target = side_in.at[side, :, pl.ds(row_to, row_len), :]
        else:
            source = field.at[:, pl.ds(HALO + row_from, row_len), :]
            target = field.at[:, pl.ds(row_to, row_len), :]
        slot = AROUND.index((-dr, -dc))
        field_copies.append(send(source, target, field_send.at[at], field_recv.at[slot], around[at]))

    prepare(1)
    prepare(2)

    for copy in ground_copies:
        copy.wait_recv()
    slots = {step: at for at, step in enumerate(AROUND)}

    def lay(row, west_height, middle, east_height, west_block, east_block):
        height = jnp.where(wide < 16, west_height, jnp.where(wide < 80, pltpu.roll(middle, 16, 1), east_height))
        block = jnp.where(wide < 16, west_block, jnp.where(wide < 80, pltpu.roll(middle, 80, 1), east_block))
        high[0, row : row + STRIP, :] = height.astype(jnp.float32)
        high[1, row : row + STRIP, :] = block.astype(jnp.float32)

    for dr, row in ((-1, 0), (1, STRIP + TILE)):
        west_in, middle, east_in = (ground_in[slots[(dr, dc)]] for dc in (-1, 0, 1))
        lay(
            row, pltpu.roll(west_in, 80, 1), middle, pltpu.roll(east_in, 80, 1),
            pltpu.roll(west_in, 16, 1), pltpu.roll(east_in, 16, 1),
        )
    west_in, east_in = ground_in[slots[(0, -1)]], ground_in[slots[(0, 1)]]
    for part in range(4):
        base = part * 32
        lay(
            STRIP + part * STRIP,
            pltpu.roll(west_in, (-base) % LANES, 1),
            ground[part * STRIP : (part + 1) * STRIP],
            pltpu.roll(east_in, (80 - base) % LANES, 1),
            pltpu.roll(west_in, (-base - 16) % LANES, 1),
            pltpu.roll(east_in, (64 - base) % LANES, 1),
        )

    @pl.when(row_index == 0)
    def _():
        high[0, STRIP - 1 : STRIP, :] = high[0, STRIP : STRIP + 1, :]

    @pl.when(row_index == row_count - 1)
    def _():
        high[0, STRIP + TILE : STRIP + TILE + 1, :] = high[0, STRIP + TILE - 1 : STRIP + TILE, :]

    shift = STRIP - HALO
    near = high[0, shift : shift + EXT, :]
    up = high[0, shift - 1 : shift - 1 + EXT, :]
    down = high[0, shift + 1 : shift + 1 + EXT, :]
    col = lax.broadcasted_iota(jnp.int32, (EXT, LANES), 1) - STRIP
    row = lax.broadcasted_iota(jnp.int32, (EXT, LANES), 0) - HALO
    grid_col = col_index * TILE + col
    grid_row = row_index * TILE + row
    before = jnp.where(grid_col == 0, near, pltpu.roll(near, 1, 1))
    after = jnp.where(grid_col == col_count * TILE - 1, near, pltpu.roll(near, LANES - 1, 1))
    grad_x = (after - before) * 0.01
    grad_y = (down - up) * 0.01
    grad_sq = grad_x * grad_x + grad_y * grad_y
    step_cost = (
        1.0 + 2.0 * grad_sq + 0.5 * grad_y / jnp.sqrt(1.0 + grad_sq)
        + 30.0 * high[1, shift : shift + EXT, :]
    )
    inside = (
        (grid_row >= 0) & (grid_row < row_count * TILE)
        & (grid_col >= 0) & (grid_col < col_count * TILE)
    )
    cost_rows[...] = jnp.where(inside, step_cost, 2.0 * FAR)
    first_column = STRIP + lane_block * OWN
    halo_shift = jnp.where(low, TILE + 4 * lane_block, 4 * lane_block - 16) - lane_block * OWN
    for at in range(STEP):
        values = cost_rows[pl.ds(at, 8, stride=STEP), :]
        for group in range(GROUPS):
            cost[group, at] = lane_take(values, first_column + (group if group < OWN else group - OWN + halo_shift))

    loads[6].wait()
    cells = [portal_smem[0, 0, at] for at in range(PORTALS)]
    for at, cell in enumerate(cells):
        shifts[at : at + 1, :] = jnp.full((1, LANES), ((cell >> 4) & (BLOCKS - 1)) * PORTALS, jnp.int32)

    for copy, (_, dc) in zip(field_copies, AROUND):
        if dc:
            copy.wait_recv()

    def started(group, at, distance):
        return jnp.minimum(distance + 0.5 * cost[group, at], FAR)

    for at in range(STEP):
        for piece in range(2):
            from_east = side_in[0, piece, pl.ds(at, 8, stride=STEP), :]
            from_west = side_in[1, piece, pl.ds(at, 8, stride=STEP), :]
            for group, values in (
                (OWN + piece, jnp.where(low, from_east, from_west)),
                (OWN + piece + 2, pltpu.roll(jnp.where(low, from_west, from_east), 64, 1)),
            ):
                dist[group, at] = started(group, at, values)

    for copy, (_, dc) in zip(field_copies, AROUND):
        if not dc:
            copy.wait_recv()

    first_block, last_block = lane_block == 0, lane_block == BLOCKS - 1

    def sweep(first, last):
        def pairs_of(here, east_of):
            below = east_of[1:] + [pltpu.roll(east_of[0], 7, 0)]
            return [jnp.minimum(a, b) for a, b in zip(here, below)]

        def column(group):
            if first and group < OWN:
                return [started(group, at, field[group, pl.ds(at, 8, stride=STEP), :]) for at in range(STEP)]
            return [dist[group, at] for at in range(STEP)]

        own_first, halo_first = column(0), column(OWN)
        own_pairs = pairs_of(
            column(OWN - 1),
            [pltpu.roll(jnp.where(first_block, a, b), LANES - PORTALS, 1) for a, b in zip(halo_first, own_first)],
        )
        halo_pairs = pairs_of(
            column(GROUPS - 1),
            [pltpu.roll(jnp.where(first_block, a, b), LANES - PORTALS, 1) for a, b in zip(own_first, halo_first)],
        )
        own_west = [pltpu.roll(jnp.where(last_block, a, b), PORTALS, 1) for a, b in zip(halo_pairs, own_pairs)]
        halo_west = [pltpu.roll(jnp.where(last_block, a, b), PORTALS, 1) for a, b in zip(own_pairs, halo_pairs)]
        for begin, end, west_of, end_pairs in ((0, OWN, own_west, own_pairs), (OWN, GROUPS, halo_west, halo_pairs)):
            if last and begin == OWN:
                continue
            now = own_first if begin == 0 else column(begin)
            for group in range(begin, end):
                if group < end - 1:
                    later = column(group + 1)
                    pairs = pairs_of(now, later)
                else:
                    pairs = end_pairs
                north = [pltpu.roll(pairs[STEP - 1], 1, 0)] + pairs[:-1]
                for at in range(STEP):
                    here = cost[group, at]
                    shortest = jnp.minimum(now[at], here + jnp.minimum(north[at], west_of[at]))
                    if last:
                        field[group, pl.ds(at, 8, stride=STEP), :] = shortest - 0.5 * here
                    else:
                        dist[group, at] = shortest
                west_of, now = pairs, later

    sweep(True, False)
    def middle(_, carry):
        sweep(False, False)
        return carry

    lax.fori_loop(0, SWEEPS - 2, middle, 0)
    for copy in field_copies:
        copy.wait_send()
    sweep(False, True)

    for at, cell in enumerate(cells):
        rows[at : at + 1, :] = field[cell & (OWN - 1), pl.ds(HALO + (cell >> 6), 1), :]
    first = jnp.zeros((8, LANES), jnp.float32)
    for part in range(4):
        index = shifts[part * 8 : part * 8 + 8, :] + lane_class
        first = jnp.where(lane_block == part, lane_take(rows[part * 8 : part * 8 + 8, :], index), first)
    table[0] = first

    table_copies = []

    def exchange(level):
        order = ((2, 1, 0), (2, 0, 1))[level]
        copies = [
            send(
                table.at[level], table_in.at[3 * level + at],
                table_send.at[3 * level + at], table_recv.at[3 * level + at], device,
            )
            for at, device in ((at, partners[level][at]) for at in order)
        ]
        table_copies.extend(copies[order.index(at)] for at in range(3))

    def left_of(values):
        return [lane_take(values, lane_block * PORTALS + at) for at in range(PORTALS)]

    def right_of(values, slot):
        for part in range(4):
            right_rows[slot, part * 8 : part * 8 + 8, :] = lane_take(values, lane_class + part * PORTALS)
        return [
            jnp.broadcast_to(right_rows[slot, at : at + 1, :], (8, LANES)) for at in range(PORTALS)
        ]

    def minplus(left, right):
        sums = [a + b for a, b in zip(left, right)]
        while len(sums) > 1:
            sums = [jnp.minimum(a, b) for a, b in zip(sums[::2], sums[1::2])]
        return sums[0]

    def pair(near_table, near_left, near_right, far_right):
        through = minplus(near_left, far_right)
        return jnp.minimum(near_table, minplus(left_of(through), near_right))

    def relax_out(part):
        for first_at in range(4):
            for_rows = [
                transposed(
                    [
                        field[4 * first_at + at, HALO + part * 16 + half * 8 : HALO + part * 16 + half * 8 + 8, :]
                        for at in range(4)
                    ]
                )
                for half in range(2)
            ]
            for at in range(4):
                group = first_at + 4 * at
                values = jnp.concatenate([for_rows[0][at], for_rows[1][at]], axis=0)
                relaxed[part * 16 : part * 16 + 16, group * LANES : (group + 1) * LANES] = values.astype(jnp.bfloat16)

    now = first
    for level in range(2):
        exchange(level)
        if level == 0:
            for copy in ground_copies:
                copy.wait_send()
        now_left, now_right = left_of(now), right_of(now, 6 * level)
        relax_out(2 * level)
        relax_out(2 * level + 1)
        def arrived(at):
            table_copies[3 * level + at].wait_recv()
            return table_in[3 * level + at]

        by_col = arrived(1)
        col_left, col_right = left_of(by_col), right_of(by_col, 6 * level + 2)
        if level == 0:
            there = pair(by_col, col_left, col_right, right_of(arrived(2), 6 * level + 3))
            there_left = left_of(there)
            here = pair(now, now_left, now_right, right_of(arrived(0), 6 * level + 1))
            around_here = minplus(there_left, right_of(here, 6 * level + 4))
            now = jnp.minimum(here, minplus(left_of(here), right_of(around_here, 6 * level + 5)))
        else:
            here = pair(now, now_left, now_right, right_of(arrived(0), 6 * level + 1))
            here_left, here_right = left_of(here), right_of(here, 6 * level + 4)
            there = pair(by_col, col_left, col_right, right_of(arrived(2), 6 * level + 3))
            now = pair(here, here_left, here_right, right_of(there, 6 * level + 5))
        if level == 0:
            table[1] = now
    now = now * 0.0625
    for part in range(4):
        merged[0, 0, part * 8 : part * 8 + 8, :] = now[:, part * PORTALS : (part + 1) * PORTALS]

    for copy in table_copies:
        copy.wait_send()


def hand_out(relaxed_in, merged_in, relaxed, merged, sem):
    copies = [
        pltpu.make_async_copy(relaxed_in, relaxed, sem.at[0]),
        pltpu.make_async_copy(merged_in, merged, sem.at[1]),
    ]
    for copy in copies:
        copy.start()
    for copy in copies:
        copy.wait()


def body(heights, blocked, estimate, portal_index):
    in_hbm = pl.BlockSpec(memory_space=pltpu.HBM)
    in_vmem = pl.BlockSpec(memory_space=pltpu.VMEM)
    outs = (
        jax.ShapeDtypeStruct(estimate.shape, jnp.bfloat16),
        jax.ShapeDtypeStruct((1, 1, PORTALS, PORTALS), jnp.float32),
    )
    results = pl.pallas_call(
        kernel,
        out_shape=outs,
        in_specs=[in_hbm] * 4,
        out_specs=(in_vmem, in_vmem),
        scratch_shapes=[
            pltpu.VMEM((TILE, TILE), jnp.int32),
            pltpu.VMEM((TILE, TILE), jnp.int32),
            pltpu.VMEM((TILE, TILE * PORTALS), jnp.bfloat16),
            pltpu.VMEM((1, 1, PORTALS), jnp.int32),
            pltpu.SMEM((1, 1, PORTALS), jnp.int32),
            pltpu.VMEM((TILE, LANES), jnp.int32),
            pltpu.VMEM((2, STRIP, LANES), jnp.int32),
            pltpu.VMEM((8, STRIP, LANES), jnp.int32),
            pltpu.VMEM((2, TILE + 2 * STRIP, LANES), jnp.float32),
            pltpu.VMEM((EXT, LANES), jnp.float32),
            pltpu.VMEM((OWN, EXT, LANES), jnp.float32),
            pltpu.VMEM((2, 2, TILE, LANES), jnp.float32),
            pltpu.VMEM((2, 2, EXT, LANES), jnp.float32),
            pltpu.VMEM((GROUPS, STEP, 8, LANES), jnp.float32),
            pltpu.VMEM((GROUPS, STEP, 8, LANES), jnp.float32),
            pltpu.VMEM((PORTALS, LANES), jnp.float32),
            pltpu.VMEM((PORTALS, LANES), jnp.int32),
            pltpu.VMEM((2, 8, LANES), jnp.float32),
            pltpu.VMEM((6, 8, LANES), jnp.float32),
            pltpu.VMEM((12, PORTALS, LANES), jnp.float32),
            pltpu.SemaphoreType.DMA((7,)),
            pltpu.SemaphoreType.DMA((8,)),
            pltpu.SemaphoreType.DMA((8,)),
            pltpu.SemaphoreType.DMA((8,)),
            pltpu.SemaphoreType.DMA((8,)),
            pltpu.SemaphoreType.DMA((6,)),
            pltpu.SemaphoreType.DMA((6,)),
        ],
        compiler_params=pltpu.CompilerParams(
            collective_id=0, has_side_effects=True, vmem_limit_bytes=16 * 2**20
        ),
    )(*(pltpu.with_memory_space_constraint(x, pltpu.HBM) for x in (heights, blocked, estimate, portal_index)))
    return pl.pallas_call(
        hand_out,
        out_shape=tuple(pltpu.HBM(x.shape, x.dtype) for x in outs),
        in_specs=[in_vmem] * 2,
        out_specs=[in_hbm] * 2,
        scratch_shapes=[pltpu.SemaphoreType.DMA((2,))],
        compiler_params=pltpu.CompilerParams(vmem_limit_bytes=2**20),
    )(*(pltpu.with_memory_space_constraint(x, pltpu.VMEM) for x in results))


def solution(mesh):
    placed = (P("row", "col"), P("row", "col"), P("row", "col"), P("row", "col", None))
    return jax.shard_map(
        body,
        mesh=mesh,
        in_specs=placed,
        out_specs=(P("row", "col"), P("row", "col", None, None)),
        check_vma=False,
    )
```
